32 devices in a mesh: dp: 4 (over z), gx: 2 (over x), gy: 4 (over y, core).
Axes of the slice: x: 2, y: 2, z: 4, core: 2. Of those that a mesh axis runs over, the one named last changes fastest.
Arguments:
- tokens: bfloat16 [960, 32768], P('gy', ('dp', 'gx')), may hold values from -6 to 6
- doc_start: int32 [32768], P(('dp', 'gx', 'gy')), may hold values from 0 to 32256, as said below
- cotangent: bfloat16 [960, 32768], P('gy', ('dp', 'gx')), may hold values from -6 to 6
- attn_gain: float32 [960], replicated, may hold values from 0.5 to 1.5
- mlp_gain: float32 [960], replicated, may hold values from 0.5 to 1.5
- w_qkv: bfloat16 [960, 1600], P('gy', 'gx'), may hold values from -0.1875 to 0.1875
- w_out: bfloat16 [960, 960], P('gx', 'gy'), may hold values from -2.5 to 2.5
- w_gate: bfloat16 [960, 2560], P('gy', 'gx'), may hold values from -0.1875 to 0.1875
- w_up: bfloat16 [960, 2560], P('gy', 'gx'), may hold values from -0.1875 to 0.1875
- w_down: bfloat16 [2560, 960], P('gx', 'gy'), may hold values from -0.125 to 0.125
Outputs:
- result: bfloat16 [960, 32768], P('gy', ('dp', 'gx'))
- input_grad: bfloat16 [960, 32768], P('gy', ('dp', 'gx'))
- grad_qkv: float32 [960, 1600], P('gy', 'gx')
- grad_out: float32 [960, 960], P('gx', 'gy')
- grad_gate: float32 [960, 2560], P('gy', 'gx')
- grad_up: float32 [960, 2560], P('gy', 'gx')
- grad_down: float32 [2560, 960], P('gx', 'gy')
- grad_attn_gain: float32 [960], replicated
- grad_mlp_gain: float32 [960], replicated
The draws below stay inside these ranges and needn't reach their ends.
Inputs may be any that keep to these rules, and one draw needn't show every extreme that they name: `doc_start`: each value is the index of the first token of its token's document. Documents lie inside aligned blocks of 2048 tokens, three to a block; the middle one holds 256 to 1024 tokens and contains the block's tokens 1024 - 1 and 1024; the others hold 512 to 896 tokens.
All inputs are finite; a program needn't handle non-finite values.
Results may differ from the reference program's by a relative error of at most 0.014.
Values may be sent and summed in bfloat16 or wider, within the bound.
No kernel may reach another device: no remote copies, remote signals or barrier semaphores. Data moves between devices by JAX's collectives and lax.ppermute only.
A program may use at most 256 MiB of HBM per device.

```python
import jax
import jax.numpy as jnp
from jax import lax

D = 960
HEADS = 15
KV_HEADS = 5
HEAD = 64
FF = 2560
TOK_DEV = 1024
DOC_MAX = 1024
SEQ_LEN = 4096
TOKENS = 32768
QKV = 1600


def draw_doc_start(key, part):
    block_len = 2 * TOK_DEV
    block_count = TOKENS // block_len
    first_key, second_key = jax.random.split(key)
    middle = TOK_DEV
    first_end = jax.random.randint(first_key, (block_count,), middle - DOC_MAX // 2, middle - DOC_MAX // 8 + 1)
    second_end = jax.random.randint(second_key, (block_count,), middle + DOC_MAX // 8, middle + DOC_MAX // 2 + 1)
    second_end = second_end.at[block_count - 1].set(middle + DOC_MAX // 2)
    places = jnp.arange(block_len, dtype=jnp.int32)[None, :]
    inside = jnp.where(places < first_end[:, None], 0, jnp.where(places < second_end[:, None], first_end[:, None], second_end[:, None]))
    offset = jnp.arange(block_count, dtype=jnp.int32)[:, None] * block_len
    return (inside + offset).reshape(-1).astype(jnp.int32)


def block_scale(stream_key, dims, cuts, low, high):
    level, own = 1.0, jax.random.fold_in(stream_key, 6)
    for dim, blocks in cuts:
        draws = jnp.exp(jax.random.uniform(jax.random.fold_in(own, dim), (blocks,), jnp.float32, low / len(cuts), high / len(cuts)))
        level = level * jnp.repeat(draws, dims[dim] // blocks).reshape([-1 if axis == dim else 1 for axis in range(len(dims))])
    return level


def normal_values(stream_key, extent, width, bound, pieces=(), kind=jnp.bfloat16):
    loudness = block_scale(stream_key, extent, pieces, -0.22, 0.18) if pieces else 1.0
    array = jax.random.normal(stream_key, extent, jnp.float32) * width * loudness
    return jnp.minimum(jnp.maximum(array, -bound), bound).astype(kind)


def setup_inputs(seed: int = 0) -> dict:
    keys = jax.random.split(jax.random.key(seed), 11)
    tokens = normal_values(keys[0], (D, TOKENS), 1.0, 6.0, ((0, 4), (1, 8)))
    doc_start = draw_doc_start(jax.random.fold_in(keys[10], 71), 0)
    cotangent = normal_values(keys[2], (D, TOKENS), 1.0, 6.0, ((0, 4), (1, 8)))
    attn_gain = jnp.clip(1.0 + 0.1 * jax.random.normal(keys[3], (D,), jnp.float32), 0.5, 1.5)
    mlp_gain = jnp.clip(1.0 + 0.1 * jax.random.normal(keys[4], (D,), jnp.float32), 0.5, 1.5)
    w_qkv = normal_values(keys[5], (D, QKV), D ** -0.5, 0.1875, ((0, 4), (1, 2)))
    w_out = normal_values(keys[6], (HEADS * HEAD, D), 6 ** -0.5, 2.5, ((0, 2), (1, 4)))
    w_gate = normal_values(keys[7], (D, FF), D ** -0.5, 0.1875, ((0, 4), (1, 2)))
    w_up = normal_values(keys[8], (D, FF), D ** -0.5, 0.1875, ((0, 4), (1, 2)))
    w_down = normal_values(keys[9], (FF, D), FF ** -0.5, 0.125, ((0, 2), (1, 4)))
    return {"tokens": tokens, "doc_start": doc_start, "cotangent": cotangent, "attn_gain": attn_gain, "mlp_gain": mlp_gain, "w_qkv": w_qkv, "w_out": w_out, "w_gate": w_gate, "w_up": w_up, "w_down": w_down}


EPS = 1e-05
THETA = 100000.0
NEG = -1e+30
HIGH = lax.Precision.HIGHEST

@jax.custom_vjp
def low(v):
    return lax.optimization_barrier(v.astype(jnp.bfloat16)).astype(jnp.float32)

@jax.custom_vjp
def low_back(v):
    return v

def low_keep(v):
    return (low(v), None)

def low_pass(kept, grad):
    return (grad,)

def back_keep(v):
    return (v, None)

def back_low(kept, grad):
    return (low(grad),)
low.defvjp(low_keep, low_pass)
low_back.defvjp(back_keep, back_low)

def matmul(left, right):
    return jnp.dot(left, right, precision=HIGH, preferred_element_type=jnp.float32)

def frequencies():
    half_size = HEAD // 2
    return jnp.power(THETA, -jnp.arange(half_size, dtype=jnp.float32) / half_size)

def rotate(values, cosine_table, sine_table):
    half_size = values.shape[-1] // 2
    front_half = values[..., :half_size]
    back_half = values[..., half_size:]
    return jnp.concatenate([front_half * cosine_table - back_half * sine_table, back_half * cosine_table + front_half * sine_table], axis=-1)

def rms_norm(values, gain_row):
    norm_scale = lax.rsqrt(lax.optimization_barrier(jnp.mean(values * values, axis=1, keepdims=True)) + EPS)
    return values * norm_scale * gain_row

def attend_block(items):
    queries, key_rows, value_rows, starts, places = items
    length = queries.shape[0]
    grouped = queries.reshape(length, KV_HEADS, HEADS // KV_HEADS, HEAD)
    scores = jnp.einsum('qgrd,kgd->grqk', grouped, key_rows, precision=HIGH)
    scores = low_back(scores * HEAD ** (-0.5))
    allowed = (places[None, :] >= starts[:, None]) & (places[None, :] <= places[:, None])
    masked = jnp.where(allowed[None, None], scores, NEG)
    row_max = lax.optimization_barrier(jnp.max(masked, axis=-1, keepdims=True))
    exp_scores = jnp.exp(masked - row_max)
    soft_rows = exp_scores / lax.optimization_barrier(jnp.sum(exp_scores, axis=-1, keepdims=True))
    mixed_rows = jnp.einsum('grqk,kgd->qgrd', low(soft_rows), value_rows, precision=HIGH)
    return mixed_rows.reshape(length, HEADS * HEAD)

def layer(inputs, starts, places, params):
    attn_gain, mlp_gain, w_qkv, w_out, w_gate, w_up, w_down = params
    row_count = inputs.shape[0]
    query_width = HEADS * HEAD
    kv_width = KV_HEADS * HEAD
    normed = low(rms_norm(inputs, attn_gain))
    projected = low_back(low(matmul(normed, w_qkv)))
    angle = (places - starts).astype(jnp.float32)[:, None] * frequencies()[None, :]
    cosine_table = jnp.cos(angle)[:, None, :]
    sine_table = jnp.sin(angle)[:, None, :]
    queries = low(rotate(projected[:, :query_width].reshape(row_count, HEADS, HEAD), cosine_table, sine_table))
    key_rows = low(rotate(projected[:, query_width:query_width + kv_width].reshape(row_count, KV_HEADS, HEAD), cosine_table, sine_table))
    value_rows = projected[:, query_width + kv_width:].reshape(row_count, KV_HEADS, HEAD)
    block_len = 2 * TOK_DEV
    block_count = row_count // block_len
    mixed = lax.map(jax.checkpoint(attend_block), (queries.reshape(block_count, block_len, HEADS, HEAD), key_rows.reshape(block_count, block_len, KV_HEADS, HEAD), value_rows.reshape(block_count, block_len, KV_HEADS, HEAD), starts.reshape(block_count, block_len), places.reshape(block_count, block_len)))
    mixed = low_back(low(mixed.reshape(row_count, query_width)))
    middle = inputs + low_back(matmul(mixed, w_out))
    normed_two = low(rms_norm(middle, mlp_gain))
    gate = low_back(matmul(normed_two, w_gate))
    up_part = low_back(matmul(normed_two, w_up))
    hidden = low(jax.nn.silu(gate) * up_part)
    return middle + matmul(hidden, w_down)

def reference(tokens, doc_start, cotangent, attn_gain, mlp_gain, w_qkv, w_out, w_gate, w_up, w_down):
    params = (attn_gain.astype(jnp.float32), mlp_gain.astype(jnp.float32), w_qkv.astype(jnp.float32), w_out.astype(jnp.float32), w_gate.astype(jnp.float32), w_up.astype(jnp.float32), w_down.astype(jnp.float32))
    step_rows = SEQ_LEN
    step_count = TOKENS // step_rows
    inputs = tokens.astype(jnp.float32).T.reshape(step_count, step_rows, D)
    upstream = cotangent.astype(jnp.float32).T.reshape(step_count, step_rows, D)
    starts = doc_start.astype(jnp.int32).reshape(step_count, step_rows)
    places = jnp.arange(TOKENS, dtype=jnp.int32).reshape(step_count, step_rows)

    def one_step(totals, items):
        rows_in, rows_up, rows_start, rows_place = items

        def forward(values, weights):
            return layer(values, rows_start, rows_place, weights)
        output, pull = jax.vjp(forward, rows_in, params)
        in_grad, weight_grads = pull(rows_up)
        totals = jax.tree.map(lambda left, right: left + right, totals, weight_grads)
        return (totals, (output.astype(jnp.bfloat16), in_grad.astype(jnp.bfloat16)))
    initial = jax.tree.map(jnp.zeros_like, params)
    totals, outputs = lax.scan(one_step, initial, (inputs, upstream, starts, places))
    result_rows, grad_rows = outputs
    return (result_rows.reshape(TOKENS, D).T, grad_rows.reshape(TOKENS, D).T, totals[2], totals[3], totals[4], totals[5], totals[6], totals[0], totals[1])
```

```python
import functools

import jax
import jax.numpy as jnp
from jax import lax
from jax.experimental import pallas as pl
from jax.experimental.pallas import tpu as pltpu
from jax.sharding import PartitionSpec as P

HEADS = 15
KV_HEADS = 5
GROUP = HEADS // KV_HEADS
HEAD = 64
HALF = HEAD // 2
PRIOR = 512
TILE = 256

EPS = 1e-05
THETA = 100000.0
NEG = -1e30

BF = jnp.bfloat16
F32 = jnp.float32


def swap(value, axis, by):
    peers = lax.axis_size(axis)
    return lax.ppermute(value, axis, [(i, i ^ by) for i in range(peers)])


def dot(left, right, left_dim, right_dim):
    return lax.dot_general(
        left, right, (((left_dim,), (right_dim,)), ((), ())), preferred_element_type=F32
    )


def add(left, right):
    return (left.astype(F32) + right.astype(F32)).astype(BF)


def frequencies():
    return jnp.power(THETA, -jnp.arange(HALF, dtype=F32) / HALF)


def to_tokens(shard):
    peers = lax.axis_size("gy")
    me = lax.axis_index("gy")
    rows = shard.shape[1] // peers
    blocks = []
    for by in range(peers):
        piece = lax.dynamic_slice_in_dim(shard, (me ^ by) * rows, rows, 1)
        blocks.append(swap(piece, "gy", by) if by else piece)
    return jnp.concatenate(blocks, axis=0)


def to_features(full):
    peers = lax.axis_size("gy")
    me = lax.axis_index("gy")
    block, rows = full.shape[0] // peers, full.shape[1]
    out = jnp.zeros((block, rows * peers), full.dtype)
    for by in range(peers):
        piece = full[by * block : (by + 1) * block]
        piece = swap(piece, "gy", by) if by else piece
        out = lax.dynamic_update_slice_in_dim(out, piece, (me ^ by) * rows, 1)
    return out


def reorder(vector):
    peers = lax.axis_size("gy")
    me = lax.axis_index("gy")
    block = vector.shape[0] // peers
    return jnp.concatenate(
        [lax.dynamic_slice_in_dim(vector, (me ^ by) * block, block, 0) for by in range(peers)]
    )


def gather_x(block, dim):
    if lax.axis_size("gx") == 2:
        return [block, swap(block, "gx", 1)]
    whole = lax.all_gather(block, "gx", axis=dim, tiled=True)
    half = whole.shape[dim] // 2
    return [
        lax.slice_in_dim(whole, 0, half, axis=dim),
        lax.slice_in_dim(whole, half, 2 * half, axis=dim),
    ]


def reduce_x(chunks, dim):
    if lax.axis_size("gx") == 2:
        return add(chunks[0], swap(chunks[1], "gx", 1))
    return lax.psum_scatter(
        jnp.concatenate(chunks, axis=dim), "gx", scatter_dimension=dim, tiled=True
    )


def gather_blocks(shard, dim):
    far = swap(shard, "gy", 2)
    own = gather_x(shard, dim)
    far = gather_x(far, dim)
    return [
        [own[c], swap(own[c], "gy", 1), far[c], swap(far[c], "gy", 1)] for c in range(2)
    ]


def join_x(chunks, dim):
    if lax.axis_size("gx") == 2:
        first = lax.axis_index("gx") == 0
        low = jnp.where(first, chunks[0], chunks[1])
        high = jnp.where(first, chunks[1], chunks[0])
        return jnp.concatenate([low, high], axis=dim)
    return jnp.concatenate(chunks, axis=dim)


def split_x(whole, dim):
    half = whole.shape[dim] // 2
    if lax.axis_size("gx") == 2:
        me = lax.axis_index("gx")
        return [
            lax.dynamic_slice_in_dim(whole, me * half, half, dim),
            lax.dynamic_slice_in_dim(whole, (1 - me) * half, half, dim),
        ]
    return [
        lax.slice_in_dim(whole, 0, half, axis=dim),
        lax.slice_in_dim(whole, half, 2 * half, axis=dim),
    ]


def sum_z(value):
    peers = lax.axis_size("dp")
    if peers != 4:
        return lax.psum(value.astype(F32), "dp")
    me = lax.axis_index("dp")
    inner = add(value, lax.ppermute(value, "dp", [(0, 1), (3, 2)]))
    total = add(inner, lax.ppermute(inner, "dp", [(1, 2), (2, 1)]))
    outer = lax.ppermute(total, "dp", [(1, 0), (2, 3)])
    return jnp.where((me == 0) | (me == 3), outer, total).astype(F32)


def reduce_blocks(chunks, dim):
    near, far = [], []
    for blocks in chunks:
        near.append(add(blocks[0], swap(blocks[1], "gy", 1)))
        far.append(add(blocks[2], swap(blocks[3], "gy", 1)))
    far = reduce_x(far, dim)
    near = reduce_x(near, dim)
    return sum_z(add(near, swap(far, "gy", 2)))


def reduce_joined(blocks, dim):
    near = add(blocks[0], swap(blocks[1], "gy", 1))
    far = add(blocks[2], swap(blocks[3], "gy", 1))
    far = reduce_x(split_x(far, dim), dim)
    near = reduce_x(split_x(near, dim), dim)
    return sum_z(add(near, swap(far, "gy", 2)))


def sum_all(value):
    for axis in ("gy", "gx", "dp"):
        by = 1
        while by < lax.axis_size(axis):
            value = value + swap(value, axis, by)
            by *= 2
    return value


RANGES = ((0, 768), (0, 1024), (512, 1280), (512, 1536))


def fill_bias(starts_ref, bias_ref):
    offset = 0
    for tile, (low, high) in enumerate(RANGES):
        size = high - low
        place = lax.broadcasted_iota(jnp.int32, (size, TILE), 0) + (low - PRIOR)
        query = lax.broadcasted_iota(jnp.int32, (size, TILE), 1) + tile * TILE
        start = starts_ref[:, tile * TILE : (tile + 1) * TILE]
        allowed = (place >= start) & (place <= query)
        bias_ref[offset : offset + size, :] = jnp.where(allowed, 0.0, NEG)
        offset += size


BIAS_ROWS = sum(high - low for low, high in RANGES)


def turned(prior_ref, own_ref, out_ref):
    out_ref[:PRIOR, :] = prior_ref[...].astype(F32).T.astype(BF)
    out_ref[PRIOR:, :] = own_ref[...].astype(F32).T.astype(BF)


def forward_kernel(
    starts_ref, q_ref, kp_ref, ko_ref, vp_ref, vo_ref, mixed_ref, lse_ref, keys, values, bias
):
    @pl.when(pl.program_id(0) == 0)
    def _():
        fill_bias(starts_ref, bias)

    turned(kp_ref, ko_ref, keys)
    values[:, :PRIOR] = vp_ref[...]
    values[:, PRIOR:] = vo_ref[...]
    offset = 0
    for tile, (low, high) in enumerate(RANGES):
        size = high - low
        lanes = slice(tile * TILE, (tile + 1) * TILE)
        for head in range(GROUP):
            rows = slice(head * HEAD, (head + 1) * HEAD)
            scores = dot(keys[low:high, :], q_ref[rows, lanes], 1, 0)
            scores = scores + bias[offset : offset + size, :]
            top = jnp.max(scores, axis=0, keepdims=True)
            weights = jnp.exp(scores - top)
            total = jnp.sum(weights, axis=0, keepdims=True)
            out = dot(values[:, low:high], weights.astype(BF), 1, 0)
            mixed_ref[rows, lanes] = (out / total).astype(BF)
            lse_ref[0, head : head + 1, lanes] = top + jnp.log(total)
        offset += size


def attention_forward(starts, queries, prior_k, own_k, prior_v, own_v):
    count = queries.shape[1]
    wide = GROUP * HEAD
    prior = pl.BlockSpec((HEAD, PRIOR), lambda g: (g, 0))
    own = pl.BlockSpec((HEAD, count), lambda g: (g, 0))
    return pl.pallas_call(
        forward_kernel,
        grid=(KV_HEADS,),
        in_specs=[
            pl.BlockSpec((1, count), lambda g: (0, 0)),
            pl.BlockSpec((wide, count), lambda g: (g, 0)),
            prior,
            own,
            prior,
            own,
        ],
        out_specs=[
            pl.BlockSpec((wide, count), lambda g: (g, 0)),
            pl.BlockSpec((1, 8, count), lambda g: (g, 0, 0)),
        ],
        out_shape=[
            jax.ShapeDtypeStruct((HEADS * HEAD, count), BF),
            jax.ShapeDtypeStruct((KV_HEADS, 8, count), F32),
        ],
        scratch_shapes=[
            pltpu.VMEM((PRIOR + count, HEAD), BF),
            pltpu.VMEM((HEAD, PRIOR + count), BF),
            pltpu.VMEM((BIAS_ROWS, TILE), F32),
        ],
        compiler_params=pltpu.CompilerParams(vmem_limit_bytes=40 * 2**20),
        cost_estimate=pl.CostEstimate(
            flops=2 * 2 * HEADS * BIAS_ROWS * TILE * 256,
            bytes_accessed=8 * 2**20,
            transcendentals=HEADS * BIAS_ROWS * TILE,
        ),
        name="attend_forward",
    )(starts, queries, prior_k, own_k, prior_v, own_v)


def backward_kernel(
    starts_ref,
    cos_ref,
    sin_ref,
    q_ref,
    kp_ref,
    ko_ref,
    vp_ref,
    vo_ref,
    mixed_ref,
    lse_ref,
    grad_ref,
    dq_ref,
    dkp_ref,
    dko_ref,
    dvp_ref,
    dvo_ref,
    keys,
    turned_keys,
    turned_values,
    dk,
    dv,
    bias,
):
    @pl.when(pl.program_id(0) == 0)
    def _():
        fill_bias(starts_ref, bias)

    turned(kp_ref, ko_ref, turned_keys)
    turned(vp_ref, vo_ref, turned_values)
    keys[:, :PRIOR] = kp_ref[...]
    keys[:, PRIOR:] = ko_ref[...]
    dk[...] = jnp.zeros_like(dk)
    dv[...] = jnp.zeros_like(dv)
    offset = 0
    for tile, (low, high) in enumerate(RANGES):
        size = high - low
        lanes = slice(tile * TILE, (tile + 1) * TILE)
        for head in range(GROUP):
            rows = slice(head * HEAD, (head + 1) * HEAD)
            query = q_ref[rows, lanes]
            grad = grad_ref[rows, lanes]
            inner = jnp.sum(
                grad.astype(F32) * mixed_ref[rows, lanes].astype(F32), axis=0, keepdims=True
            )
            lse = lse_ref[0, head : head + 1, lanes]
            scores = dot(turned_keys[low:high, :], query, 1, 0)
            weights = jnp.exp(scores + bias[offset : offset + size, :] - lse)
            prob_grad = dot(turned_values[low:high, :], grad, 1, 0)
            score_grad = (weights * (prob_grad - inner)).astype(BF)
            weights = weights.astype(BF)
            dv[low:high, :] += dot(weights, grad, 1, 1)
            dk[low:high, :] += dot(score_grad, query, 1, 1)
            dq = dot(keys[:, low:high], score_grad, 1, 0) * HEAD ** (-0.5)
            cosine, sine = cos_ref[:, lanes], sin_ref[:, lanes]
            front, back = dq[:HALF], dq[HALF:]
            base = head * HEAD
            dq_ref[base : base + HALF, lanes] = (front * cosine + back * sine).astype(BF)
            dq_ref[base + HALF : base + HEAD, lanes] = (back * cosine - front * sine).astype(BF)
        offset += size
    dkp_ref[...] = dk[:PRIOR, :].T.astype(BF)
    dvp_ref[...] = dv[:PRIOR, :].T.astype(BF)
    dko_ref[...] = dk[PRIOR:, :].T
    dvo_ref[...] = dv[PRIOR:, :].T


def attention_backward(
    starts, cosine, sine, queries, prior_k, own_k, prior_v, own_v, mixed, lse, grads
):
    count = queries.shape[1]
    wide = GROUP * HEAD
    prior = pl.BlockSpec((HEAD, PRIOR), lambda g: (g, 0))
    own = pl.BlockSpec((HEAD, count), lambda g: (g, 0))
    heads = pl.BlockSpec((wide, count), lambda g: (g, 0))
    table = pl.BlockSpec((HALF, count), lambda g: (0, 0))
    return pl.pallas_call(
        backward_kernel,
        grid=(KV_HEADS,),
        in_specs=[
            pl.BlockSpec((1, count), lambda g: (0, 0)),
            table,
            table,
            heads,
            prior,
            own,
            prior,
            own,
            heads,
            pl.BlockSpec((1, 8, count), lambda g: (g, 0, 0)),
            heads,
        ],
        out_specs=[heads, prior, own, prior, own],
        out_shape=[
            jax.ShapeDtypeStruct((HEADS * HEAD, count), BF),
            jax.ShapeDtypeStruct((KV_HEADS * HEAD, PRIOR), BF),
            jax.ShapeDtypeStruct((KV_HEADS * HEAD, count), F32),
            jax.ShapeDtypeStruct((KV_HEADS * HEAD, PRIOR), BF),
            jax.ShapeDtypeStruct((KV_HEADS * HEAD, count), F32),
        ],
        scratch_shapes=[
            pltpu.VMEM((HEAD, PRIOR + count), BF),
            pltpu.VMEM((PRIOR + count, HEAD), BF),
            pltpu.VMEM((PRIOR + count, HEAD), BF),
            pltpu.VMEM((PRIOR + count, HEAD), F32),
            pltpu.VMEM((PRIOR + count, HEAD), F32),
            pltpu.VMEM((BIAS_ROWS, TILE), F32),
        ],
        compiler_params=pltpu.CompilerParams(vmem_limit_bytes=44 * 2**20),
        cost_estimate=pl.CostEstimate(
            flops=5 * 2 * HEADS * BIAS_ROWS * TILE * 256,
            bytes_accessed=16 * 2**20,
            transcendentals=HEADS * BIAS_ROWS * TILE,
        ),
        name="attend_backward",
    )(starts, cosine, sine, queries, prior_k, own_k, prior_v, own_v, mixed, lse, grads)


def mlp_kernel(first, *refs):
    normed_ref, up_ref, base_ref = refs[:3]
    refs = refs[3:]
    if not first:
        grad_in_ref, refs = refs[0], refs[1:]
    gates, ups, downs = refs[0:4], refs[4:8], refs[8:12]
    out_ref, grad_out_ref = refs[12:14]
    gate_grads, up_grads, down_grads = refs[14:18], refs[18:22], refs[22:26]
    total_ref, grad_total_ref = refs[26:28]
    step = pl.program_id(0)
    last = pl.num_programs(0) - 1

    @pl.when(step == 0)
    def _():
        total_ref[...] = base_ref[...]
        if first:
            grad_total_ref[...] = jnp.zeros_like(grad_total_ref)
        else:
            grad_total_ref[...] = grad_in_ref[...]

    normed = normed_ref[...]
    block = normed.shape[0] // 4
    w_gate = jnp.concatenate([ref[...] for ref in gates], axis=0)
    w_up = jnp.concatenate([ref[...] for ref in ups], axis=0)
    gate = dot(w_gate, normed, 0, 0)
    up = dot(w_up, normed, 0, 0)
    sigmoid = 1.0 / (1.0 + jnp.exp(-gate))
    silu = gate * sigmoid
    hidden = (silu * up).astype(BF)
    hidden_grad = dot(downs[0][...], up_ref[:block, :], 1, 0)
    for j in range(1, 4):
        hidden_grad += dot(downs[j][...], up_ref[j * block : (j + 1) * block, :], 1, 0)
    gate_grad = (hidden_grad * up * (sigmoid * (1.0 + gate * (1.0 - sigmoid)))).astype(BF)
    up_grad = (hidden_grad * silu).astype(BF)
    for j in range(4):
        rows = slice(j * block, (j + 1) * block)
        total_ref[rows, :] += dot(downs[j][...], hidden, 0, 0)
        down_grads[j][...] = dot(hidden, up_ref[rows, :], 1, 1).astype(BF)
    grad_total_ref[...] += dot(w_gate, gate_grad, 1, 0) + dot(w_up, up_grad, 1, 0)
    made = dot(normed, gate_grad, 1, 1).astype(BF)
    for j in range(4):
        gate_grads[j][...] = made[j * block : (j + 1) * block]
    made = dot(normed, up_grad, 1, 1).astype(BF)
    for j in range(4):
        up_grads[j][...] = made[j * block : (j + 1) * block]

    @pl.when(step == last)
    def _():
        out_ref[...] = total_ref[...].astype(out_ref.dtype)
        grad_out_ref[...] = grad_total_ref[...]


def mlp_chunk(normed, upstream, base, grad_in, gates, ups, downs):
    first = grad_in is None
    width, count = normed.shape
    block, size = gates[0].shape
    tile = TILE
    whole = pl.BlockSpec((width, count), lambda i: (0, 0), pipeline_mode=pl.Buffered(1))
    across = pl.BlockSpec((block, tile), lambda i: (0, i))
    down = pl.BlockSpec((tile, block), lambda i: (i, 0))
    operands = [normed, upstream, base] + ([] if first else [grad_in])
    return pl.pallas_call(
        functools.partial(mlp_kernel, first),
        grid=(size // tile,),
        in_specs=[whole] * len(operands) + [across] * 8 + [down] * 4,
        out_specs=[whole, whole] + [across] * 8 + [down] * 4,
        out_shape=[
            jax.ShapeDtypeStruct((width, count), F32 if first else BF),
            jax.ShapeDtypeStruct((width, count), F32),
        ]
        + [jax.ShapeDtypeStruct((block, size), BF)] * 8
        + [jax.ShapeDtypeStruct((size, block), BF)] * 4,
        scratch_shapes=[pltpu.VMEM((width, count), F32), pltpu.VMEM((width, count), F32)],
        compiler_params=pltpu.CompilerParams(vmem_limit_bytes=56 * 2**20),
        cost_estimate=pl.CostEstimate(
            flops=9 * 2 * width * count * size,
            bytes_accessed=30 * 2**20,
            transcendentals=size * count,
        ),
        name="feed_forward",
    )(*operands, *gates, *ups, *downs)


def norm_scale_of(values):
    return lax.rsqrt(jnp.mean(values * values, axis=0, keepdims=True) + EPS)


def norm_back(values, scale, gain, gradient):
    weighted = gradient * gain
    inner = jnp.mean(weighted * values, axis=0, keepdims=True)
    values_grad = scale * weighted - values * (scale * scale * scale) * inner
    return (values_grad, jnp.sum(gradient * values * scale, axis=1))


def rotate(values, cosine, sine):
    heads = values.shape[0] // HEAD
    count = values.shape[1]
    pairs = values.astype(F32).reshape(heads, 2, HALF, count)
    front, back = pairs[:, 0], pairs[:, 1]
    return jnp.stack(
        [front * cosine - back * sine, back * cosine + front * sine], axis=1
    ).reshape(heads * HEAD, count)


def on_device(
    tokens, doc_start, cotangent, attn_gain, mlp_gain, w_qkv, w_out, w_gate, w_up, w_down
):
    count = doc_start.shape[0]
    query_width = HEADS * HEAD
    kv_width = KV_HEADS * HEAD
    score_scale = HEAD ** (-0.5)

    inputs = to_tokens(tokens)
    qkv_chunks = gather_blocks(w_qkv, 1)
    full_qkv = join_x([jnp.concatenate(blocks, axis=0) for blocks in qkv_chunks], 1)
    out_chunks = gather_blocks(w_out, 0)
    full_out = join_x([jnp.concatenate(blocks, axis=1) for blocks in out_chunks], 0)
    upstream = to_tokens(cotangent)
    gate_chunks = gather_blocks(w_gate, 1)
    up_chunks = gather_blocks(w_up, 1)
    down_chunks = gather_blocks(w_down, 0)

    attn_gain = reorder(attn_gain)[:, None]
    mlp_gain = reorder(mlp_gain)[:, None]

    residual = inputs.astype(F32)
    scale_one = norm_scale_of(residual)
    normed_one = (residual * scale_one * attn_gain).astype(BF)
    projected = dot(full_qkv, normed_one, 0, 0).astype(BF)

    first_row = lax.axis_index(("dp", "gx", "gy")) * count
    places = first_row + jnp.arange(count, dtype=jnp.int32)
    angle = frequencies()[:, None] * (places - doc_start).astype(F32)[None, :]
    cosine, sine = jnp.cos(angle), jnp.sin(angle)
    starts = (doc_start - first_row)[None, :]

    queries = (rotate(projected[:query_width], cosine, sine) * score_scale).astype(BF)
    own_k = rotate(projected[query_width : query_width + kv_width], cosine, sine).astype(BF)
    own_v = projected[query_width + kv_width :]
    peers = lax.axis_size("gy")
    ahead = [(i, i + 1) for i in range(0, peers, 2)]
    behind = [(i + 1, i) for i in range(0, peers, 2)]
    prior_k = lax.ppermute(own_k[:, count - PRIOR :], "gy", ahead)
    prior_v = lax.ppermute(own_v[:, count - PRIOR :], "gy", ahead)

    mixed, lse = attention_forward(starts, queries, prior_k, own_k, prior_v, own_v)

    middle = residual + dot(full_out, mixed, 0, 0)
    scale_two = norm_scale_of(middle)
    normed_two = (middle * scale_two * mlp_gain).astype(BF)

    made = mlp_chunk(
        normed_two, upstream, middle, None, gate_chunks[0], up_chunks[0], down_chunks[0]
    )
    later = mlp_chunk(
        normed_two, upstream, made[0], made[1], gate_chunks[1], up_chunks[1], down_chunks[1]
    )
    result, normed_two_grad = later[0], later[1]
    shard_gate = reduce_blocks([made[2:6], later[2:6]], 1)
    shard_up = reduce_blocks([made[6:10], later[6:10]], 1)
    shard_down = reduce_blocks([made[10:14], later[10:14]], 0)
    result_shard = to_features(result)

    mid_grad, gain_two = norm_back(middle, scale_two, mlp_gain, normed_two_grad)
    mid_grad = mid_grad + upstream.astype(F32)
    branch_grad = mid_grad.astype(BF)
    mixed_grad = dot(full_out, branch_grad, 1, 0).astype(BF)
    grad_out = dot(mixed, branch_grad, 1, 1).astype(BF)
    width = grad_out.shape[1]
    block = width // 4
    shard_out = reduce_joined([grad_out[:, j * block : (j + 1) * block] for j in range(4)], 0)

    dq, dkp, dko, dvp, dvo = attention_backward(
        starts, cosine, sine, queries, prior_k, own_k, prior_v, own_v, mixed, lse, mixed_grad
    )
    sent_k = lax.ppermute(dkp, "gy", behind).astype(F32)
    sent_v = lax.ppermute(dvp, "gy", behind).astype(F32)
    zeros = jnp.zeros((kv_width, count - PRIOR), F32)
    dk = dko + jnp.concatenate([zeros, sent_k], axis=1)
    dv = dvo + jnp.concatenate([zeros, sent_v], axis=1)
    projected_grad = jnp.concatenate(
        [dq, rotate(dk, cosine, -sine).astype(BF), dv.astype(BF)], axis=0
    )
    grad_qkv = dot(normed_one, projected_grad, 1, 1).astype(BF)
    shard_qkv = reduce_joined([grad_qkv[j * block : (j + 1) * block] for j in range(4)], 1)
    normed_one_grad = dot(full_qkv, projected_grad, 1, 0)
    in_grad, gain_one = norm_back(residual, scale_one, attn_gain, normed_one_grad)
    grad_shard = to_features((in_grad + mid_grad).astype(BF))
    gain_one = sum_all(reorder(gain_one))
    gain_two = sum_all(reorder(gain_two))
    return (
        result_shard,
        grad_shard,
        shard_qkv,
        shard_out,
        shard_gate,
        shard_up,
        shard_down,
        gain_one,
        gain_two,
    )


def solution(mesh):
    placed = (
        P("gy", ("dp", "gx")),
        P(("dp", "gx", "gy")),
        P("gy", ("dp", "gx")),
        P(),
        P(),
        P("gy", "gx"),
        P("gx", "gy"),
        P("gy", "gx"),
        P("gy", "gx"),
        P("gx", "gy"),
    )
    return jax.shard_map(
        on_device,
        mesh=mesh,
        in_specs=placed,
        out_specs=(
            P("gy", ("dp", "gx")),
            P("gy", ("dp", "gx")),
            P("gy", "gx"),
            P("gx", "gy"),
            P("gy", "gx"),
            P("gy", "gx"),
            P("gx", "gy"),
            P(),
            P(),
        ),
        check_vma=False,
    )
```

```python
import functools

import jax
import jax.numpy as jnp
from jax import lax
from jax.experimental import pallas as pl
from jax.experimental.pallas import tpu as pltpu
from jax.sharding import PartitionSpec as P

HEADS = 15
KV_HEADS = 5
GROUP = HEADS // KV_HEADS
HEAD = 64
HALF = HEAD // 2
PRIOR = 512
TILE = 256

EPS = 1e-05
THETA = 100000.0
NEG = -1e30

TINY = pl.CostEstimate(flops=1000, bytes_accessed=1000, transcendentals=0)

BF = jnp.bfloat16
F32 = jnp.float32


def swap(value, axis, by):
    peers = lax.axis_size(axis)
    return lax.ppermute(value, axis, [(i, i ^ by) for i in range(peers)])


def dot(left, right, left_dim, right_dim):
    return lax.dot_general(
        left, right, (((left_dim,), (right_dim,)), ((), ())), preferred_element_type=F32
    )


def add(left, right):
    return (left.astype(F32) + right.astype(F32)).astype(BF)


def frequencies():
    return jnp.power(THETA, -jnp.arange(HALF, dtype=F32) / HALF)


def after(value, *earlier):
    return lax.optimization_barrier((value, earlier))[0]


def ordered(mine, theirs, bit, axis):
    return jnp.where(
        bit == 0,
        jnp.concatenate([mine, theirs], axis=axis),
        jnp.concatenate([theirs, mine], axis=axis),
    )


def tokens_far(shard):
    me = lax.axis_index("gy")
    pair = shard.shape[1] // 2
    other = lax.dynamic_slice_in_dim(shard, (1 - me // 2) * pair, pair, 1)
    return swap(other, "gy", 2)


def tokens_near(shard, far):
    me = lax.axis_index("gy")
    rows = far.shape[1] // 2
    own, mate = (me % 2) * rows, (1 - me % 2) * rows
    base = (me // 2) * 2 * rows
    sent = jnp.concatenate(
        [
            lax.dynamic_slice_in_dim(shard, base + mate, rows, 1),
            lax.dynamic_slice_in_dim(far, mate, rows, 1),
        ],
        axis=0,
    )
    got = swap(sent, "gy", 1)
    return (
        lax.dynamic_slice_in_dim(shard, base + own, rows, 1),
        got,
        lax.dynamic_slice_in_dim(far, own, rows, 1),
    )


def to_features(full):
    me = lax.axis_index("gy")
    block = full.shape[0] // 4
    sent = jnp.concatenate([full[block : 2 * block], full[3 * block :]], axis=0)
    got = swap(sent, "gy", 1)
    near = ordered(full[:block], got[:block], me % 2, 1)
    far = ordered(full[2 * block : 3 * block], got[block:], me % 2, 1)
    return near, swap(far, "gy", 2)


def assemble(near, far):
    return ordered(near, far, lax.axis_index("gy") // 2, 1)


def reorder(vector):
    me = lax.axis_index("gy")
    block = vector.shape[0] // 4
    return jnp.concatenate(
        [lax.dynamic_slice_in_dim(vector, (me ^ by) * block, block, 0) for by in range(4)]
    )


def gather_x(block):
    if lax.axis_size("gx") == 2:
        return [block, swap(block, "gx", 1)]
    whole = lax.all_gather(block, "gx", axis=1, tiled=True)
    half = whole.shape[1] // 2
    return [whole[:, :half], whole[:, half:]]


def split_x(whole):
    half = whole.shape[-1] // 2
    if lax.axis_size("gx") == 2:
        me = lax.axis_index("gx")
        return [
            lax.dynamic_slice_in_dim(whole, me * half, half, whole.ndim - 1),
            lax.dynamic_slice_in_dim(whole, (1 - me) * half, half, whole.ndim - 1),
        ]
    return [whole[..., :half], whole[..., half:]]


def reduce_x(chunks, dim=-1):
    if lax.axis_size("gx") == 2:
        return add(chunks[0], swap(chunks[1], "gx", 1))
    dim = chunks[0].ndim + dim
    return lax.psum_scatter(
        jnp.concatenate(chunks, axis=dim), "gx", scatter_dimension=dim, tiled=True
    )


def sum_z(value):
    peers = lax.axis_size("dp")
    if peers != 4:
        return lax.psum(value.astype(F32), "dp")
    me = lax.axis_index("dp")
    inner = add(value, lax.ppermute(value, "dp", [(0, 1), (3, 2)]))
    total = add(inner, lax.ppermute(inner, "dp", [(1, 2), (2, 1)]))
    outer = lax.ppermute(total, "dp", [(1, 0), (2, 3)])
    return jnp.where((me == 0) | (me == 3), outer, total).astype(F32)


def sum_all(value):
    for axis in ("gy", "gx", "dp"):
        by = 1
        while by < lax.axis_size(axis):
            value = value + swap(value, axis, by)
            by *= 2
    return value


RANGES = ((0, 768), (0, 1024), (512, 1280), (512, 1536))


def fill_bias(starts_ref, bias_ref):
    offset = 0
    for tile, (low, high) in enumerate(RANGES):
        size = high - low
        place = lax.broadcasted_iota(jnp.int32, (size, TILE), 0) + (low - PRIOR)
        query = lax.broadcasted_iota(jnp.int32, (size, TILE), 1) + tile * TILE
        start = starts_ref[:, tile * TILE : (tile + 1) * TILE]
        allowed = (place >= start) & (place <= query)
        bias_ref[offset : offset + size, :] = jnp.where(allowed, 0.0, NEG)
        offset += size


BIAS_ROWS = sum(high - low for low, high in RANGES)


def turned(prior, own, out_ref):
    out_ref[:PRIOR, :] = prior.astype(F32).T.astype(BF)
    out_ref[PRIOR:, :] = own.astype(F32).T.astype(BF)


def forward_kernel(
    starts_ref, q_ref, prior_ref, own_ref, mixed_ref, lse_ref, keys, values, bias
):
    @pl.when(pl.program_id(0) == 0)
    def _():
        fill_bias(starts_ref, bias)

    turned(prior_ref[0, :HEAD, :], own_ref[0, :HEAD, :], keys)
    values[:, :PRIOR] = prior_ref[0, HEAD:, :]
    values[:, PRIOR:] = own_ref[0, HEAD:, :]
    offset = 0
    for tile, (low, high) in enumerate(RANGES):
        size = high - low
        lanes = slice(tile * TILE, (tile + 1) * TILE)
        for head in range(GROUP):
            rows = slice(head * HEAD, (head + 1) * HEAD)
            scores = dot(keys[low:high, :], q_ref[rows, lanes], 1, 0)
            scores = scores + bias[offset : offset + size, :]
            top = jnp.max(scores, axis=0, keepdims=True)
            weights = jnp.exp(scores - top)
            total = jnp.sum(weights, axis=0, keepdims=True)
            out = dot(values[:, low:high], weights.astype(BF), 1, 0)
            mixed_ref[rows, lanes] = (out / total).astype(BF)
            lse_ref[0, head : head + 1, lanes] = top + jnp.log(total)
        offset += size


def attention_forward(starts, queries, prior_kv, own_kv):
    count = queries.shape[1]
    wide = GROUP * HEAD
    prior = pl.BlockSpec((1, 2 * HEAD, PRIOR), lambda g: (g, 0, 0))
    own = pl.BlockSpec((1, 2 * HEAD, count), lambda g: (g, 0, 0))
    return pl.pallas_call(
        forward_kernel,
        grid=(KV_HEADS,),
        in_specs=[
            pl.BlockSpec((1, count), lambda g: (0, 0)),
            pl.BlockSpec((wide, count), lambda g: (g, 0)),
            prior,
            own,
        ],
        out_specs=[
            pl.BlockSpec((wide, count), lambda g: (g, 0)),
            pl.BlockSpec((1, 8, count), lambda g: (g, 0, 0)),
        ],
        out_shape=[
            jax.ShapeDtypeStruct((HEADS * HEAD, count), BF),
            jax.ShapeDtypeStruct((KV_HEADS, 8, count), F32),
        ],
        scratch_shapes=[
            pltpu.VMEM((PRIOR + count, HEAD), BF),
            pltpu.VMEM((HEAD, PRIOR + count), BF),
            pltpu.VMEM((BIAS_ROWS, TILE), F32),
        ],
        compiler_params=pltpu.CompilerParams(vmem_limit_bytes=40 * 2**20),
        cost_estimate=TINY,
        name="attend_forward",
    )(starts, queries, prior_kv, own_kv)


def backward_kernel(
    starts_ref,
    cos_ref,
    sin_ref,
    q_ref,
    prior_ref,
    own_ref,
    mixed_ref,
    lse_ref,
    grad_ref,
    dq_ref,
    dprior_ref,
    down_ref,
    keys,
    turned_keys,
    turned_values,
    dk,
    dv,
    bias,
):
    @pl.when(pl.program_id(0) == 0)
    def _():
        fill_bias(starts_ref, bias)

    turned(prior_ref[0, :HEAD, :], own_ref[0, :HEAD, :], turned_keys)
    turned(prior_ref[0, HEAD:, :], own_ref[0, HEAD:, :], turned_values)
    keys[:, :PRIOR] = prior_ref[0, :HEAD, :]
    keys[:, PRIOR:] = own_ref[0, :HEAD, :]
    dk[...] = jnp.zeros_like(dk)
    dv[...] = jnp.zeros_like(dv)
    offset = 0
    for tile, (low, high) in enumerate(RANGES):
        size = high - low
        lanes = slice(tile * TILE, (tile + 1) * TILE)
        for head in range(GROUP):
            rows = slice(head * HEAD, (head + 1) * HEAD)
            query = q_ref[rows, lanes]
            grad = grad_ref[rows, lanes]
            inner = jnp.sum(
                grad.astype(F32) * mixed_ref[rows, lanes].astype(F32), axis=0, keepdims=True
            )
            lse = lse_ref[0, head : head + 1, lanes]
            scores = dot(turned_keys[low:high, :], query, 1, 0)
            weights = jnp.exp(scores + bias[offset : offset + size, :] - lse)
            prob_grad = dot(turned_values[low:high, :], grad, 1, 0)
            score_grad = (weights * (prob_grad - inner)).astype(BF)
            weights = weights.astype(BF)
            dv[low:high, :] += dot(weights, grad, 1, 1)
            dk[low:high, :] += dot(score_grad, query, 1, 1)
            dq = dot(keys[:, low:high], score_grad, 1, 0) * HEAD ** (-0.5)
            cosine, sine = cos_ref[:, lanes], sin_ref[:, lanes]
            front, back = dq[:HALF], dq[HALF:]
            base = head * HEAD
            dq_ref[base : base + HALF, lanes] = (front * cosine + back * sine).astype(BF)
            dq_ref[base + HALF : base + HEAD, lanes] = (back * cosine - front * sine).astype(BF)
        offset += size
    dprior_ref[0, :HEAD, :] = dk[:PRIOR, :].T.astype(BF)
    dprior_ref[0, HEAD:, :] = dv[:PRIOR, :].T.astype(BF)
    down_ref[0, :HEAD, :] = dk[PRIOR:, :].T
    down_ref[0, HEAD:, :] = dv[PRIOR:, :].T


def attention_backward(
    starts, cosine, sine, queries, prior_kv, own_kv, mixed, lse, grads
):
    count = queries.shape[1]
    wide = GROUP * HEAD
    prior = pl.BlockSpec((1, 2 * HEAD, PRIOR), lambda g: (g, 0, 0))
    own = pl.BlockSpec((1, 2 * HEAD, count), lambda g: (g, 0, 0))
    heads = pl.BlockSpec((wide, count), lambda g: (g, 0))
    table = pl.BlockSpec((HALF, count), lambda g: (0, 0))
    return pl.pallas_call(
        backward_kernel,
        grid=(KV_HEADS,),
        in_specs=[
            pl.BlockSpec((1, count), lambda g: (0, 0)),
            table,
            table,
            heads,
            prior,
            own,
            heads,
            pl.BlockSpec((1, 8, count), lambda g: (g, 0, 0)),
            heads,
        ],
        out_specs=[heads, prior, own],
        out_shape=[
            jax.ShapeDtypeStruct((HEADS * HEAD, count), BF),
            jax.ShapeDtypeStruct((KV_HEADS, 2 * HEAD, PRIOR), BF),
            jax.ShapeDtypeStruct((KV_HEADS, 2 * HEAD, count), F32),
        ],
        scratch_shapes=[
            pltpu.VMEM((HEAD, PRIOR + count), BF),
            pltpu.VMEM((PRIOR + count, HEAD), BF),
            pltpu.VMEM((PRIOR + count, HEAD), BF),
            pltpu.VMEM((PRIOR + count, HEAD), F32),
            pltpu.VMEM((PRIOR + count, HEAD), F32),
            pltpu.VMEM((BIAS_ROWS, TILE), F32),
        ],
        compiler_params=pltpu.CompilerParams(vmem_limit_bytes=44 * 2**20),
        cost_estimate=TINY,
        name="attend_backward",
    )(starts, cosine, sine, queries, prior_kv, own_kv, mixed, lse, grads)


def mlp_kernel(first, *refs):
    normed_ref, up_ref, base_ref = refs[:3]
    refs = refs[3:]
    if not first:
        grad_in_ref, refs = refs[0], refs[1:]
    blocks = refs[0:4]
    out_ref, grad_out_ref, keep_ref, send_ref, total_ref, grad_total_ref = refs[4:]
    step = pl.program_id(0)
    last = pl.num_programs(0) - 1

    @pl.when(step == 0)
    def _():
        total_ref[...] = base_ref[...]
        if first:
            grad_total_ref[...] = jnp.zeros_like(grad_total_ref)
        else:
            grad_total_ref[...] = grad_in_ref[...]

    normed = normed_ref[...]
    upstream = up_ref[...]
    block = normed.shape[0] // 4
    w_gate = jnp.concatenate([ref[:block] for ref in blocks], axis=0)
    w_up = jnp.concatenate([ref[block : 2 * block] for ref in blocks], axis=0)
    w_down = jnp.concatenate([ref[2 * block :] for ref in blocks], axis=0)
    gate = dot(w_gate, normed, 0, 0)
    up = dot(w_up, normed, 0, 0)
    hidden_grad = dot(w_down, upstream, 0, 0)
    sigmoid = 1.0 / (1.0 + jnp.exp(-gate))
    silu = gate * sigmoid
    hidden = (silu * up).astype(BF)
    gate_grad = (hidden_grad * up * (sigmoid * (1.0 + gate * (1.0 - sigmoid)))).astype(BF)
    up_grad = (hidden_grad * silu).astype(BF)
    total_ref[...] += dot(w_down, hidden, 1, 0)
    grad_total_ref[...] += dot(w_gate, gate_grad, 1, 0) + dot(w_up, up_grad, 1, 0)
    for place, (left, right) in enumerate(
        ((normed, gate_grad), (normed, up_grad), (upstream, hidden))
    ):
        made = dot(left, right, 1, 1).astype(BF)
        rows = slice(place * block, (place + 1) * block)
        keep_ref[0, rows, :] = made[:block]
        send_ref[0, rows, :] = made[block : 2 * block]
        keep_ref[1, rows, :] = made[2 * block : 3 * block]
        send_ref[1, rows, :] = made[3 * block :]

    @pl.when(step == last)
    def _():
        out_ref[...] = total_ref[...].astype(out_ref.dtype)
        grad_out_ref[...] = grad_total_ref[...]


def mlp_chunk(normed, upstream, base, grad_in, blocks):
    first = grad_in is None
    width, count = normed.shape
    rows, size = blocks[0].shape
    tile = TILE
    whole = pl.BlockSpec((width, count), lambda i: (0, 0), pipeline_mode=pl.Buffered(1))
    across = pl.BlockSpec((rows, tile), lambda i: (0, i))
    made = pl.BlockSpec((2, rows, tile), lambda i: (0, 0, i))
    operands = [normed, upstream, base] + ([] if first else [grad_in])
    return pl.pallas_call(
        functools.partial(mlp_kernel, first),
        grid=(size // tile,),
        in_specs=[whole] * len(operands) + [across] * 4,
        out_specs=[whole, whole, made, made],
        out_shape=[
            jax.ShapeDtypeStruct((width, count), F32 if first else BF),
            jax.ShapeDtypeStruct((width, count), F32),
            jax.ShapeDtypeStruct((2, rows, size), BF),
            jax.ShapeDtypeStruct((2, rows, size), BF),
        ],
        scratch_shapes=[pltpu.VMEM((width, count), F32), pltpu.VMEM((width, count), F32)],
        compiler_params=pltpu.CompilerParams(vmem_limit_bytes=56 * 2**20),
        cost_estimate=TINY,
        name="feed_forward",
    )(*operands, *blocks)


VMEM = pl.BlockSpec(memory_space=pltpu.VMEM)
SMEM = pl.BlockSpec(memory_space=pltpu.SMEM)
Q_WIDTH = HEADS * HEAD
KV_WIDTH = KV_HEADS * HEAD
QKV_WIDTH = Q_WIDTH + 2 * KV_WIDTH
QKV_PART = QKV_WIDTH // 2
OUT_PART = Q_WIDTH // 2


def place_of(flip_ref, half, size):
    return pl.ds(pl.multiple_of((flip_ref[0] ^ half) * size, 16), size)


def stacked(refs, columns):
    return jnp.concatenate([ref[:, columns] for ref in refs], axis=0)


QKV_COLUMNS = slice(0, QKV_PART)
OUT_COLUMNS = slice(QKV_PART, QKV_PART + OUT_PART)


def norm_scale_of(values):
    return lax.rsqrt(jnp.mean(values * values, axis=0, keepdims=True) + EPS)


def norm_back(values, scale, gain, gradient):
    weighted = gradient * gain
    inner = jnp.mean(weighted * values, axis=0, keepdims=True)
    values_grad = scale * weighted - values * (scale * scale * scale) * inner
    return (values_grad, jnp.sum(gradient * values * scale, axis=1, keepdims=True))


def project_kernel(flip_ref, near_ref, got_ref, far_ref, gain_ref, cos_ref, sin_ref, *refs):
    weights = refs[:8]
    x_ref, normed_ref, q_ref, own_ref, prior_ref, made = refs[8:]
    block = near_ref.shape[0]
    x_ref[:block, :] = near_ref[...]
    x_ref[block : 2 * block, :] = got_ref[:block, :]
    x_ref[2 * block : 3 * block, :] = far_ref[...]
    x_ref[3 * block :, :] = got_ref[block:, :]
    x = x_ref[...].astype(F32)
    normed = (x * norm_scale_of(x) * gain_ref[...]).astype(BF)
    normed_ref[...] = normed
    for half in range(2):
        weight = stacked(weights[4 * half : 4 * half + 4], QKV_COLUMNS)
        made[place_of(flip_ref, half, QKV_PART), :] = dot(weight, normed, 0, 0).astype(BF)
    cosine, sine = cos_ref[...], sin_ref[...]
    count = cosine.shape[1]

    def rotated(base, scale):
        front = made[base : base + HALF, :].astype(F32)
        back = made[base + HALF : base + HEAD, :].astype(F32)
        return (
            ((front * cosine - back * sine) * scale).astype(BF),
            ((back * cosine + front * sine) * scale).astype(BF),
        )

    for head in range(HEADS):
        base = head * HEAD
        front, back = rotated(base, HEAD ** (-0.5))
        q_ref[base : base + HALF, :] = front
        q_ref[base + HALF : base + HEAD, :] = back
    for head in range(KV_HEADS):
        front, back = rotated(Q_WIDTH + head * HEAD, 1.0)
        base = Q_WIDTH + KV_WIDTH + head * HEAD
        value = made[base : base + HEAD, :]
        own_ref[head, :HALF, :] = front
        own_ref[head, HALF:HEAD, :] = back
        own_ref[head, HEAD:, :] = value
        prior_ref[head, :HALF, :] = front[:, count - PRIOR :]
        prior_ref[head, HALF:HEAD, :] = back[:, count - PRIOR :]
        prior_ref[head, HEAD:, :] = value[:, count - PRIOR :]


def call_whole(kernel, name, ins, outs, scratch=()):
    return pl.pallas_call(
        kernel,
        in_specs=[SMEM] + [VMEM] * (len(ins) - 1),
        out_specs=[VMEM] * len(outs),
        out_shape=[jax.ShapeDtypeStruct(shape, kind) for shape, kind in outs],
        scratch_shapes=list(scratch),
        compiler_params=pltpu.CompilerParams(vmem_limit_bytes=56 * 2**20),
        cost_estimate=TINY,
        name=name,
    )(*ins)


def project(flip, pieces, gain, cosine, sine, weights):
    block, count = pieces[0].shape
    width = 4 * block
    return call_whole(
        project_kernel,
        "project",
        (flip, *pieces, gain, cosine, sine, *weights),
        (
            ((width, count), BF),
            ((width, count), BF),
            ((Q_WIDTH, count), BF),
            ((KV_HEADS, 2 * HEAD, count), BF),
            ((KV_HEADS, 2 * HEAD, PRIOR), BF),
        ),
        (pltpu.VMEM((QKV_WIDTH, count), BF),),
    )


def branch_kernel(flip_ref, x_ref, gain_ref, mixed_ref, *refs):
    weights = refs[:8]
    middle_ref, normed_ref = refs[8:]
    middle = x_ref[...].astype(F32)
    for half in range(2):
        weight = stacked(weights[4 * half : 4 * half + 4], OUT_COLUMNS)
        middle = middle + dot(weight, mixed_ref[place_of(flip_ref, half, OUT_PART), :], 1, 0)
    middle_ref[...] = middle
    normed_ref[...] = (middle * norm_scale_of(middle) * gain_ref[...]).astype(BF)


def branch(flip, inputs, gain, mixed, weights):
    shape = inputs.shape
    return call_whole(
        branch_kernel,
        "branch",
        (flip, inputs, gain, mixed, *weights),
        ((shape, F32), (shape, BF)),
    )


def store_blocks(keep_ref, send_ref, half, made):
    block = made.shape[0] // 4
    keep_ref[half, 0] = made[:block]
    send_ref[half, 0] = made[block : 2 * block]
    keep_ref[half, 1] = made[2 * block : 3 * block]
    send_ref[half, 1] = made[3 * block :]


def branch_back_kernel(flip_ref, grad_ref, middle_ref, up_ref, gain_ref, mixed_ref, *refs):
    weights = refs[:8]
    mid_grad_ref, mixed_grad_ref, gain_grad_ref, keep_ref, send_ref = refs[8:]
    middle = middle_ref[...]
    mid_grad, gain_grad = norm_back(
        middle, norm_scale_of(middle), gain_ref[...], grad_ref[...]
    )
    gain_grad_ref[...] = gain_grad
    mid_grad = mid_grad + up_ref[...].astype(F32)
    mid_grad_ref[...] = mid_grad
    branch_grad = mid_grad.astype(BF)
    for half in range(2):
        place = place_of(flip_ref, half, OUT_PART)
        weight = stacked(weights[4 * half : 4 * half + 4], OUT_COLUMNS)
        mixed_grad_ref[place, :] = dot(weight, branch_grad, 0, 0).astype(BF)
        made = dot(branch_grad, mixed_ref[place, :], 1, 1).astype(BF)
        store_blocks(keep_ref, send_ref, half, made)


def branch_back(flip, grad, middle, upstream, gain, mixed, weights):
    width, count = middle.shape
    parts = (2, 2, width // 4, OUT_PART)
    return call_whole(
        branch_back_kernel,
        "branch_back",
        (flip, grad, middle, upstream, gain, mixed, *weights),
        (
            ((width, count), F32),
            ((Q_WIDTH, count), BF),
            ((width, 1), F32),
            (parts, BF),
            (parts, BF),
        ),
    )


def qkv_grad_kernel(
    flip_ref, normed_ref, dq_ref, own_ref, prior_ref, cos_ref, sin_ref, made_ref, keep_ref, send_ref
):
    made_ref[:Q_WIDTH, :] = dq_ref[...]
    count = own_ref.shape[2]
    cosine, sine = cos_ref[...], sin_ref[...]
    for head in range(KV_HEADS):
        sent = prior_ref[head].astype(F32)
        both = jnp.concatenate(
            [own_ref[head, :, : count - PRIOR], own_ref[head, :, count - PRIOR :] + sent], axis=1
        )
        front, back = both[:HALF], both[HALF:HEAD]
        base = Q_WIDTH + head * HEAD
        made_ref[base : base + HALF, :] = (front * cosine + back * sine).astype(BF)
        made_ref[base + HALF : base + HEAD, :] = (back * cosine - front * sine).astype(BF)
        base += KV_WIDTH
        made_ref[base : base + HEAD, :] = both[HEAD:].astype(BF)
    normed = normed_ref[...]
    block = normed.shape[0] // 4
    for half in range(2):
        grads = made_ref[place_of(flip_ref, half, QKV_PART), :]
        for number in range(4):
            rows = normed[number * block : (number + 1) * block]
            target = send_ref if number % 2 else keep_ref
            target[half, number // 2] = dot(grads, rows, 1, 1).astype(BF)


def qkv_grad(flip, normed, dq, own, prior, cosine, sine):
    width, count = normed.shape
    parts = (2, 2, QKV_PART, width // 4)
    return call_whole(
        qkv_grad_kernel,
        "qkv_grad",
        (flip, normed, dq, own, prior, cosine, sine),
        (((QKV_WIDTH, count), BF), (parts, BF), (parts, BF)),
    )


def input_grad_kernel(flip_ref, grads_ref, x_ref, gain_ref, mid_grad_ref, *refs):
    weights = refs[:8]
    out_ref, gain_grad_ref = refs[8:]
    total = jnp.zeros(x_ref.shape, F32)
    for half in range(2):
        weight = stacked(weights[4 * half : 4 * half + 4], QKV_COLUMNS)
        total = total + dot(weight, grads_ref[place_of(flip_ref, half, QKV_PART), :], 1, 0)
    x = x_ref[...].astype(F32)
    grad, gain_grad = norm_back(x, norm_scale_of(x), gain_ref[...], total)
    gain_grad_ref[...] = gain_grad
    out_ref[...] = (grad + mid_grad_ref[...]).astype(BF)


def input_grad(flip, grads, inputs, gain, mid_grad, weights):
    width, count = inputs.shape
    return call_whole(
        input_grad_kernel,
        "input_grad",
        (flip, grads, inputs, gain, mid_grad, *weights),
        (((width, count), BF), ((width, 1), F32)),
    )


def attention_halves(shard, cut):
    if lax.axis_size("gx") == 2:
        return [shard, swap(shard, "gx", 1)]
    peers = lax.axis_size("gx")
    block, width = shard.shape
    whole = lax.all_gather(shard, "gx", axis=1, tiled=True)
    whole = whole.reshape(block, 2, peers // 2, width)
    return [
        jnp.concatenate(
            [
                whole[:, c, :, :cut].reshape(block, peers // 2 * cut),
                whole[:, c, :, cut:].reshape(block, peers // 2 * (width - cut)),
            ],
            axis=1,
        )
        for c in range(2)
    ]


def on_device(
    tokens, doc_start, cotangent, attn_gain, mlp_gain, w_qkv, w_out, w_gate, w_up, w_down
):
    count = doc_start.shape[0]
    block = w_qkv.shape[0]
    pairs_x = lax.axis_size("gx") == 2
    flip = lax.axis_index("gx") if pairs_x else jnp.int32(0)
    flip = jnp.reshape(flip, (1,)).astype(jnp.int32)

    shard = jnp.concatenate([w_qkv, w_out.T], axis=1)
    shard_far = swap(shard, "gy", 2)
    inputs_far = tokens_far(tokens)
    near_halves = attention_halves(shard, w_qkv.shape[1])
    far_halves = attention_halves(shard_far, w_qkv.shape[1])
    weights = []
    for near, far in zip(near_halves, far_halves):
        weights += [near, swap(near, "gy", 1), far, swap(far, "gy", 1)]
    pieces = tokens_near(tokens, inputs_far)

    ff_shard = jnp.concatenate([w_gate, w_up, w_down.T], axis=0)
    ff_shard = after(ff_shard, inputs_far, *near_halves, *far_halves)
    ff_far = swap(ff_shard, "gy", 2)
    ff_near_halves = gather_x(ff_shard)
    ff_mate = swap(ff_shard, "gy", 1)

    attn_gain = reorder(attn_gain)[:, None]
    mlp_gain = reorder(mlp_gain)[:, None]

    first_row = lax.axis_index(("dp", "gx", "gy")) * count
    places = first_row + jnp.arange(count, dtype=jnp.int32)
    angle = frequencies()[:, None] * (places - doc_start).astype(F32)[None, :]
    cosine, sine = jnp.cos(angle), jnp.sin(angle)
    starts = (doc_start - first_row)[None, :]

    inputs, normed_one, queries, own_kv, sent_kv = project(
        flip, pieces, attn_gain, cosine, sine, weights
    )
    cotangent = after(cotangent, sent_kv)
    upstream_far = tokens_far(cotangent)
    peers = lax.axis_size("gy")
    ahead = [(i, i + 1) for i in range(0, peers, 2)]
    behind = [(i + 1, i) for i in range(0, peers, 2)]
    prior_kv = lax.ppermute(sent_kv, "gy", ahead)
    mixed, lse = attention_forward(starts, queries, prior_kv, own_kv)

    ff_far, ff_other, upstream_far = after((ff_far, ff_near_halves[1], upstream_far), mixed)
    ff_far_halves = gather_x(ff_far)
    ff_own = ff_near_halves[0] if pairs_x else after(ff_near_halves[0], mixed)
    ff_blocks = [
        [ff_own, ff_mate if pairs_x else swap(ff_own, "gy", 1)],
        [ff_other, swap(ff_other, "gy", 1)],
    ]
    for blocks, far in zip(ff_blocks, ff_far_halves):
        blocks += [far, swap(far, "gy", 1)]
    near, got, far = tokens_near(cotangent, upstream_far)
    upstream = jnp.concatenate([near, got[:block], far, got[block:]], axis=0)
    middle, normed_two = branch(flip, inputs, mlp_gain, mixed, weights)

    made = mlp_chunk(normed_two, upstream, middle, None, ff_blocks[0])
    later = mlp_chunk(normed_two, upstream, made[0], made[1], ff_blocks[1])
    result, normed_two_grad = later[0], later[1]

    first_half = add(made[2], swap(made[3], "gy", 1))
    second_half = add(later[2], swap(later[3], "gy", 1))
    split = 432
    low = reduce_x([first_half[:, :split], second_half[:, :split]])
    high_parts = [part[0, split:] for part in (first_half, second_half)]
    high_far = [swap(part[1, split:], "gy", 2) for part in (first_half, second_half)]

    mid_grad, mixed_grad, gain_two, out_keep, out_send = branch_back(
        flip, normed_two_grad, middle, upstream, mlp_gain, mixed, weights
    )
    result_near, result_far = to_features(result)
    out_paired = add(out_keep, swap(out_send, "gy", 1))
    mixed_grad = after(mixed_grad, first_half, second_half, out_paired)
    out_far = swap(out_paired[1], "gx", 1) if pairs_x else out_paired[1]

    dq, sent_grad, own_grad = attention_backward(
        starts, cosine, sine, queries, prior_kv, own_kv, mixed, lse, mixed_grad
    )
    prior_grad = lax.ppermute(sent_grad, "gy", behind)
    own_grad = after(own_grad, low, high_far)
    out_far, result_far = after((out_far, result_far), dq)
    out_both = (
        add(out_paired[0], out_far) if pairs_x else reduce_x([out_paired[0], out_far])
    )
    sum_out = sum_z(add(out_both[0], swap(out_both[1], "gy", 2)))
    low = add(low[0], swap(low[1], "gy", 2))
    high = reduce_x([add(mine, theirs) for mine, theirs in zip(high_parts, high_far)])
    ff_sum = jnp.concatenate([sum_z(low), sum_z(high)], axis=0)
    grads, qkv_keep, qkv_send = qkv_grad(
        flip, normed_one, dq, own_grad, prior_grad, cosine, sine
    )
    qkv_mate = swap(qkv_send, "gy", 1)
    grads = after(grads, qkv_mate)
    paired = add(qkv_keep, qkv_mate)
    both = reduce_x([paired[0], paired[1]], -2)
    sum_qkv = sum_z(add(both[0], swap(both[1], "gy", 2)))
    in_grad, gain_one = input_grad(flip, grads, inputs, attn_gain, mid_grad, weights)
    grad_near, grad_far = to_features(in_grad)
    gains = sum_all(jnp.stack([reorder(gain_one[:, 0]), reorder(gain_two[:, 0])]))
    return (
        assemble(result_near, result_far),
        assemble(grad_near, grad_far),
        sum_qkv.T,
        sum_out.T,
        ff_sum[:block],
        ff_sum[block : 2 * block],
        ff_sum[2 * block :].T,
        gains[0],
        gains[1],
    )


def solution(mesh):
    placed = (
        P("gy", ("dp", "gx")),
        P(("dp", "gx", "gy")),
        P("gy", ("dp", "gx")),
        P(),
        P(),
        P("gy", "gx"),
        P("gx", "gy"),
        P("gy", "gx"),
        P("gy", "gx"),
        P("gx", "gy"),
    )
    return jax.shard_map(
        on_device,
        mesh=mesh,
        in_specs=placed,
        out_specs=(
            P("gy", ("dp", "gx")),
            P("gy", ("dp", "gx")),
            P("gy", "gx"),
            P("gx", "gy"),
            P("gy", "gx"),
            P("gy", "gx"),
            P("gx", "gy"),
            P(),
            P(),
        ),
        check_vma=False,
    )
```

```python
import functools

import jax
import jax.numpy as jnp
from jax import lax
from jax.experimental import pallas as pl
from jax.experimental.pallas import tpu as pltpu
from jax.sharding import PartitionSpec as P

HEADS = 15
KV_HEADS = 5
GROUP = HEADS // KV_HEADS
HEAD = 64
HALF = HEAD // 2
PRIOR = 512
TILE = 256

EPS = 1e-05
THETA = 100000.0
NEG = -1e30

TINY = pl.CostEstimate(flops=1000, bytes_accessed=1000, transcendentals=0)

BF = jnp.bfloat16
F32 = jnp.float32


def swap(value, axis, by):
    peers = lax.axis_size(axis)
    return lax.ppermute(value, axis, [(i, i ^ by) for i in range(peers)])


def dot(left, right, left_dim, right_dim):
    return lax.dot_general(
        left, right, (((left_dim,), (right_dim,)), ((), ())), preferred_element_type=F32
    )


def add_kernel(left_ref, right_ref, out_ref):
    out_ref[...] = (left_ref[...].astype(F32) + right_ref[...].astype(F32)).astype(BF)


def add(left, right):
    width = left.shape[-1]
    rows = left.size // width
    if left.shape[-2] % 16:
        return (left.astype(F32) + right.astype(F32)).astype(BF)
    step = max(
        size for size in range(16, 513, 16) if rows % size == 0
    )
    spec = pl.BlockSpec((step, width), lambda i: (i, 0))
    return pl.pallas_call(
        add_kernel,
        grid=(rows // step,),
        in_specs=[spec, spec],
        out_specs=spec,
        out_shape=jax.ShapeDtypeStruct((rows, width), BF),
        compiler_params=pltpu.CompilerParams(vmem_limit_bytes=24 * 2**20),
        cost_estimate=TINY,
        name="add",
    )(left.reshape(rows, width), right.reshape(rows, width)).reshape(left.shape)


def add_pair_kernel(left_ref, right_ref, first_ref, second_ref):
    for k, out_ref in enumerate((first_ref, second_ref)):
        out_ref[...] = (left_ref[k].astype(F32) + right_ref[k].astype(F32)).astype(BF)


def add_pair(left, right):
    shape = left.shape[1:]
    width = shape[-1]
    rows = left.size // (2 * width)
    step = max(size for size in range(16, 257, 16) if rows % size == 0)
    spec = pl.BlockSpec((2, step, width), lambda i: (0, i, 0))
    out = pl.BlockSpec((step, width), lambda i: (i, 0))
    first, second = pl.pallas_call(
        add_pair_kernel,
        grid=(rows // step,),
        in_specs=[spec, spec],
        out_specs=[out, out],
        out_shape=[jax.ShapeDtypeStruct((rows, width), BF)] * 2,
        compiler_params=pltpu.CompilerParams(vmem_limit_bytes=24 * 2**20),
        cost_estimate=TINY,
        name="add_pair",
    )(left.reshape(2, rows, width), right.reshape(2, rows, width))
    return first.reshape(shape), second.reshape(shape)


def frequencies():
    return jnp.power(THETA, -jnp.arange(HALF, dtype=F32) / HALF)


def after(value, *earlier):
    return lax.optimization_barrier((value, earlier))[0]


def ordered(mine, theirs, bit, axis):
    return jnp.where(
        bit == 0,
        jnp.concatenate([mine, theirs], axis=axis),
        jnp.concatenate([theirs, mine], axis=axis),
    )


def tokens_far(shard):
    me = lax.axis_index("gy")
    pair = shard.shape[1] // 2
    other = lax.dynamic_slice_in_dim(shard, (1 - me // 2) * pair, pair, 1)
    return swap(other, "gy", 2)


def tokens_near(shard, far):
    me = lax.axis_index("gy")
    rows = far.shape[1] // 2
    own, mate = (me % 2) * rows, (1 - me % 2) * rows
    base = (me // 2) * 2 * rows
    sent = jnp.concatenate(
        [
            lax.dynamic_slice_in_dim(shard, base + mate, rows, 1),
            lax.dynamic_slice_in_dim(far, mate, rows, 1),
        ],
        axis=0,
    )
    got = swap(sent, "gy", 1)
    return (
        lax.dynamic_slice_in_dim(shard, base + own, rows, 1),
        got,
        lax.dynamic_slice_in_dim(far, own, rows, 1),
    )


def to_features(full):
    me = lax.axis_index("gy")
    block = full.shape[0] // 4
    sent = jnp.concatenate([full[block : 2 * block], full[3 * block :]], axis=0)
    got = swap(sent, "gy", 1)
    near = ordered(full[:block], got[:block], me % 2, 1)
    far = ordered(full[2 * block : 3 * block], got[block:], me % 2, 1)
    return near, far


def assemble(near, far):
    return ordered(near, far, lax.axis_index("gy") // 2, 1)


def reorder(vector):
    me = lax.axis_index("gy")
    block = vector.shape[0] // 4
    return jnp.concatenate(
        [lax.dynamic_slice_in_dim(vector, (me ^ by) * block, block, 0) for by in range(4)]
    )


def gather_x(block):
    if lax.axis_size("gx") == 2:
        return [block, swap(block, "gx", 1)]
    whole = lax.all_gather(block, "gx", axis=1, tiled=True)
    half = whole.shape[1] // 2
    return [whole[:, :half], whole[:, half:]]


def split_x(whole):
    half = whole.shape[-1] // 2
    if lax.axis_size("gx") == 2:
        me = lax.axis_index("gx")
        return [
            lax.dynamic_slice_in_dim(whole, me * half, half, whole.ndim - 1),
            lax.dynamic_slice_in_dim(whole, (1 - me) * half, half, whole.ndim - 1),
        ]
    return [whole[..., :half], whole[..., half:]]


def reduce_x(chunks, dim=-1):
    if lax.axis_size("gx") == 2:
        return add(chunks[0], swap(chunks[1], "gx", 1))
    dim = chunks[0].ndim + dim
    return lax.psum_scatter(
        jnp.concatenate(chunks, axis=dim), "gx", scatter_dimension=dim, tiled=True
    )


def sum_z(value):
    peers = lax.axis_size("dp")
    if peers != 4:
        return lax.psum(value.astype(F32), "dp")
    me = lax.axis_index("dp")
    inner = add(value, lax.ppermute(value, "dp", [(0, 1), (3, 2)]))
    total = add(inner, lax.ppermute(inner, "dp", [(1, 2), (2, 1)]))
    outer = lax.ppermute(total, "dp", [(1, 0), (2, 3)])
    return jnp.where((me == 0) | (me == 3), outer, total).astype(F32)


def bit_z(by):
    return (lax.axis_index("dp") // by) % 2


def kept_z(value, by):
    half = value.shape[0] // 2
    return lax.dynamic_slice_in_dim(value, bit_z(by) * half, half, 0)


def halve_z(value, by):
    half = value.shape[0] // 2
    return swap(lax.dynamic_slice_in_dim(value, (1 - bit_z(by)) * half, half, 0), "dp", by)


def sum_all(value):
    for axis in ("gy", "gx", "dp"):
        by = 1
        while by < lax.axis_size(axis):
            value = value + swap(value, axis, by)
            by *= 2
    return value


RANGES = ((0, 768), (0, 1024), (512, 1280), (512, 1536))


def fill_bias(starts_ref, bias_ref):
    offset = 0
    for tile, (low, high) in enumerate(RANGES):
        size = high - low
        place = lax.broadcasted_iota(jnp.int32, (size, TILE), 0) + (low - PRIOR)
        query = lax.broadcasted_iota(jnp.int32, (size, TILE), 1) + tile * TILE
        start = starts_ref[:, tile * TILE : (tile + 1) * TILE]
        allowed = (place >= start) & (place <= query)
        bias_ref[offset : offset + size, :] = jnp.where(allowed, 0.0, NEG)
        offset += size


BIAS_ROWS = sum(high - low for low, high in RANGES)


def turned(prior, own, out_ref):
    out_ref[:PRIOR, :] = prior.astype(F32).T.astype(BF)
    out_ref[PRIOR:, :] = own.astype(F32).T.astype(BF)


def forward_kernel(
    starts_ref, q_ref, prior_ref, own_ref, mixed_ref, lse_ref, keys, values, bias
):
    @pl.when(pl.program_id(0) == 0)
    def _():
        fill_bias(starts_ref, bias)

    turned(prior_ref[0, :HEAD, :], own_ref[0, :HEAD, :], keys)
    values[:, :PRIOR] = prior_ref[0, HEAD:, :]
    values[:, PRIOR:] = own_ref[0, HEAD:, :]
    offset = 0
    for tile, (low, high) in enumerate(RANGES):
        size = high - low
        lanes = slice(tile * TILE, (tile + 1) * TILE)
        for head in range(GROUP):
            rows = slice(head * HEAD, (head + 1) * HEAD)
            scores = dot(keys[low:high, :], q_ref[rows, lanes], 1, 0)
            scores = scores + bias[offset : offset + size, :]
            top = jnp.max(scores, axis=0, keepdims=True)
            weights = jnp.exp(scores - top)
            total = jnp.sum(weights, axis=0, keepdims=True)
            out = dot(values[:, low:high], weights.astype(BF), 1, 0)
            mixed_ref[rows, lanes] = (out / total).astype(BF)
            lse_ref[0, head : head + 1, lanes] = top + jnp.log(total)
        offset += size


def attention_forward(starts, queries, prior_kv, own_kv):
    count = queries.shape[1]
    wide = GROUP * HEAD
    prior = pl.BlockSpec((1, 2 * HEAD, PRIOR), lambda g: (g, 0, 0))
    own = pl.BlockSpec((1, 2 * HEAD, count), lambda g: (g, 0, 0))
    return pl.pallas_call(
        forward_kernel,
        grid=(KV_HEADS,),
        in_specs=[
            pl.BlockSpec((1, count), lambda g: (0, 0)),
            pl.BlockSpec((wide, count), lambda g: (g, 0)),
            prior,
            own,
        ],
        out_specs=[
            pl.BlockSpec((wide, count), lambda g: (g, 0)),
            pl.BlockSpec((1, 8, count), lambda g: (g, 0, 0)),
        ],
        out_shape=[
            jax.ShapeDtypeStruct((HEADS * HEAD, count), BF),
            jax.ShapeDtypeStruct((KV_HEADS, 8, count), F32),
        ],
        scratch_shapes=[
            pltpu.VMEM((PRIOR + count, HEAD), BF),
            pltpu.VMEM((HEAD, PRIOR + count), BF),
            pltpu.VMEM((BIAS_ROWS, TILE), F32),
        ],
        compiler_params=pltpu.CompilerParams(vmem_limit_bytes=40 * 2**20),
        cost_estimate=TINY,
        name="attend_forward",
    )(starts, queries, prior_kv, own_kv)


def backward_kernel(
    starts_ref,
    cos_ref,
    sin_ref,
    q_ref,
    prior_ref,
    own_ref,
    mixed_ref,
    lse_ref,
    grad_ref,
    dq_ref,
    dprior_ref,
    down_ref,
    keys,
    turned_keys,
    turned_values,
    dk,
    dv,
    bias,
):
    @pl.when(pl.program_id(0) == 0)
    def _():
        fill_bias(starts_ref, bias)

    turned(prior_ref[0, :HEAD, :], own_ref[0, :HEAD, :], turned_keys)
    turned(prior_ref[0, HEAD:, :], own_ref[0, HEAD:, :], turned_values)
    keys[:, :PRIOR] = prior_ref[0, :HEAD, :]
    keys[:, PRIOR:] = own_ref[0, :HEAD, :]
    dk[...] = jnp.zeros_like(dk)
    dv[...] = jnp.zeros_like(dv)
    offset = 0
    for tile, (low, high) in enumerate(RANGES):
        size = high - low
        lanes = slice(tile * TILE, (tile + 1) * TILE)
        for head in range(GROUP):
            rows = slice(head * HEAD, (head + 1) * HEAD)
            query = q_ref[rows, lanes]
            grad = grad_ref[rows, lanes]
            inner = jnp.sum(
                grad.astype(F32) * mixed_ref[rows, lanes].astype(F32), axis=0, keepdims=True
            )
            lse = lse_ref[0, head : head + 1, lanes]
            scores = dot(turned_keys[low:high, :], query, 1, 0)
            weights = jnp.exp(scores + bias[offset : offset + size, :] - lse)
            prob_grad = dot(turned_values[low:high, :], grad, 1, 0)
            score_grad = (weights * (prob_grad - inner)).astype(BF)
            weights = weights.astype(BF)
            dv[low:high, :] += dot(weights, grad, 1, 1)
            dk[low:high, :] += dot(score_grad, query, 1, 1)
            dq = dot(keys[:, low:high], score_grad, 1, 0) * HEAD ** (-0.5)
            cosine, sine = cos_ref[:, lanes], sin_ref[:, lanes]
            front, back = dq[:HALF], dq[HALF:]
            base = head * HEAD
            dq_ref[base : base + HALF, lanes] = (front * cosine + back * sine).astype(BF)
            dq_ref[base + HALF : base + HEAD, lanes] = (back * cosine - front * sine).astype(BF)
        offset += size
    dprior_ref[0, :HEAD, :] = dk[:PRIOR, :].T.astype(BF)
    dprior_ref[0, HEAD:, :] = dv[:PRIOR, :].T.astype(BF)
    down_ref[0, :HEAD, :] = dk[PRIOR:, :].T
    down_ref[0, HEAD:, :] = dv[PRIOR:, :].T


def attention_backward(
    starts, cosine, sine, queries, prior_kv, own_kv, mixed, lse, grads
):
    count = queries.shape[1]
    wide = GROUP * HEAD
    prior = pl.BlockSpec((1, 2 * HEAD, PRIOR), lambda g: (g, 0, 0))
    own = pl.BlockSpec((1, 2 * HEAD, count), lambda g: (g, 0, 0))
    heads = pl.BlockSpec((wide, count), lambda g: (g, 0))
    table = pl.BlockSpec((HALF, count), lambda g: (0, 0))
    return pl.pallas_call(
        backward_kernel,
        grid=(KV_HEADS,),
        in_specs=[
            pl.BlockSpec((1, count), lambda g: (0, 0)),
            table,
            table,
            heads,
            prior,
            own,
            heads,
            pl.BlockSpec((1, 8, count), lambda g: (g, 0, 0)),
            heads,
        ],
        out_specs=[heads, prior, own],
        out_shape=[
            jax.ShapeDtypeStruct((HEADS * HEAD, count), BF),
            jax.ShapeDtypeStruct((KV_HEADS, 2 * HEAD, PRIOR), BF),
            jax.ShapeDtypeStruct((KV_HEADS, 2 * HEAD, count), F32),
        ],
        scratch_shapes=[
            pltpu.VMEM((HEAD, PRIOR + count), BF),
            pltpu.VMEM((PRIOR + count, HEAD), BF),
            pltpu.VMEM((PRIOR + count, HEAD), BF),
            pltpu.VMEM((PRIOR + count, HEAD), F32),
            pltpu.VMEM((PRIOR + count, HEAD), F32),
            pltpu.VMEM((BIAS_ROWS, TILE), F32),
        ],
        compiler_params=pltpu.CompilerParams(vmem_limit_bytes=44 * 2**20),
        cost_estimate=TINY,
        name="attend_backward",
    )(starts, cosine, sine, queries, prior_kv, own_kv, mixed, lse, grads)


def mlp_kernel(first, *refs):
    normed_ref, up_ref, base_ref = refs[:3]
    refs = refs[3:]
    if not first:
        grad_in_ref, refs = refs[0], refs[1:]
    blocks = refs[0:4]
    out_ref, grad_out_ref, keep_ref, send_ref, total_ref, grad_total_ref = refs[4:]
    step = pl.program_id(0)
    last = pl.num_programs(0) - 1

    @pl.when(step == 0)
    def _():
        total_ref[...] = base_ref[...]
        if first:
            grad_total_ref[...] = jnp.zeros_like(grad_total_ref)
        else:
            grad_total_ref[...] = grad_in_ref[...]

    normed = normed_ref[...]
    upstream = up_ref[...]
    block = normed.shape[0] // 4
    w_gate = jnp.concatenate([ref[:block] for ref in blocks], axis=0)
    w_up = jnp.concatenate([ref[block : 2 * block] for ref in blocks], axis=0)
    w_down = jnp.concatenate([ref[2 * block :] for ref in blocks], axis=0)
    gate = dot(w_gate, normed, 0, 0)
    up = dot(w_up, normed, 0, 0)
    hidden_grad = dot(w_down, upstream, 0, 0)
    sigmoid = 1.0 / (1.0 + jnp.exp(-gate))
    silu = gate * sigmoid
    hidden = (silu * up).astype(BF)
    gate_grad = (hidden_grad * up * (sigmoid * (1.0 + gate * (1.0 - sigmoid)))).astype(BF)
    up_grad = (hidden_grad * silu).astype(BF)
    total_ref[...] += dot(w_down, hidden, 1, 0)
    grad_total_ref[...] += dot(w_gate, gate_grad, 1, 0) + dot(w_up, up_grad, 1, 0)
    for place, (left, right) in enumerate(
        ((normed, gate_grad), (normed, up_grad), (upstream, hidden))
    ):
        made = dot(left, right, 1, 1).astype(BF)
        rows = slice(place * block, (place + 1) * block)
        keep_ref[0, rows, :] = made[:block]
        send_ref[0, rows, :] = made[block : 2 * block]
        keep_ref[1, rows, :] = made[2 * block : 3 * block]
        send_ref[1, rows, :] = made[3 * block :]

    @pl.when(step == last)
    def _():
        out_ref[...] = total_ref[...].astype(out_ref.dtype)
        grad_out_ref[...] = grad_total_ref[...]


def mlp_chunk(normed, upstream, base, grad_in, blocks):
    first = grad_in is None
    width, count = normed.shape
    rows, size = blocks[0].shape
    tile = TILE
    whole = pl.BlockSpec((width, count), lambda i: (0, 0), pipeline_mode=pl.Buffered(1))
    across = pl.BlockSpec((rows, tile), lambda i: (0, i))
    made = pl.BlockSpec((2, rows, tile), lambda i: (0, 0, i))
    operands = [normed, upstream, base] + ([] if first else [grad_in])
    return pl.pallas_call(
        functools.partial(mlp_kernel, first),
        grid=(size // tile,),
        in_specs=[whole] * len(operands) + [across] * 4,
        out_specs=[whole, whole, made, made],
        out_shape=[
            jax.ShapeDtypeStruct((width, count), F32 if first else BF),
            jax.ShapeDtypeStruct((width, count), F32),
            jax.ShapeDtypeStruct((2, rows, size), BF),
            jax.ShapeDtypeStruct((2, rows, size), BF),
        ],
        scratch_shapes=[pltpu.VMEM((width, count), F32), pltpu.VMEM((width, count), F32)],
        compiler_params=pltpu.CompilerParams(vmem_limit_bytes=56 * 2**20),
        cost_estimate=TINY,
        name="feed_forward",
    )(*operands, *blocks)


VMEM = pl.BlockSpec(memory_space=pltpu.VMEM)
SMEM = pl.BlockSpec(memory_space=pltpu.SMEM)
Q_WIDTH = HEADS * HEAD
KV_WIDTH = KV_HEADS * HEAD
QKV_WIDTH = Q_WIDTH + 2 * KV_WIDTH
QKV_PART = QKV_WIDTH // 2
OUT_PART = Q_WIDTH // 2


def place_of(flip_ref, half, size):
    return pl.ds(pl.multiple_of((flip_ref[0] ^ half) * size, 16), size)


def stacked(refs, columns):
    return jnp.concatenate([ref[:, columns] for ref in refs], axis=0)


QKV_COLUMNS = slice(0, QKV_PART)
OUT_COLUMNS = slice(QKV_PART, QKV_PART + OUT_PART)


def norm_scale_of(values):
    return lax.rsqrt(jnp.mean(values * values, axis=0, keepdims=True) + EPS)


def norm_back(values, scale, gain, gradient):
    weighted = gradient * gain
    inner = jnp.mean(weighted * values, axis=0, keepdims=True)
    values_grad = scale * weighted - values * (scale * scale * scale) * inner
    return (values_grad, jnp.sum(gradient * values * scale, axis=1, keepdims=True))


def project_kernel(flip_ref, near_ref, got_ref, far_ref, gain_ref, cos_ref, sin_ref, *refs):
    weights = refs[:8]
    x_ref, normed_ref, q_ref, own_ref, prior_ref, made = refs[8:]
    block = near_ref.shape[0]
    x_ref[:block, :] = near_ref[...]
    x_ref[block : 2 * block, :] = got_ref[:block, :]
    x_ref[2 * block : 3 * block, :] = far_ref[...]
    x_ref[3 * block :, :] = got_ref[block:, :]
    x = x_ref[...].astype(F32)
    normed = (x * norm_scale_of(x) * gain_ref[...]).astype(BF)
    normed_ref[...] = normed
    for half in range(2):
        weight = stacked(weights[4 * half : 4 * half + 4], QKV_COLUMNS)
        made[place_of(flip_ref, half, QKV_PART), :] = dot(weight, normed, 0, 0).astype(BF)
    cosine, sine = cos_ref[...], sin_ref[...]
    count = cosine.shape[1]

    def rotated(base, scale):
        front = made[base : base + HALF, :].astype(F32)
        back = made[base + HALF : base + HEAD, :].astype(F32)
        return (
            ((front * cosine - back * sine) * scale).astype(BF),
            ((back * cosine + front * sine) * scale).astype(BF),
        )

    for head in range(HEADS):
        base = head * HEAD
        front, back = rotated(base, HEAD ** (-0.5))
        q_ref[base : base + HALF, :] = front
        q_ref[base + HALF : base + HEAD, :] = back
    for head in range(KV_HEADS):
        front, back = rotated(Q_WIDTH + head * HEAD, 1.0)
        base = Q_WIDTH + KV_WIDTH + head * HEAD
        value = made[base : base + HEAD, :]
        own_ref[head, :HALF, :] = front
        own_ref[head, HALF:HEAD, :] = back
        own_ref[head, HEAD:, :] = value
        prior_ref[head, :HALF, :] = front[:, count - PRIOR :]
        prior_ref[head, HALF:HEAD, :] = back[:, count - PRIOR :]
        prior_ref[head, HEAD:, :] = value[:, count - PRIOR :]


def call_whole(kernel, name, ins, outs, scratch=()):
    return pl.pallas_call(
        kernel,
        in_specs=[SMEM] + [VMEM] * (len(ins) - 1),
        out_specs=[VMEM] * len(outs),
        out_shape=[jax.ShapeDtypeStruct(shape, kind) for shape, kind in outs],
        scratch_shapes=list(scratch),
        compiler_params=pltpu.CompilerParams(vmem_limit_bytes=56 * 2**20),
        cost_estimate=TINY,
        name=name,
    )(*ins)


def project(flip, pieces, gain, cosine, sine, weights):
    block, count = pieces[0].shape
    width = 4 * block
    return call_whole(
        project_kernel,
        "project",
        (flip, *pieces, gain, cosine, sine, *weights),
        (
            ((width, count), BF),
            ((width, count), BF),
            ((Q_WIDTH, count), BF),
            ((KV_HEADS, 2 * HEAD, count), BF),
            ((KV_HEADS, 2 * HEAD, PRIOR), BF),
        ),
        (pltpu.VMEM((QKV_WIDTH, count), BF),),
    )


def branch_kernel(flip_ref, x_ref, gain_ref, mixed_ref, *refs):
    weights = refs[:8]
    middle_ref, normed_ref = refs[8:]
    middle = x_ref[...].astype(F32)
    for half in range(2):
        weight = stacked(weights[4 * half : 4 * half + 4], OUT_COLUMNS)
        middle = middle + dot(weight, mixed_ref[place_of(flip_ref, half, OUT_PART), :], 1, 0)
    middle_ref[...] = middle
    normed_ref[...] = (middle * norm_scale_of(middle) * gain_ref[...]).astype(BF)


def branch(flip, inputs, gain, mixed, weights):
    shape = inputs.shape
    return call_whole(
        branch_kernel,
        "branch",
        (flip, inputs, gain, mixed, *weights),
        ((shape, F32), (shape, BF)),
    )


def store_blocks(keep_ref, send_ref, half, made):
    block = made.shape[0] // 4
    keep_ref[half, 0] = made[:block]
    send_ref[half, 0] = made[block : 2 * block]
    keep_ref[half, 1] = made[2 * block : 3 * block]
    send_ref[half, 1] = made[3 * block :]


def branch_back_kernel(flip_ref, grad_ref, middle_ref, up_ref, gain_ref, mixed_ref, *refs):
    weights = refs[:8]
    mid_grad_ref, mixed_grad_ref, gain_grad_ref, keep_ref, send_ref = refs[8:]
    middle = middle_ref[...]
    mid_grad, gain_grad = norm_back(
        middle, norm_scale_of(middle), gain_ref[...], grad_ref[...]
    )
    gain_grad_ref[...] = gain_grad
    mid_grad = mid_grad + up_ref[...].astype(F32)
    mid_grad_ref[...] = mid_grad
    branch_grad = mid_grad.astype(BF)
    for half in range(2):
        place = place_of(flip_ref, half, OUT_PART)
        weight = stacked(weights[4 * half : 4 * half + 4], OUT_COLUMNS)
        mixed_grad_ref[place, :] = dot(weight, branch_grad, 0, 0).astype(BF)
        made = dot(branch_grad, mixed_ref[place, :], 1, 1).astype(BF)
        store_blocks(keep_ref, send_ref, half, made)


def branch_back(flip, grad, middle, upstream, gain, mixed, weights):
    width, count = middle.shape
    parts = (2, 2, width // 4, OUT_PART)
    return call_whole(
        branch_back_kernel,
        "branch_back",
        (flip, grad, middle, upstream, gain, mixed, *weights),
        (
            ((width, count), F32),
            ((Q_WIDTH, count), BF),
            ((width, 1), F32),
            (parts, BF),
            (parts, BF),
        ),
    )


def qkv_grad_kernel(
    flip_ref, normed_ref, dq_ref, own_ref, prior_ref, cos_ref, sin_ref, made_ref, keep_ref, send_ref
):
    made_ref[:Q_WIDTH, :] = dq_ref[...]
    count = own_ref.shape[2]
    cosine, sine = cos_ref[...], sin_ref[...]
    for head in range(KV_HEADS):
        sent = prior_ref[head].astype(F32)
        both = jnp.concatenate(
            [own_ref[head, :, : count - PRIOR], own_ref[head, :, count - PRIOR :] + sent], axis=1
        )
        front, back = both[:HALF], both[HALF:HEAD]
        base = Q_WIDTH + head * HEAD
        made_ref[base : base + HALF, :] = (front * cosine + back * sine).astype(BF)
        made_ref[base + HALF : base + HEAD, :] = (back * cosine - front * sine).astype(BF)
        base += KV_WIDTH
        made_ref[base : base + HEAD, :] = both[HEAD:].astype(BF)
    normed = normed_ref[...]
    block = normed.shape[0] // 4
    for half in range(2):
        grads = made_ref[place_of(flip_ref, half, QKV_PART), :]
        for number in range(4):
            rows = normed[number * block : (number + 1) * block]
            target = send_ref if number % 2 else keep_ref
            target[half, number // 2] = dot(grads, rows, 1, 1).astype(BF)


def qkv_grad(flip, normed, dq, own, prior, cosine, sine):
    width, count = normed.shape
    parts = (2, 2, QKV_PART, width // 4)
    return call_whole(
        qkv_grad_kernel,
        "qkv_grad",
        (flip, normed, dq, own, prior, cosine, sine),
        (((QKV_WIDTH, count), BF), (parts, BF), (parts, BF)),
    )


def input_grad_kernel(flip_ref, grads_ref, x_ref, gain_ref, mid_grad_ref, *refs):
    weights = refs[:8]
    out_ref, gain_grad_ref = refs[8:]
    total = jnp.zeros(x_ref.shape, F32)
    for half in range(2):
        weight = stacked(weights[4 * half : 4 * half + 4], QKV_COLUMNS)
        total = total + dot(weight, grads_ref[place_of(flip_ref, half, QKV_PART), :], 1, 0)
    x = x_ref[...].astype(F32)
    grad, gain_grad = norm_back(x, norm_scale_of(x), gain_ref[...], total)
    gain_grad_ref[...] = gain_grad
    out_ref[...] = (grad + mid_grad_ref[...]).astype(BF)


def input_grad(flip, grads, inputs, gain, mid_grad, weights):
    width, count = inputs.shape
    return call_whole(
        input_grad_kernel,
        "input_grad",
        (flip, grads, inputs, gain, mid_grad, *weights),
        (((width, count), BF), ((width, 1), F32)),
    )


def attention_halves(shard, cut):
    if lax.axis_size("gx") == 2:
        return [shard, swap(shard, "gx", 1)]
    peers = lax.axis_size("gx")
    block, width = shard.shape
    whole = lax.all_gather(shard, "gx", axis=1, tiled=True)
    whole = whole.reshape(block, 2, peers // 2, width)
    return [
        jnp.concatenate(
            [
                whole[:, c, :, :cut].reshape(block, peers // 2 * cut),
                whole[:, c, :, cut:].reshape(block, peers // 2 * (width - cut)),
            ],
            axis=1,
        )
        for c in range(2)
    ]


def on_device(
    tokens, doc_start, cotangent, attn_gain, mlp_gain, w_qkv, w_out, w_gate, w_up, w_down
):
    count = doc_start.shape[0]
    block = w_qkv.shape[0]
    pairs_x = lax.axis_size("gx") == 2
    flip = lax.axis_index("gx") if pairs_x else jnp.int32(0)
    flip = jnp.reshape(flip, (1,)).astype(jnp.int32)

    shard = jnp.concatenate([w_qkv, w_out.T], axis=1)
    shard_far = swap(shard, "gy", 2)
    mate = swap(shard, "gy", 1)
    inputs_far = tokens_far(after(tokens, mate))
    near_halves = attention_halves(shard, w_qkv.shape[1])
    far_halves = attention_halves(shard_far, w_qkv.shape[1])
    weights = []
    for half, (near, far) in enumerate(zip(near_halves, far_halves)):
        near_mate = mate if pairs_x and half == 0 else swap(near, "gy", 1)
        weights += [near, near_mate, far, swap(far, "gy", 1)]
    pieces = tokens_near(tokens, inputs_far)

    ff_shard = jnp.concatenate([w_gate, w_up, w_down.T], axis=0)
    ff_shard = after(ff_shard, inputs_far, *near_halves, *far_halves)
    ff_far = swap(ff_shard, "gy", 2)
    ff_near_halves = gather_x(ff_shard)
    ff_mate = swap(ff_shard, "gy", 1)

    attn_gain = reorder(attn_gain)[:, None]
    mlp_gain = reorder(mlp_gain)[:, None]

    first_row = lax.axis_index(("dp", "gx", "gy")) * count
    places = first_row + jnp.arange(count, dtype=jnp.int32)
    angle = frequencies()[:, None] * (places - doc_start).astype(F32)[None, :]
    cosine, sine = jnp.cos(angle), jnp.sin(angle)
    starts = (doc_start - first_row)[None, :]

    inputs, normed_one, queries, own_kv, sent_kv = project(
        flip, pieces, attn_gain, cosine, sine, weights
    )
    cotangent = after(cotangent, sent_kv)
    upstream_far = tokens_far(cotangent)
    peers = lax.axis_size("gy")
    ahead = [(i, i + 1) for i in range(0, peers, 2)]
    behind = [(i + 1, i) for i in range(0, peers, 2)]
    prior_kv = lax.ppermute(sent_kv, "gy", ahead)
    mixed, lse = attention_forward(starts, queries, prior_kv, own_kv)

    ff_far, ff_other, upstream_far = after((ff_far, ff_near_halves[1], upstream_far), mixed)
    ff_far_halves = gather_x(ff_far)
    ff_own = ff_near_halves[0] if pairs_x else after(ff_near_halves[0], mixed)
    ff_blocks = [
        [ff_own, ff_mate if pairs_x else swap(ff_own, "gy", 1)],
        [ff_other, swap(ff_other, "gy", 1)],
    ]
    ff_blocks[0] += [ff_far_halves[0], swap(ff_far_halves[0], "gy", 1)]
    near, got, far = tokens_near(cotangent, upstream_far)
    upstream = jnp.concatenate([near, got[:block], far, got[block:]], axis=0)
    middle, normed_two = branch(flip, inputs, mlp_gain, mixed, weights)

    made = mlp_chunk(normed_two, upstream, middle, None, ff_blocks[0])
    ff_far_other = after(ff_far_halves[1], made[0])
    ff_blocks[1] += [ff_far_other, swap(ff_far_other, "gy", 1)]
    later = mlp_chunk(normed_two, upstream, made[0], made[1], ff_blocks[1])
    result, normed_two_grad = later[0], later[1]

    mid_grad, mixed_grad, gain_two, out_keep, out_send = branch_back(
        flip, normed_two_grad, middle, upstream, mlp_gain, mixed, weights
    )
    result_near, result_sent = to_features(result)

    first_half = add(made[2], swap(made[3], "gy", 1))
    second_half = add(later[2], swap(later[3], "gy", 1))
    out_paired = add(out_keep, swap(out_send, "gy", 1))

    def attend_back(mixed_grad, *earlier):
        dq, sent_grad, own_grad = attention_backward(
            starts, cosine, sine, queries, prior_kv, own_kv, mixed, lse, mixed_grad
        )
        prior_grad = lax.ppermute(sent_grad, "gy", behind)
        own_grad = after(own_grad, *earlier)
        grads, keep, send = qkv_grad(
            flip, normed_one, dq, own_grad, prior_grad, cosine, sine
        )
        return grads, keep, swap(send, "gy", 1)

    if not pairs_x:
        grads, qkv_keep, qkv_mate = attend_back(mixed_grad)
        ff_both = reduce_x([first_half, second_half])
        ff_sum = sum_z(add(ff_both[0], swap(ff_both[1], "gy", 2)))
        both = reduce_x([out_paired[0], out_paired[1]])
        sum_out = sum_z(add(both[0], swap(both[1], "gy", 2)))
        paired = add(qkv_keep, qkv_mate)
        both = reduce_x([paired[0], paired[1]], -2)
        sum_qkv = sum_z(add(both[0], swap(both[1], "gy", 2)))
        in_grad, gain_one = input_grad(flip, grads, inputs, attn_gain, mid_grad, weights)
        grad_near, grad_sent = to_features(in_grad)
        grad_far = swap(grad_sent, "gy", 2)
        result_far = swap(result_sent, "gy", 2)
        gains = sum_all(jnp.stack([reorder(gain_one[:, 0]), reorder(gain_two[:, 0])]))
    else:
        split = 400
        wide = first_half.shape[2]
        out_rows = out_paired[0].size // (2 * wide)
        filler = jnp.zeros((2, -(split + out_rows) % 64, wide), BF)
        low_own, low_other = (
            jnp.concatenate([half[:, :split], out_half.reshape(2, -1, wide), filler], axis=1)
            for half, out_half in ((first_half, out_paired[0]), (second_half, out_paired[1]))
        )
        high_near, high_far = (
            jnp.stack([first_half[k, split:], second_half[k, split:]]) for k in (0, 1)
        )
        mixed_grad = after(
            mixed_grad, low_own, low_other, high_near, high_far, result_near, result_sent
        )
        low_got = swap(low_other, "gx", 1)
        high_got = swap(high_far, "gy", 2)
        grads, qkv_keep, qkv_mate = attend_back(mixed_grad, high_got)

        high_near, high_sent = add_pair(high_near, after(high_got, grads))
        qkv_near, qkv_sent = add_pair(qkv_keep, after(qkv_mate, high_near))
        qkv_got = swap(qkv_sent, "gx", 1)
        high_got = swap(after(high_sent, qkv_near), "gx", 1)
        in_grad, gain_one = input_grad(
            flip, after(grads, qkv_near), inputs, attn_gain, mid_grad, weights
        )
        low_near, low_sent = add_pair(low_own, after(low_got, in_grad))
        low_got = swap(low_sent, "gy", 2)
        qkv_near, qkv_sent = add_pair(qkv_near, after(qkv_got, low_near))
        qkv_got = swap(qkv_sent, "gy", 2)
        grad_near, grad_sent = to_features(after(in_grad, low_near))
        grad_far = swap(grad_sent, "gy", 2)
        result_far = swap(after(result_sent, grads), "gy", 2)
        gains = jnp.stack([reorder(gain_one[:, 0]), reorder(gain_two[:, 0])])
        gains_got = swap(gains, "gy", 1)
        high = add(high_near, after(high_got, grad_near))
        high_got = halve_z(high, 1)
        gains = gains + after(gains_got, high)
        gains_got = swap(gains, "gx", 1)
        low = add(low_near, after(low_got, gains))
        result_far = after(result_far, low)
        low_got = halve_z(low, 1)
        qkv_sum = add(qkv_near, after(qkv_got, low))
        qkv_got = lax.ppermute(qkv_sum, "dp", [(0, 1), (3, 2)])
        gains = gains + after(gains_got, qkv_sum)
        gains_got = swap(gains, "gy", 2)
        high = add(kept_z(high, 1), after(high_got, gains))
        high_got = halve_z(high, 2)
        qkv_sum = add(qkv_sum, after(qkv_got, high))
        qkv_got = lax.ppermute(qkv_sum, "dp", [(1, 2), (2, 1)])
        low = add(kept_z(low, 1), after(low_got, qkv_sum))
        low_got = halve_z(low, 2)
        gains = gains + after(gains_got, low)
        gains_got = swap(gains, "dp", 1)
        high = add(kept_z(high, 2), after(high_got, gains))
        high_got = swap(high, "dp", 2)
        qkv_sum = add(qkv_sum, after(qkv_got, high))
        qkv_got = lax.ppermute(qkv_sum, "dp", [(1, 0), (2, 3)])
        low = add(kept_z(low, 2), after(low_got, qkv_sum))
        low_got = swap(low, "dp", 2)
        gains = gains + after(gains_got, low)
        gains_got = swap(gains, "dp", 2)
        high = ordered(high, after(high_got, gains), bit_z(2), 0)
        high_got = swap(high, "dp", 1)
        low = ordered(low, after(low_got, high), bit_z(2), 0)
        low_got = swap(low, "dp", 1)
        at = lax.axis_index("dp")
        sum_qkv = jnp.where(
            (at == 0) | (at == 3), after(qkv_got, low), qkv_sum
        ).astype(F32)
        gains = gains + after(gains_got, sum_qkv)
        high = ordered(high, after(high_got, gains), bit_z(1), 0).astype(F32)
        low = ordered(low, after(low_got, high), bit_z(1), 0).astype(F32)
        ff_sum = jnp.concatenate([low[:split], high], axis=0)
        sum_out = low[split : split + out_rows].reshape(block, -1)
    return (
        assemble(result_near, result_far),
        assemble(grad_near, grad_far),
        sum_qkv.T,
        sum_out.T,
        ff_sum[:block],
        ff_sum[block : 2 * block],
        ff_sum[2 * block :].T,
        gains[0],
        gains[1],
    )


def solution(mesh):
    placed = (
        P("gy", ("dp", "gx")),
        P(("dp", "gx", "gy")),
        P("gy", ("dp", "gx")),
        P(),
        P(),
        P("gy", "gx"),
        P("gx", "gy"),
        P("gy", "gx"),
        P("gy", "gx"),
        P("gx", "gy"),
    )
    return jax.shard_map(
        on_device,
        mesh=mesh,
        in_specs=placed,
        out_specs=(
            P("gy", ("dp", "gx")),
            P("gy", ("dp", "gx")),
            P("gy", "gx"),
            P("gx", "gy"),
            P("gy", "gx"),
            P("gy", "gx"),
            P("gx", "gy"),
            P(),
            P(),
        ),
        check_vma=False,
    )
```

```python
import functools

import jax
import jax.numpy as jnp
from jax import lax
from jax.experimental import pallas as pl
from jax.experimental.pallas import tpu as pltpu
from jax.sharding import PartitionSpec as P

HEADS = 15
KV_HEADS = 5
GROUP = HEADS // KV_HEADS
HEAD = 64
HALF = HEAD // 2
PRIOR = 512
TILE = 256

EPS = 1e-05
THETA = 100000.0
NEG = -1e30

TINY = pl.CostEstimate(flops=1000, bytes_accessed=1000, transcendentals=0)

BF = jnp.bfloat16
F32 = jnp.float32


def swap(value, axis, by):
    peers = lax.axis_size(axis)
    return lax.ppermute(value, axis, [(i, i ^ by) for i in range(peers)])


def dot(left, right, left_dim, right_dim):
    return lax.dot_general(
        left, right, (((left_dim,), (right_dim,)), ((), ())), preferred_element_type=F32
    )


def add_kernel(left_ref, right_ref, out_ref):
    out_ref[...] = (left_ref[...].astype(F32) + right_ref[...].astype(F32)).astype(BF)


def add(left, right):
    width = left.shape[-1]
    rows = left.size // width
    if left.shape[-2] % 16:
        return (left.astype(F32) + right.astype(F32)).astype(BF)
    step = max(
        size for size in range(16, 513, 16) if rows % size == 0
    )
    spec = pl.BlockSpec((step, width), lambda i: (i, 0))
    return pl.pallas_call(
        add_kernel,
        grid=(rows // step,),
        in_specs=[spec, spec],
        out_specs=spec,
        out_shape=jax.ShapeDtypeStruct((rows, width), BF),
        compiler_params=pltpu.CompilerParams(vmem_limit_bytes=24 * 2**20),
        cost_estimate=TINY,
        name="add",
    )(left.reshape(rows, width), right.reshape(rows, width)).reshape(left.shape)


def add_pair_kernel(left_ref, right_ref, first_ref, second_ref):
    for k, out_ref in enumerate((first_ref, second_ref)):
        out_ref[...] = (left_ref[k].astype(F32) + right_ref[k].astype(F32)).astype(BF)


def add_pair(left, right):
    shape = left.shape[1:]
    width = shape[-1]
    rows = left.size // (2 * width)
    step = max(size for size in range(16, 257, 16) if rows % size == 0)
    spec = pl.BlockSpec((2, step, width), lambda i: (0, i, 0))
    out = pl.BlockSpec((step, width), lambda i: (i, 0))
    first, second = pl.pallas_call(
        add_pair_kernel,
        grid=(rows // step,),
        in_specs=[spec, spec],
        out_specs=[out, out],
        out_shape=[jax.ShapeDtypeStruct((rows, width), BF)] * 2,
        compiler_params=pltpu.CompilerParams(vmem_limit_bytes=24 * 2**20),
        cost_estimate=TINY,
        name="add_pair",
    )(left.reshape(2, rows, width), right.reshape(2, rows, width))
    return first.reshape(shape), second.reshape(shape)


def frequencies():
    return jnp.power(THETA, -jnp.arange(HALF, dtype=F32) / HALF)


def after(value, *earlier):
    return lax.optimization_barrier((value, earlier))[0]


def ordered(mine, theirs, bit, axis):
    return jnp.where(
        bit == 0,
        jnp.concatenate([mine, theirs], axis=axis),
        jnp.concatenate([theirs, mine], axis=axis),
    )


def tokens_far(shard):
    me = lax.axis_index("gy")
    pair = shard.shape[1] // 2
    other = lax.dynamic_slice_in_dim(shard, (1 - me // 2) * pair, pair, 1)
    return swap(other, "gy", 2)


def tokens_near(shard, far):
    me = lax.axis_index("gy")
    rows = far.shape[1] // 2
    own, mate = (me % 2) * rows, (1 - me % 2) * rows
    base = (me // 2) * 2 * rows
    sent = jnp.concatenate(
        [
            lax.dynamic_slice_in_dim(shard, base + mate, rows, 1),
            lax.dynamic_slice_in_dim(far, mate, rows, 1),
        ],
        axis=0,
    )
    got = swap(sent, "gy", 1)
    return (
        lax.dynamic_slice_in_dim(shard, base + own, rows, 1),
        got,
        lax.dynamic_slice_in_dim(far, own, rows, 1),
    )


def to_features(kept, got):
    me = lax.axis_index("gy")
    block = kept.shape[0] // 2
    near = ordered(kept[:block], got[:block], me % 2, 1)
    far = ordered(kept[block:], got[block:], me % 2, 1)
    return near, far


def assemble(near, far):
    return ordered(near, far, lax.axis_index("gy") // 2, 1)


def reorder(vector):
    me = lax.axis_index("gy")
    block = vector.shape[0] // 4
    return jnp.concatenate(
        [lax.dynamic_slice_in_dim(vector, (me ^ by) * block, block, 0) for by in range(4)]
    )


def gather_x(block):
    if lax.axis_size("gx") == 2:
        return [block, swap(block, "gx", 1)]
    whole = lax.all_gather(block, "gx", axis=1, tiled=True)
    half = whole.shape[1] // 2
    return [whole[:, :half], whole[:, half:]]


def split_x(whole):
    half = whole.shape[-1] // 2
    if lax.axis_size("gx") == 2:
        me = lax.axis_index("gx")
        return [
            lax.dynamic_slice_in_dim(whole, me * half, half, whole.ndim - 1),
            lax.dynamic_slice_in_dim(whole, (1 - me) * half, half, whole.ndim - 1),
        ]
    return [whole[..., :half], whole[..., half:]]


def reduce_x(chunks, dim=-1):
    if lax.axis_size("gx") == 2:
        return add(chunks[0], swap(chunks[1], "gx", 1))
    dim = chunks[0].ndim + dim
    return lax.psum_scatter(
        jnp.concatenate(chunks, axis=dim), "gx", scatter_dimension=dim, tiled=True
    )


def sum_z(value):
    peers = lax.axis_size("dp")
    if peers != 4:
        return lax.psum(value.astype(F32), "dp")
    me = lax.axis_index("dp")
    inner = add(value, lax.ppermute(value, "dp", [(0, 1), (3, 2)]))
    total = add(inner, lax.ppermute(inner, "dp", [(1, 2), (2, 1)]))
    outer = lax.ppermute(total, "dp", [(1, 0), (2, 3)])
    return jnp.where((me == 0) | (me == 3), outer, total).astype(F32)


def unfold(rows, block):
    return jnp.concatenate(
        [rows[..., part * 256 : part * 256 + block] for part in range(5)], axis=-2
    )


LOW = 352
HIGH_PAD = 16


def pair_sums_kernel(keep_ref, got_ref, out_keep_ref, out_got_ref, low_ref, near_ref, far_ref):
    def total(k, rows):
        return (keep_ref[k, rows, :].astype(F32) + got_ref[k, rows, :].astype(F32)).astype(BF)

    low_ref[:, LOW:, :] = (
        out_keep_ref[0].astype(F32) + out_got_ref[...].astype(F32)
    ).astype(BF)
    for k, high_ref in enumerate((near_ref, far_ref)):
        low_ref[k, :LOW, :] = total(k, slice(0, LOW))
        size = high_ref.shape[0] - HIGH_PAD
        high_ref[:size, :] = total(k, slice(LOW, LOW + size))
        high_ref[size:, :] = jnp.zeros((HIGH_PAD, high_ref.shape[1]), BF)


def pair_sums(keep, got, half, out_keep, out_got):
    rows, width = keep.shape[1:]
    out_rows = out_keep.shape[2]
    out_block = pl.BlockSpec((1, 2, out_rows, 256), lambda i: (half, 0, 0, i))
    high = rows - LOW + HIGH_PAD
    tile = 256

    def block(*dims):
        return pl.BlockSpec((*dims, tile), lambda i: (*(0 for _ in dims), i))

    return pl.pallas_call(
        pair_sums_kernel,
        grid=(width // tile,),
        in_specs=[block(2, rows), block(2, rows), out_block, block(2, out_rows)],
        out_specs=[block(2, LOW + out_rows), block(high), block(high)],
        out_shape=[
            jax.ShapeDtypeStruct((2, LOW + out_rows, width), BF),
            jax.ShapeDtypeStruct((high, width), BF),
            jax.ShapeDtypeStruct((high, width), BF),
        ],
        compiler_params=pltpu.CompilerParams(vmem_limit_bytes=32 * 2**20),
        cost_estimate=TINY,
        name="pair_sums",
    )(keep, got, out_keep, out_got)


def bit_z(by):
    return (lax.axis_index("dp") // by) % 2


def kept_z(value, by):
    half = value.shape[0] // 2
    return lax.dynamic_slice_in_dim(value, bit_z(by) * half, half, 0)


def halve_z(value, by):
    half = value.shape[0] // 2
    return swap(lax.dynamic_slice_in_dim(value, (1 - bit_z(by)) * half, half, 0), "dp", by)


def sum_all(value):
    for axis in ("gy", "gx", "dp"):
        by = 1
        while by < lax.axis_size(axis):
            value = value + swap(value, axis, by)
            by *= 2
    return value


RANGES = ((0, 768), (0, 1024), (512, 1280), (512, 1536))


def fill_bias(starts_ref, bias_ref):
    offset = 0
    for tile, (low, high) in enumerate(RANGES):
        size = high - low
        place = lax.broadcasted_iota(jnp.int32, (size, TILE), 0) + (low - PRIOR)
        query = lax.broadcasted_iota(jnp.int32, (size, TILE), 1) + tile * TILE
        start = starts_ref[:, tile * TILE : (tile + 1) * TILE]
        allowed = (place >= start) & (place <= query)
        bias_ref[offset : offset + size, :] = jnp.where(allowed, 0.0, NEG)
        offset += size


BIAS_ROWS = sum(high - low for low, high in RANGES)


def turned(prior, own, out_ref):
    out_ref[:PRIOR, :] = prior.astype(F32).T.astype(BF)
    out_ref[PRIOR:, :] = own.astype(F32).T.astype(BF)


def forward_kernel(
    starts_ref, q_ref, prior_ref, own_ref, mixed_ref, lse_ref, keys, values, bias
):
    @pl.when(pl.program_id(0) == 0)
    def _():
        fill_bias(starts_ref, bias)

    turned(prior_ref[0, :HEAD, :], own_ref[0, :HEAD, :], keys)
    values[:, :PRIOR] = prior_ref[0, HEAD:, :]
    values[:, PRIOR:] = own_ref[0, HEAD:, :]
    offset = 0
    for tile, (low, high) in enumerate(RANGES):
        size = high - low
        lanes = slice(tile * TILE, (tile + 1) * TILE)
        for head in range(GROUP):
            rows = slice(head * HEAD, (head + 1) * HEAD)
            scores = dot(keys[low:high, :], q_ref[rows, lanes], 1, 0)
            scores = scores + bias[offset : offset + size, :]
            top = jnp.max(scores, axis=0, keepdims=True)
            weights = jnp.exp(scores - top)
            total = jnp.sum(weights, axis=0, keepdims=True)
            out = dot(values[:, low:high], weights.astype(BF), 1, 0)
            mixed_ref[rows, lanes] = (out / total).astype(BF)
            lse_ref[0, head : head + 1, lanes] = top + jnp.log(total)
        offset += size


def attention_forward(starts, queries, prior_kv, own_kv):
    count = queries.shape[1]
    wide = GROUP * HEAD
    prior = pl.BlockSpec((1, 2 * HEAD, PRIOR), lambda g: (g, 0, 0))
    own = pl.BlockSpec((1, 2 * HEAD, count), lambda g: (g, 0, 0))
    return pl.pallas_call(
        forward_kernel,
        grid=(KV_HEADS,),
        in_specs=[
            pl.BlockSpec((1, count), lambda g: (0, 0)),
            pl.BlockSpec((wide, count), lambda g: (g, 0)),
            prior,
            own,
        ],
        out_specs=[
            pl.BlockSpec((wide, count), lambda g: (g, 0)),
            pl.BlockSpec((1, 8, count), lambda g: (g, 0, 0)),
        ],
        out_shape=[
            jax.ShapeDtypeStruct((HEADS * HEAD, count), BF),
            jax.ShapeDtypeStruct((KV_HEADS, 8, count), F32),
        ],
        scratch_shapes=[
            pltpu.VMEM((PRIOR + count, HEAD), BF),
            pltpu.VMEM((HEAD, PRIOR + count), BF),
            pltpu.VMEM((BIAS_ROWS, TILE), F32),
        ],
        compiler_params=pltpu.CompilerParams(vmem_limit_bytes=40 * 2**20),
        cost_estimate=TINY,
        name="attend_forward",
    )(starts, queries, prior_kv, own_kv)


def backward_kernel(
    starts_ref,
    cos_ref,
    sin_ref,
    q_ref,
    prior_ref,
    own_ref,
    mixed_ref,
    lse_ref,
    grad_ref,
    dq_ref,
    dprior_ref,
    down_ref,
    keys,
    turned_keys,
    turned_values,
    dk,
    dv,
    bias,
):
    @pl.when(pl.program_id(0) == 0)
    def _():
        fill_bias(starts_ref, bias)

    turned(prior_ref[0, :HEAD, :], own_ref[0, :HEAD, :], turned_keys)
    turned(prior_ref[0, HEAD:, :], own_ref[0, HEAD:, :], turned_values)
    keys[:, :PRIOR] = prior_ref[0, :HEAD, :]
    keys[:, PRIOR:] = own_ref[0, :HEAD, :]
    dk[...] = jnp.zeros_like(dk)
    dv[...] = jnp.zeros_like(dv)
    offset = 0
    for tile, (low, high) in enumerate(RANGES):
        size = high - low
        lanes = slice(tile * TILE, (tile + 1) * TILE)
        for head in range(GROUP):
            rows = slice(head * HEAD, (head + 1) * HEAD)
            query = q_ref[rows, lanes]
            grad = grad_ref[rows, lanes]
            inner = jnp.sum(
                grad.astype(F32) * mixed_ref[rows, lanes].astype(F32), axis=0, keepdims=True
            )
            lse = lse_ref[0, head : head + 1, lanes]
            scores = dot(turned_keys[low:high, :], query, 1, 0)
            weights = jnp.exp(scores + bias[offset : offset + size, :] - lse)
            prob_grad = dot(turned_values[low:high, :], grad, 1, 0)
            score_grad = (weights * (prob_grad - inner)).astype(BF)
            weights = weights.astype(BF)
            dv[low:high, :] += dot(weights, grad, 1, 1)
            dk[low:high, :] += dot(score_grad, query, 1, 1)
            dq = dot(keys[:, low:high], score_grad, 1, 0) * HEAD ** (-0.5)
            cosine, sine = cos_ref[:, lanes], sin_ref[:, lanes]
            front, back = dq[:HALF], dq[HALF:]
            base = head * HEAD
            dq_ref[base : base + HALF, lanes] = (front * cosine + back * sine).astype(BF)
            dq_ref[base + HALF : base + HEAD, lanes] = (back * cosine - front * sine).astype(BF)
        offset += size
    dprior_ref[0, :HEAD, :] = dk[:PRIOR, :].T.astype(BF)
    dprior_ref[0, HEAD:, :] = dv[:PRIOR, :].T.astype(BF)
    down_ref[0, :HEAD, :] = dk[PRIOR:, :].T
    down_ref[0, HEAD:, :] = dv[PRIOR:, :].T


def attention_backward(
    starts, cosine, sine, queries, prior_kv, own_kv, mixed, lse, grads
):
    count = queries.shape[1]
    wide = GROUP * HEAD
    prior = pl.BlockSpec((1, 2 * HEAD, PRIOR), lambda g: (g, 0, 0))
    own = pl.BlockSpec((1, 2 * HEAD, count), lambda g: (g, 0, 0))
    heads = pl.BlockSpec((wide, count), lambda g: (g, 0))
    table = pl.BlockSpec((HALF, count), lambda g: (0, 0))
    return pl.pallas_call(
        backward_kernel,
        grid=(KV_HEADS,),
        in_specs=[
            pl.BlockSpec((1, count), lambda g: (0, 0)),
            table,
            table,
            heads,
            prior,
            own,
            heads,
            pl.BlockSpec((1, 8, count), lambda g: (g, 0, 0)),
            heads,
        ],
        out_specs=[heads, prior, own],
        out_shape=[
            jax.ShapeDtypeStruct((HEADS * HEAD, count), BF),
            jax.ShapeDtypeStruct((KV_HEADS, 2 * HEAD, PRIOR), BF),
            jax.ShapeDtypeStruct((KV_HEADS, 2 * HEAD, count), F32),
        ],
        scratch_shapes=[
            pltpu.VMEM((HEAD, PRIOR + count), BF),
            pltpu.VMEM((PRIOR + count, HEAD), BF),
            pltpu.VMEM((PRIOR + count, HEAD), BF),
            pltpu.VMEM((PRIOR + count, HEAD), F32),
            pltpu.VMEM((PRIOR + count, HEAD), F32),
            pltpu.VMEM((BIAS_ROWS, TILE), F32),
        ],
        compiler_params=pltpu.CompilerParams(vmem_limit_bytes=44 * 2**20),
        cost_estimate=TINY,
        name="attend_backward",
    )(starts, cosine, sine, queries, prior_kv, own_kv, mixed, lse, grads)


def mlp_kernel(first, *refs):
    normed_ref, up_ref, base_ref = refs[:3]
    refs = refs[3:]
    if not first:
        grad_in_ref, refs = refs[0], refs[1:]
    blocks, refs = refs[:4], refs[4:]
    out_refs, refs = (refs[:1], refs[1:]) if first else (refs[:2], refs[2:])
    grad_out_ref, keep_ref, send_ref, total_ref, grad_total_ref = refs
    step = pl.program_id(0)
    last = pl.num_programs(0) - 1

    @pl.when(step == 0)
    def _():
        total_ref[...] = base_ref[...]
        if first:
            grad_total_ref[...] = jnp.zeros_like(grad_total_ref)
        else:
            grad_total_ref[...] = grad_in_ref[...]

    normed = normed_ref[...]
    upstream = up_ref[...]
    block = normed.shape[0] // 4
    w_gate = jnp.concatenate([ref[:block] for ref in blocks], axis=0)
    w_up = jnp.concatenate([ref[block : 2 * block] for ref in blocks], axis=0)
    w_down = jnp.concatenate([ref[2 * block :] for ref in blocks], axis=0)
    gate = dot(w_gate, normed, 0, 0)
    up = dot(w_up, normed, 0, 0)
    hidden_grad = dot(w_down, upstream, 0, 0)
    sigmoid = 1.0 / (1.0 + jnp.exp(-gate))
    silu = gate * sigmoid
    hidden = (silu * up).astype(BF)
    gate_grad = (hidden_grad * up * (sigmoid * (1.0 + gate * (1.0 - sigmoid)))).astype(BF)
    up_grad = (hidden_grad * silu).astype(BF)
    total_ref[...] += dot(w_down, hidden, 1, 0)
    grad_total_ref[...] += dot(w_gate, gate_grad, 1, 0) + dot(w_up, up_grad, 1, 0)
    for place, (left, right) in enumerate(
        ((normed, gate_grad), (normed, up_grad), (upstream, hidden))
    ):
        made = dot(left, right, 1, 1).astype(BF)
        rows = slice(place * block, (place + 1) * block)
        keep_ref[0, rows, :] = made[:block]
        send_ref[0, rows, :] = made[block : 2 * block]
        keep_ref[1, rows, :] = made[2 * block : 3 * block]
        send_ref[1, rows, :] = made[3 * block :]

    @pl.when(step == last)
    def _():
        if first:
            out_refs[0][...] = total_ref[...]
        else:
            for number in range(4):
                rows = slice((number // 2) * block, (number // 2 + 1) * block)
                source = slice(number * block, (number + 1) * block)
                out_refs[number % 2][rows, :] = total_ref[source, :].astype(BF)
        grad_out_ref[...] = grad_total_ref[...]


def mlp_chunk(normed, upstream, base, grad_in, blocks):
    first = grad_in is None
    width, count = normed.shape
    rows, size = blocks[0].shape
    tile = TILE
    whole = pl.BlockSpec((width, count), lambda i: (0, 0), pipeline_mode=pl.Buffered(1))
    half = pl.BlockSpec((width // 2, count), lambda i: (0, 0), pipeline_mode=pl.Buffered(1))
    across = pl.BlockSpec((rows, tile), lambda i: (0, i))
    made = pl.BlockSpec((2, rows, tile), lambda i: (0, 0, i))
    operands = [normed, upstream, base] + ([] if first else [grad_in])
    return pl.pallas_call(
        functools.partial(mlp_kernel, first),
        grid=(size // tile,),
        in_specs=[whole] * len(operands) + [across] * 4,
        out_specs=([whole] if first else [half, half]) + [whole, made, made],
        out_shape=(
            [jax.ShapeDtypeStruct((width, count), F32)]
            if first
            else [jax.ShapeDtypeStruct((width // 2, count), BF)] * 2
        )
        + [
            jax.ShapeDtypeStruct((width, count), F32),
            jax.ShapeDtypeStruct((2, rows, size), BF),
            jax.ShapeDtypeStruct((2, rows, size), BF),
        ],
        scratch_shapes=[pltpu.VMEM((width, count), F32), pltpu.VMEM((width, count), F32)],
        compiler_params=pltpu.CompilerParams(vmem_limit_bytes=56 * 2**20),
        cost_estimate=TINY,
        name="feed_forward",
    )(*operands, *blocks)


VMEM = pl.BlockSpec(memory_space=pltpu.VMEM)
SMEM = pl.BlockSpec(memory_space=pltpu.SMEM)
Q_WIDTH = HEADS * HEAD
KV_WIDTH = KV_HEADS * HEAD
QKV_WIDTH = Q_WIDTH + 2 * KV_WIDTH
QKV_PART = QKV_WIDTH // 2
OUT_PART = Q_WIDTH // 2
OUT_ROWS = OUT_PART // 5


def place_of(flip_ref, half, size):
    return pl.ds(pl.multiple_of((flip_ref[0] ^ half) * size, 16), size)


def stacked(refs, columns):
    return jnp.concatenate([ref[:, columns] for ref in refs], axis=0)


QKV_COLUMNS = slice(0, QKV_PART)
OUT_COLUMNS = slice(QKV_PART, QKV_PART + OUT_PART)


def norm_scale_of(values):
    return lax.rsqrt(jnp.mean(values * values, axis=0, keepdims=True) + EPS)


def norm_back(values, scale, gain, gradient):
    weighted = gradient * gain
    inner = jnp.mean(weighted * values, axis=0, keepdims=True)
    values_grad = scale * weighted - values * (scale * scale * scale) * inner
    return (values_grad, jnp.sum(gradient * values * scale, axis=1, keepdims=True))


def project_kernel(flip_ref, near_ref, got_ref, far_ref, gain_ref, cos_ref, sin_ref, *refs):
    weights = refs[:8]
    x_ref, normed_ref, q_ref, own_ref, prior_ref, made = refs[8:]
    block = near_ref.shape[0]
    x_ref[:block, :] = near_ref[...]
    x_ref[block : 2 * block, :] = got_ref[:block, :]
    x_ref[2 * block : 3 * block, :] = far_ref[...]
    x_ref[3 * block :, :] = got_ref[block:, :]
    x = x_ref[...].astype(F32)
    normed = (x * norm_scale_of(x) * gain_ref[...]).astype(BF)
    normed_ref[...] = normed
    for half in range(2):
        weight = stacked(weights[4 * half : 4 * half + 4], QKV_COLUMNS)
        made[place_of(flip_ref, half, QKV_PART), :] = dot(weight, normed, 0, 0).astype(BF)
    cosine, sine = cos_ref[...], sin_ref[...]
    count = cosine.shape[1]

    def rotated(base, scale):
        front = made[base : base + HALF, :].astype(F32)
        back = made[base + HALF : base + HEAD, :].astype(F32)
        return (
            ((front * cosine - back * sine) * scale).astype(BF),
            ((back * cosine + front * sine) * scale).astype(BF),
        )

    for head in range(HEADS):
        base = head * HEAD
        front, back = rotated(base, HEAD ** (-0.5))
        q_ref[base : base + HALF, :] = front
        q_ref[base + HALF : base + HEAD, :] = back
    for head in range(KV_HEADS):
        front, back = rotated(Q_WIDTH + head * HEAD, 1.0)
        base = Q_WIDTH + KV_WIDTH + head * HEAD
        value = made[base : base + HEAD, :]
        own_ref[head, :HALF, :] = front
        own_ref[head, HALF:HEAD, :] = back
        own_ref[head, HEAD:, :] = value
        prior_ref[head, :HALF, :] = front[:, count - PRIOR :]
        prior_ref[head, HALF:HEAD, :] = back[:, count - PRIOR :]
        prior_ref[head, HEAD:, :] = value[:, count - PRIOR :]


def call_whole(kernel, name, ins, outs, scratch=()):
    return pl.pallas_call(
        kernel,
        in_specs=[SMEM] + [VMEM] * (len(ins) - 1),
        out_specs=[VMEM] * len(outs),
        out_shape=[jax.ShapeDtypeStruct(shape, kind) for shape, kind in outs],
        scratch_shapes=list(scratch),
        compiler_params=pltpu.CompilerParams(vmem_limit_bytes=56 * 2**20),
        cost_estimate=TINY,
        name=name,
    )(*ins)


def project(flip, pieces, gain, cosine, sine, weights):
    block, count = pieces[0].shape
    width = 4 * block
    return call_whole(
        project_kernel,
        "project",
        (flip, *pieces, gain, cosine, sine, *weights),
        (
            ((width, count), BF),
            ((width, count), BF),
            ((Q_WIDTH, count), BF),
            ((KV_HEADS, 2 * HEAD, count), BF),
            ((KV_HEADS, 2 * HEAD, PRIOR), BF),
        ),
        (pltpu.VMEM((QKV_WIDTH, count), BF),),
    )


def branch_kernel(flip_ref, x_ref, gain_ref, mixed_ref, *refs):
    weights = refs[:8]
    middle_ref, normed_ref = refs[8:]
    middle = x_ref[...].astype(F32)
    for half in range(2):
        weight = stacked(weights[4 * half : 4 * half + 4], OUT_COLUMNS)
        middle = middle + dot(weight, mixed_ref[place_of(flip_ref, half, OUT_PART), :], 1, 0)
    middle_ref[...] = middle
    normed_ref[...] = (middle * norm_scale_of(middle) * gain_ref[...]).astype(BF)


def branch(flip, inputs, gain, mixed, weights):
    shape = inputs.shape
    return call_whole(
        branch_kernel,
        "branch",
        (flip, inputs, gain, mixed, *weights),
        ((shape, F32), (shape, BF)),
    )


def branch_back_kernel(flip_ref, grad_ref, middle_ref, up_ref, gain_ref, mixed_ref, *refs):
    weights = refs[:8]
    mid_grad_ref, mixed_grad_ref, gain_grad_ref, keep_ref, *send_refs = refs[8:]
    middle = middle_ref[...]
    mid_grad, gain_grad = norm_back(
        middle, norm_scale_of(middle), gain_ref[...], grad_ref[...]
    )
    gain_grad_ref[...] = gain_grad
    mid_grad = mid_grad + up_ref[...].astype(F32)
    mid_grad_ref[...] = mid_grad
    branch_grad = mid_grad.astype(BF)
    block = branch_grad.shape[0] // 4
    keep_ref[...] = jnp.zeros_like(keep_ref)
    for send_ref in send_refs:
        send_ref[...] = jnp.zeros_like(send_ref)
    for half in range(2):
        place = place_of(flip_ref, half, OUT_PART)
        weight = stacked(weights[4 * half : 4 * half + 4], OUT_COLUMNS)
        mixed_grad_ref[place, :] = dot(weight, branch_grad, 0, 0).astype(BF)
        heads = mixed_ref[place, :]
        for number in range(4):
            rows = branch_grad[number * block : (number + 1) * block]
            made = dot(heads, rows, 1, 1).astype(BF)
            target = send_refs[half] if number % 2 else keep_ref.at[half]
            for part in range(5):
                target[number // 2, :, part * 256 : part * 256 + block] = made[
                    part * OUT_ROWS : (part + 1) * OUT_ROWS
                ]


def branch_back(flip, grad, middle, upstream, gain, mixed, weights):
    width, count = middle.shape
    parts = (2, 2, OUT_ROWS, 5 * 256)
    return call_whole(
        branch_back_kernel,
        "branch_back",
        (flip, grad, middle, upstream, gain, mixed, *weights),
        (
            ((width, count), F32),
            ((Q_WIDTH, count), BF),
            ((width, 1), F32),
            (parts, BF),
            (parts[1:], BF),
            (parts[1:], BF),
        ),
    )


def qkv_grad_kernel(
    flip_ref, normed_ref, dq_ref, own_ref, prior_ref, cos_ref, sin_ref, made_ref, keep_ref, send_ref
):
    made_ref[:Q_WIDTH, :] = dq_ref[...]
    count = own_ref.shape[2]
    cosine, sine = cos_ref[...], sin_ref[...]
    for head in range(KV_HEADS):
        sent = prior_ref[head].astype(F32)
        both = jnp.concatenate(
            [own_ref[head, :, : count - PRIOR], own_ref[head, :, count - PRIOR :] + sent], axis=1
        )
        front, back = both[:HALF], both[HALF:HEAD]
        base = Q_WIDTH + head * HEAD
        made_ref[base : base + HALF, :] = (front * cosine + back * sine).astype(BF)
        made_ref[base + HALF : base + HEAD, :] = (back * cosine - front * sine).astype(BF)
        base += KV_WIDTH
        made_ref[base : base + HEAD, :] = both[HEAD:].astype(BF)
    normed = normed_ref[...]
    block = normed.shape[0] // 4
    for half in range(2):
        grads = made_ref[place_of(flip_ref, half, QKV_PART), :]
        for number in range(4):
            rows = normed[number * block : (number + 1) * block]
            target = send_ref if number % 2 else keep_ref
            target[half, number // 2] = dot(grads, rows, 1, 1).astype(BF)


def qkv_grad(flip, normed, dq, own, prior, cosine, sine):
    width, count = normed.shape
    parts = (2, 2, QKV_PART, width // 4)
    return call_whole(
        qkv_grad_kernel,
        "qkv_grad",
        (flip, normed, dq, own, prior, cosine, sine),
        (((QKV_WIDTH, count), BF), (parts, BF), (parts, BF)),
    )


def input_grad_kernel(flip_ref, grads_ref, x_ref, gain_ref, mid_grad_ref, *refs):
    weights = refs[:8]
    keep_ref, send_ref, gain_grad_ref = refs[8:]
    total = jnp.zeros(x_ref.shape, F32)
    for half in range(2):
        weight = stacked(weights[4 * half : 4 * half + 4], QKV_COLUMNS)
        total = total + dot(weight, grads_ref[place_of(flip_ref, half, QKV_PART), :], 1, 0)
    x = x_ref[...].astype(F32)
    grad, gain_grad = norm_back(x, norm_scale_of(x), gain_ref[...], total)
    gain_grad_ref[...] = gain_grad
    grad = (grad + mid_grad_ref[...]).astype(BF)
    block = grad.shape[0] // 4
    for number in range(4):
        target = send_ref if number % 2 else keep_ref
        rows = slice((number // 2) * block, (number // 2 + 1) * block)
        target[rows, :] = grad[number * block : (number + 1) * block]


def input_grad(flip, grads, inputs, gain, mid_grad, weights):
    width, count = inputs.shape
    return call_whole(
        input_grad_kernel,
        "input_grad",
        (flip, grads, inputs, gain, mid_grad, *weights),
        (((width // 2, count), BF), ((width // 2, count), BF), ((width, 1), F32)),
    )


def attention_halves(shard, cut):
    if lax.axis_size("gx") == 2:
        return [shard, swap(shard, "gx", 1)]
    peers = lax.axis_size("gx")
    block, width = shard.shape
    whole = lax.all_gather(shard, "gx", axis=1, tiled=True)
    whole = whole.reshape(block, 2, peers // 2, width)
    return [
        jnp.concatenate(
            [
                whole[:, c, :, :cut].reshape(block, peers // 2 * cut),
                whole[:, c, :, cut:].reshape(block, peers // 2 * (width - cut)),
            ],
            axis=1,
        )
        for c in range(2)
    ]


def on_device(
    tokens, doc_start, cotangent, attn_gain, mlp_gain, w_qkv, w_out, w_gate, w_up, w_down
):
    count = doc_start.shape[0]
    block = w_qkv.shape[0]
    pairs_x = lax.axis_size("gx") == 2
    flip = lax.axis_index("gx") if pairs_x else jnp.int32(0)
    flip = jnp.reshape(flip, (1,)).astype(jnp.int32)

    shard = jnp.concatenate([w_qkv, w_out.T], axis=1)
    shard_far = swap(shard, "gy", 2)
    mate = swap(shard, "gy", 1)
    near_halves = attention_halves(shard, w_qkv.shape[1])
    inputs_far = tokens_far(after(tokens, shard_far, *near_halves))
    far_halves = attention_halves(shard_far, w_qkv.shape[1])
    weights = []
    for half, (near, far) in enumerate(zip(near_halves, far_halves)):
        near_mate = mate if pairs_x and half == 0 else swap(near, "gy", 1)
        weights += [near, near_mate, far, swap(far, "gy", 1)]
    pieces = tokens_near(tokens, inputs_far)

    ff_shard = jnp.concatenate([w_gate, w_up, w_down.T], axis=0)
    ff_shard = after(ff_shard, inputs_far, *near_halves, *far_halves)
    ff_far = swap(ff_shard, "gy", 2)
    ff_near_halves = gather_x(ff_shard)
    ff_mate = swap(ff_shard, "gy", 1)

    attn_gain = reorder(attn_gain)[:, None]
    mlp_gain = reorder(mlp_gain)[:, None]

    first_row = lax.axis_index(("dp", "gx", "gy")) * count
    places = first_row + jnp.arange(count, dtype=jnp.int32)
    angle = frequencies()[:, None] * (places - doc_start).astype(F32)[None, :]
    cosine, sine = jnp.cos(angle), jnp.sin(angle)
    starts = (doc_start - first_row)[None, :]

    inputs, normed_one, queries, own_kv, sent_kv = project(
        flip, pieces, attn_gain, cosine, sine, weights
    )
    cotangent = after(cotangent, sent_kv)
    upstream_far = tokens_far(cotangent)
    peers = lax.axis_size("gy")
    ahead = [(i, i + 1) for i in range(0, peers, 2)]
    behind = [(i + 1, i) for i in range(0, peers, 2)]
    prior_kv = lax.ppermute(sent_kv, "gy", ahead)
    mixed, lse = attention_forward(starts, queries, prior_kv, own_kv)

    ff_far, ff_other, upstream_far = after((ff_far, ff_near_halves[1], upstream_far), mixed)
    ff_far_halves = gather_x(ff_far)
    ff_own = ff_near_halves[0] if pairs_x else after(ff_near_halves[0], mixed)
    ff_blocks = [
        [ff_own, ff_mate if pairs_x else swap(ff_own, "gy", 1)],
        [ff_other, swap(ff_other, "gy", 1)],
    ]
    ff_blocks[0] += [ff_far_halves[0], swap(ff_far_halves[0], "gy", 1)]
    near, got, far = tokens_near(cotangent, upstream_far)
    upstream = jnp.concatenate([near, got[:block], far, got[block:]], axis=0)
    middle, normed_two = branch(flip, inputs, mlp_gain, mixed, weights)

    made = mlp_chunk(normed_two, upstream, middle, None, ff_blocks[0])
    ff_far_other = after(ff_far_halves[1], made[0])
    ff_blocks[1] += [ff_far_other, swap(ff_far_other, "gy", 1)]
    later = mlp_chunk(normed_two, upstream, made[0], made[1], ff_blocks[1])
    result_keep, result_send, normed_two_grad, later_keep, later_send = later
    result_near, result_sent = to_features(result_keep, swap(result_send, "gy", 1))
    result_far = swap(result_sent, "gy", 2)
    first_got = swap(made[3], "gy", 1)
    later_got = swap(later_send, "gy", 1)

    mid_grad, mixed_grad, gain_two, out_keep, *out_sent = branch_back(
        flip,
        after(normed_two_grad, result_near, result_sent),
        middle,
        upstream,
        mlp_gain,
        mixed,
        weights,
    )
    out_got = [swap(part, "gy", 1) for part in out_sent]
    result_shard = assemble(result_near, result_far)

    def attend_back(mixed_grad, *earlier):
        dq, sent_grad, own_grad = attention_backward(
            starts, cosine, sine, queries, prior_kv, own_kv, mixed, lse, mixed_grad
        )
        prior_grad = lax.ppermute(sent_grad, "gy", behind)
        own_grad = after(own_grad, *earlier)
        grads, keep, send = qkv_grad(
            flip, normed_one, dq, own_grad, prior_grad, cosine, sine
        )
        return grads, keep, swap(send, "gy", 1)

    if not pairs_x:
        grads, qkv_keep, qkv_mate = attend_back(mixed_grad)
        ff_both = reduce_x([add(made[2], first_got), add(later_keep, later_got)])
        ff_sum = sum_z(add(ff_both[0], swap(ff_both[1], "gy", 2)))
        paired = unfold(add(out_keep, jnp.stack(out_got)), block)
        both = reduce_x([paired[0], paired[1]], -2)
        sum_out = sum_z(add(both[0], swap(both[1], "gy", 2)))
        paired = add(qkv_keep, qkv_mate)
        both = reduce_x([paired[0], paired[1]], -2)
        sum_qkv = sum_z(add(both[0], swap(both[1], "gy", 2)))
        grad_keep, grad_send, gain_one = input_grad(
            flip, grads, inputs, attn_gain, mid_grad, weights
        )
        grad_near, grad_sent = to_features(grad_keep, swap(grad_send, "gy", 1))
        grad_far = swap(grad_sent, "gy", 2)
        gains = sum_all(jnp.stack([reorder(gain_one[:, 0]), reorder(gain_two[:, 0])]))
    else:
        low_own, near_own, far_own = pair_sums(made[2], first_got, 0, out_keep, out_got[0])
        low_other, near_other, far_other = pair_sums(
            later_keep, later_got, 1, out_keep, out_got[1]
        )
        mixed_grad = after(
            mixed_grad, low_own, low_other, near_own, near_other, far_own, far_other, result_shard
        )
        low_got = swap(low_other, "gx", 1)
        own_got = swap(far_own, "gy", 2)
        other_got = swap(far_other, "gy", 2)
        grads, qkv_keep, qkv_mate = attend_back(mixed_grad, own_got, other_got)

        high_sent = add(near_other, after(other_got, grads))
        high_near = add(near_own, after(own_got, high_sent))
        low_near, low_sent = add_pair(low_own, after(low_got, high_near))
        low_got = swap(low_sent, "gy", 2)
        qkv_near, qkv_sent = add_pair(qkv_keep, after(qkv_mate, low_near))
        qkv_got = swap(qkv_sent, "gx", 1)
        high_got = swap(after(high_sent, qkv_near), "gx", 1)
        grad_keep, grad_send, gain_one = input_grad(
            flip, after(grads, qkv_near), inputs, attn_gain, mid_grad, weights
        )
        grad_got = swap(grad_send, "gy", 1)
        qkv_near, qkv_sent = add_pair(qkv_near, after(qkv_got, grad_keep))
        qkv_got = swap(qkv_sent, "gy", 2)
        low = add(low_near, after(low_got, qkv_near))
        low_got = halve_z(low, 1)
        grad_near, grad_sent = to_features(grad_keep, after(grad_got, low))
        grad_far = swap(grad_sent, "gy", 2)
        high = add(high_near, after(high_got, grad_near))
        high_got = halve_z(high, 1)
        gain_one, gain_two = after((gain_one, gain_two), high)
        gains = jnp.stack([reorder(gain_one[:, 0]), reorder(gain_two[:, 0])])
        gains_got = swap(gains, "gx", 1)
        qkv_sum = add(qkv_near, after(qkv_got, high))
        qkv_got = lax.ppermute(qkv_sum, "dp", [(0, 1), (3, 2)])
        gains = gains + after(gains_got, qkv_sum)
        gains_got = swap(gains, "gy", 1)
        high = add(kept_z(high, 1), after(high_got, gains))
        high_got = halve_z(high, 2)
        qkv_sum = add(qkv_sum, after(qkv_got, high))
        qkv_got = lax.ppermute(qkv_sum, "dp", [(1, 2), (2, 1)])
        low = add(kept_z(low, 1), after(low_got, qkv_sum))
        low_got = halve_z(low, 2)
        gains = gains + after(gains_got, low)
        gains_got = swap(gains, "gy", 2)
        high = add(kept_z(high, 2), after(high_got, gains))
        high_got = swap(high, "dp", 2)
        qkv_sum = add(qkv_sum, after(qkv_got, high))
        qkv_got = lax.ppermute(qkv_sum, "dp", [(1, 0), (2, 3)])
        low = add(kept_z(low, 2), after(low_got, qkv_sum))
        low_got = swap(low, "dp", 2)
        gains = gains + after(gains_got, low)
        gains_got = swap(gains, "dp", 1)
        high = ordered(high, after(high_got, low), bit_z(2), 0)
        high_got = swap(high, "dp", 1)
        low = ordered(low, after(low_got, high), bit_z(2), 0)
        low_got = swap(low, "dp", 1)
        gains = gains + after(gains_got, low)
        gains_got = swap(gains, "dp", 2)
        at = lax.axis_index("dp")
        sum_qkv = jnp.where(
            (at == 0) | (at == 3), after(qkv_got, low), qkv_sum
        ).astype(F32)
        high = ordered(high, after(high_got, sum_qkv), bit_z(1), 0).astype(F32)
        low = ordered(low, after(low_got, high), bit_z(1), 0).astype(F32)
        gains = gains + after(gains_got, low)
        ff_sum = jnp.concatenate([low[:LOW], high[: high.shape[0] - HIGH_PAD]], axis=0)
        sum_out = unfold(low[LOW:], block)
    return (
        result_shard,
        assemble(grad_near, grad_far),
        sum_qkv.T,
        sum_out,
        ff_sum[:block],
        ff_sum[block : 2 * block],
        ff_sum[2 * block :].T,
        gains[0],
        gains[1],
    )


def solution(mesh):
    placed = (
        P("gy", ("dp", "gx")),
        P(("dp", "gx", "gy")),
        P("gy", ("dp", "gx")),
        P(),
        P(),
        P("gy", "gx"),
        P("gx", "gy"),
        P("gy", "gx"),
        P("gy", "gx"),
        P("gx", "gy"),
    )
    return jax.shard_map(
        on_device,
        mesh=mesh,
        in_specs=placed,
        out_specs=(
            P("gy", ("dp", "gx")),
            P("gy", ("dp", "gx")),
            P("gy", "gx"),
            P("gx", "gy"),
            P("gy", "gx"),
            P("gy", "gx"),
            P("gx", "gy"),
            P(),
            P(),
        ),
        check_vma=False,
    )
```

```python
import functools

import jax
import jax.numpy as jnp
from jax import lax
from jax.experimental import pallas as pl
from jax.experimental.pallas import tpu as pltpu
from jax.sharding import PartitionSpec as P

HEADS = 15
KV_HEADS = 5
GROUP = HEADS // KV_HEADS
HEAD = 64
HALF = HEAD // 2
PRIOR = 512
TILE = 256

EPS = 1e-05
THETA = 100000.0
NEG = -1e30

TINY = pl.CostEstimate(flops=1000, bytes_accessed=1000, transcendentals=0)

BF = jnp.bfloat16
F32 = jnp.float32


def swap(value, axis, by):
    peers = lax.axis_size(axis)
    return lax.ppermute(value, axis, [(i, i ^ by) for i in range(peers)])


def dot(left, right, left_dim, right_dim):
    return lax.dot_general(
        left, right, (((left_dim,), (right_dim,)), ((), ())), preferred_element_type=F32
    )


def add_kernel(left_ref, right_ref, out_ref):
    out_ref[...] = (left_ref[...].astype(F32) + right_ref[...].astype(F32)).astype(BF)


def add(left, right):
    width = left.shape[-1]
    rows = left.size // width
    if left.shape[-2] % 16:
        return (left.astype(F32) + right.astype(F32)).astype(BF)
    step = max(
        size for size in range(16, 513, 16) if rows % size == 0
    )
    spec = pl.BlockSpec((step, width), lambda i: (i, 0))
    return pl.pallas_call(
        add_kernel,
        grid=(rows // step,),
        in_specs=[spec, spec],
        out_specs=spec,
        out_shape=jax.ShapeDtypeStruct((rows, width), BF),
        compiler_params=pltpu.CompilerParams(vmem_limit_bytes=24 * 2**20),
        cost_estimate=TINY,
        name="add",
    )(left.reshape(rows, width), right.reshape(rows, width)).reshape(left.shape)


def add_pair_kernel(left_ref, right_ref, first_ref, second_ref):
    for k, out_ref in enumerate((first_ref, second_ref)):
        out_ref[...] = (left_ref[k].astype(F32) + right_ref[k].astype(F32)).astype(BF)


def add_pair(left, right):
    shape = left.shape[1:]
    width = shape[-1]
    rows = left.size // (2 * width)
    step = max(size for size in range(16, 257, 16) if rows % size == 0)
    spec = pl.BlockSpec((2, step, width), lambda i: (0, i, 0))
    out = pl.BlockSpec((step, width), lambda i: (i, 0))
    first, second = pl.pallas_call(
        add_pair_kernel,
        grid=(rows // step,),
        in_specs=[spec, spec],
        out_specs=[out, out],
        out_shape=[jax.ShapeDtypeStruct((rows, width), BF)] * 2,
        compiler_params=pltpu.CompilerParams(vmem_limit_bytes=24 * 2**20),
        cost_estimate=TINY,
        name="add_pair",
    )(left.reshape(2, rows, width), right.reshape(2, rows, width))
    return first.reshape(shape), second.reshape(shape)


def frequencies():
    return jnp.power(THETA, -jnp.arange(HALF, dtype=F32) / HALF)


def after(value, *earlier):
    return lax.optimization_barrier((value, earlier))[0]


def ordered(mine, theirs, bit, axis):
    return jnp.where(
        bit == 0,
        jnp.concatenate([mine, theirs], axis=axis),
        jnp.concatenate([theirs, mine], axis=axis),
    )


def tokens_far(shard):
    me = lax.axis_index("gy")
    pair = shard.shape[1] // 2
    other = lax.dynamic_slice_in_dim(shard, (1 - me // 2) * pair, pair, 1)
    return swap(other, "gy", 2)


def tokens_near(shard, far):
    me = lax.axis_index("gy")
    rows = far.shape[1] // 2
    own, mate = (me % 2) * rows, (1 - me % 2) * rows
    base = (me // 2) * 2 * rows
    sent = jnp.concatenate(
        [
            lax.dynamic_slice_in_dim(shard, base + mate, rows, 1),
            lax.dynamic_slice_in_dim(far, mate, rows, 1),
        ],
        axis=0,
    )
    got = swap(sent, "gy", 1)
    return (
        lax.dynamic_slice_in_dim(shard, base + own, rows, 1),
        got,
        lax.dynamic_slice_in_dim(far, own, rows, 1),
    )


def to_features(kept, got):
    me = lax.axis_index("gy")
    block = kept.shape[0] // 2
    near = ordered(kept[:block], got[:block], me % 2, 1)
    far = ordered(kept[block:], got[block:], me % 2, 1)
    return near, far


def assemble(near, far):
    return ordered(near, far, lax.axis_index("gy") // 2, 1)


def reorder(vector):
    me = lax.axis_index("gy")
    block = vector.shape[0] // 4
    return jnp.concatenate(
        [lax.dynamic_slice_in_dim(vector, (me ^ by) * block, block, 0) for by in range(4)]
    )


def gather_x(block):
    if lax.axis_size("gx") == 2:
        return [block, swap(block, "gx", 1)]
    whole = lax.all_gather(block, "gx", axis=1, tiled=True)
    half = whole.shape[1] // 2
    return [whole[:, :half], whole[:, half:]]


def split_x(whole):
    half = whole.shape[-1] // 2
    if lax.axis_size("gx") == 2:
        me = lax.axis_index("gx")
        return [
            lax.dynamic_slice_in_dim(whole, me * half, half, whole.ndim - 1),
            lax.dynamic_slice_in_dim(whole, (1 - me) * half, half, whole.ndim - 1),
        ]
    return [whole[..., :half], whole[..., half:]]


def reduce_x(chunks, dim=-1):
    if lax.axis_size("gx") == 2:
        return add(chunks[0], swap(chunks[1], "gx", 1))
    dim = chunks[0].ndim + dim
    return lax.psum_scatter(
        jnp.concatenate(chunks, axis=dim), "gx", scatter_dimension=dim, tiled=True
    )


def sum_z(value):
    peers = lax.axis_size("dp")
    if peers != 4:
        return lax.psum(value.astype(F32), "dp")
    me = lax.axis_index("dp")
    inner = add(value, lax.ppermute(value, "dp", [(0, 1), (3, 2)]))
    total = add(inner, lax.ppermute(inner, "dp", [(1, 2), (2, 1)]))
    outer = lax.ppermute(total, "dp", [(1, 0), (2, 3)])
    return jnp.where((me == 0) | (me == 3), outer, total).astype(F32)


LOW = 448
HIGH_PAD = 48


def pair_sums_kernel(keep_ref, got_ref, low_ref, near_ref, far_ref):
    def total(k, rows):
        return (keep_ref[k, rows, :].astype(F32) + got_ref[k, rows, :].astype(F32)).astype(BF)

    for k, high_ref in enumerate((near_ref, far_ref)):
        low_ref[k] = total(k, slice(0, LOW))
        size = high_ref.shape[0] - HIGH_PAD
        high_ref[:size, :] = total(k, slice(LOW, LOW + size))
        high_ref[size:, :] = jnp.zeros((HIGH_PAD, high_ref.shape[1]), BF)


def pair_sums(keep, got):
    rows, width = keep.shape[1:]
    high = rows - LOW + HIGH_PAD
    tile = 256

    def block(*dims):
        return pl.BlockSpec((*dims, tile), lambda i: (*(0 for _ in dims), i))

    return pl.pallas_call(
        pair_sums_kernel,
        grid=(width // tile,),
        in_specs=[block(2, rows), block(2, rows)],
        out_specs=[block(2, LOW), block(high), block(high)],
        out_shape=[
            jax.ShapeDtypeStruct((2, LOW, width), BF),
            jax.ShapeDtypeStruct((high, width), BF),
            jax.ShapeDtypeStruct((high, width), BF),
        ],
        compiler_params=pltpu.CompilerParams(vmem_limit_bytes=32 * 2**20),
        cost_estimate=TINY,
        name="pair_sums",
    )(keep, got)


def bit_z(by):
    return (lax.axis_index("dp") // by) % 2


def kept_z(value, by):
    half = value.shape[0] // 2
    return lax.dynamic_slice_in_dim(value, bit_z(by) * half, half, 0)


def halve_z(value, by):
    half = value.shape[0] // 2
    return swap(lax.dynamic_slice_in_dim(value, (1 - bit_z(by)) * half, half, 0), "dp", by)


def sum_all(value):
    for axis in ("gy", "gx", "dp"):
        by = 1
        while by < lax.axis_size(axis):
            value = value + swap(value, axis, by)
            by *= 2
    return value


RANGES = ((0, 768), (0, 1024), (512, 1280), (512, 1536))


def fill_bias(starts_ref, bias_ref):
    offset = 0
    for tile, (low, high) in enumerate(RANGES):
        size = high - low
        place = lax.broadcasted_iota(jnp.int32, (size, TILE), 0) + (low - PRIOR)
        query = lax.broadcasted_iota(jnp.int32, (size, TILE), 1) + tile * TILE
        start = starts_ref[:, tile * TILE : (tile + 1) * TILE]
        allowed = (place >= start) & (place <= query)
        bias_ref[offset : offset + size, :] = jnp.where(allowed, 0.0, NEG)
        offset += size


BIAS_ROWS = sum(high - low for low, high in RANGES)


def turned(prior, own, out_ref):
    out_ref[:PRIOR, :] = prior.astype(F32).T.astype(BF)
    out_ref[PRIOR:, :] = own.astype(F32).T.astype(BF)


def forward_kernel(
    starts_ref, q_ref, prior_ref, own_ref, mixed_ref, lse_ref, keys, values, bias
):
    @pl.when(pl.program_id(0) == 0)
    def _():
        fill_bias(starts_ref, bias)

    turned(prior_ref[0, :HEAD, :], own_ref[0, :HEAD, :], keys)
    values[:, :PRIOR] = prior_ref[0, HEAD:, :]
    values[:, PRIOR:] = own_ref[0, HEAD:, :]
    offset = 0
    for tile, (low, high) in enumerate(RANGES):
        size = high - low
        lanes = slice(tile * TILE, (tile + 1) * TILE)
        for head in range(GROUP):
            rows = slice(head * HEAD, (head + 1) * HEAD)
            scores = dot(keys[low:high, :], q_ref[rows, lanes], 1, 0)
            scores = scores + bias[offset : offset + size, :]
            top = jnp.max(scores, axis=0, keepdims=True)
            weights = jnp.exp(scores - top)
            total = jnp.sum(weights, axis=0, keepdims=True)
            out = dot(values[:, low:high], weights.astype(BF), 1, 0)
            mixed_ref[rows, lanes] = (out / total).astype(BF)
            lse_ref[0, head : head + 1, lanes] = top + jnp.log(total)
        offset += size


def attention_forward(starts, queries, prior_kv, own_kv):
    count = queries.shape[1]
    wide = GROUP * HEAD
    prior = pl.BlockSpec((1, 2 * HEAD, PRIOR), lambda g: (g, 0, 0))
    own = pl.BlockSpec((1, 2 * HEAD, count), lambda g: (g, 0, 0))
    return pl.pallas_call(
        forward_kernel,
        grid=(KV_HEADS,),
        in_specs=[
            pl.BlockSpec((1, count), lambda g: (0, 0)),
            pl.BlockSpec((wide, count), lambda g: (g, 0)),
            prior,
            own,
        ],
        out_specs=[
            pl.BlockSpec((wide, count), lambda g: (g, 0)),
            pl.BlockSpec((1, 8, count), lambda g: (g, 0, 0)),
        ],
        out_shape=[
            jax.ShapeDtypeStruct((HEADS * HEAD, count), BF),
            jax.ShapeDtypeStruct((KV_HEADS, 8, count), F32),
        ],
        scratch_shapes=[
            pltpu.VMEM((PRIOR + count, HEAD), BF),
            pltpu.VMEM((HEAD, PRIOR + count), BF),
            pltpu.VMEM((BIAS_ROWS, TILE), F32),
        ],
        compiler_params=pltpu.CompilerParams(vmem_limit_bytes=40 * 2**20),
        cost_estimate=TINY,
        name="attend_forward",
    )(starts, queries, prior_kv, own_kv)


def backward_kernel(
    starts_ref,
    cos_ref,
    sin_ref,
    q_ref,
    prior_ref,
    own_ref,
    mixed_ref,
    lse_ref,
    grad_ref,
    dq_ref,
    dprior_ref,
    down_ref,
    keys,
    turned_keys,
    turned_values,
    dk,
    dv,
    bias,
):
    @pl.when(pl.program_id(0) == 0)
    def _():
        fill_bias(starts_ref, bias)

    turned(prior_ref[0, :HEAD, :], own_ref[0, :HEAD, :], turned_keys)
    turned(prior_ref[0, HEAD:, :], own_ref[0, HEAD:, :], turned_values)
    keys[:, :PRIOR] = prior_ref[0, :HEAD, :]
    keys[:, PRIOR:] = own_ref[0, :HEAD, :]
    dk[...] = jnp.zeros_like(dk)
    dv[...] = jnp.zeros_like(dv)
    offset = 0
    for tile, (low, high) in enumerate(RANGES):
        size = high - low
        lanes = slice(tile * TILE, (tile + 1) * TILE)
        for head in range(GROUP):
            rows = slice(head * HEAD, (head + 1) * HEAD)
            query = q_ref[rows, lanes]
            grad = grad_ref[rows, lanes]
            inner = jnp.sum(
                grad.astype(F32) * mixed_ref[rows, lanes].astype(F32), axis=0, keepdims=True
            )
            lse = lse_ref[0, head : head + 1, lanes]
            scores = dot(turned_keys[low:high, :], query, 1, 0)
            weights = jnp.exp(scores + bias[offset : offset + size, :] - lse)
            prob_grad = dot(turned_values[low:high, :], grad, 1, 0)
            score_grad = (weights * (prob_grad - inner)).astype(BF)
            weights = weights.astype(BF)
            dv[low:high, :] += dot(weights, grad, 1, 1)
            dk[low:high, :] += dot(score_grad, query, 1, 1)
            dq = dot(keys[:, low:high], score_grad, 1, 0) * HEAD ** (-0.5)
            cosine, sine = cos_ref[:, lanes], sin_ref[:, lanes]
            front, back = dq[:HALF], dq[HALF:]
            base = head * HEAD
            dq_ref[base : base + HALF, lanes] = (front * cosine + back * sine).astype(BF)
            dq_ref[base + HALF : base + HEAD, lanes] = (back * cosine - front * sine).astype(BF)
        offset += size
    dprior_ref[0, :HEAD, :] = dk[:PRIOR, :].T.astype(BF)
    dprior_ref[0, HEAD:, :] = dv[:PRIOR, :].T.astype(BF)
    down_ref[0, :HEAD, :] = dk[PRIOR:, :].T
    down_ref[0, HEAD:, :] = dv[PRIOR:, :].T


def attention_backward(
    starts, cosine, sine, queries, prior_kv, own_kv, mixed, lse, grads
):
    count = queries.shape[1]
    wide = GROUP * HEAD
    prior = pl.BlockSpec((1, 2 * HEAD, PRIOR), lambda g: (g, 0, 0))
    own = pl.BlockSpec((1, 2 * HEAD, count), lambda g: (g, 0, 0))
    heads = pl.BlockSpec((wide, count), lambda g: (g, 0))
    table = pl.BlockSpec((HALF, count), lambda g: (0, 0))
    return pl.pallas_call(
        backward_kernel,
        grid=(KV_HEADS,),
        in_specs=[
            pl.BlockSpec((1, count), lambda g: (0, 0)),
            table,
            table,
            heads,
            prior,
            own,
            heads,
            pl.BlockSpec((1, 8, count), lambda g: (g, 0, 0)),
            heads,
        ],
        out_specs=[heads, prior, own],
        out_shape=[
            jax.ShapeDtypeStruct((HEADS * HEAD, count), BF),
            jax.ShapeDtypeStruct((KV_HEADS, 2 * HEAD, PRIOR), BF),
            jax.ShapeDtypeStruct((KV_HEADS, 2 * HEAD, count), F32),
        ],
        scratch_shapes=[
            pltpu.VMEM((HEAD, PRIOR + count), BF),
            pltpu.VMEM((PRIOR + count, HEAD), BF),
            pltpu.VMEM((PRIOR + count, HEAD), BF),
            pltpu.VMEM((PRIOR + count, HEAD), F32),
            pltpu.VMEM((PRIOR + count, HEAD), F32),
            pltpu.VMEM((BIAS_ROWS, TILE), F32),
        ],
        compiler_params=pltpu.CompilerParams(vmem_limit_bytes=44 * 2**20),
        cost_estimate=TINY,
        name="attend_backward",
    )(starts, cosine, sine, queries, prior_kv, own_kv, mixed, lse, grads)


def mlp_kernel(first, *refs):
    normed_ref, up_ref, base_ref = refs[:3]
    refs = refs[3:]
    if not first:
        grad_in_ref, refs = refs[0], refs[1:]
    blocks, refs = refs[:4], refs[4:]
    out_refs, refs = (refs[:1], refs[1:]) if first else (refs[:2], refs[2:])
    grad_out_ref, keep_ref, send_ref, total_ref, grad_total_ref = refs
    step = pl.program_id(0)
    last = pl.num_programs(0) - 1

    @pl.when(step == 0)
    def _():
        total_ref[...] = base_ref[...]
        if first:
            grad_total_ref[...] = jnp.zeros_like(grad_total_ref)
        else:
            grad_total_ref[...] = grad_in_ref[...]

    normed = normed_ref[...]
    upstream = up_ref[...]
    block = normed.shape[0] // 4
    w_gate = jnp.concatenate([ref[:block] for ref in blocks], axis=0)
    w_up = jnp.concatenate([ref[block : 2 * block] for ref in blocks], axis=0)
    w_down = jnp.concatenate([ref[2 * block :] for ref in blocks], axis=0)
    gate = dot(w_gate, normed, 0, 0)
    up = dot(w_up, normed, 0, 0)
    hidden_grad = dot(w_down, upstream, 0, 0)
    sigmoid = 1.0 / (1.0 + jnp.exp(-gate))
    silu = gate * sigmoid
    hidden = (silu * up).astype(BF)
    gate_grad = (hidden_grad * up * (sigmoid * (1.0 + gate * (1.0 - sigmoid)))).astype(BF)
    up_grad = (hidden_grad * silu).astype(BF)
    total_ref[...] += dot(w_down, hidden, 1, 0)
    grad_total_ref[...] += dot(w_gate, gate_grad, 1, 0) + dot(w_up, up_grad, 1, 0)
    for place, (left, right) in enumerate(
        ((normed, gate_grad), (normed, up_grad), (upstream, hidden))
    ):
        made = dot(left, right, 1, 1).astype(BF)
        rows = slice(place * block, (place + 1) * block)
        keep_ref[0, rows, :] = made[:block]
        send_ref[0, rows, :] = made[block : 2 * block]
        keep_ref[1, rows, :] = made[2 * block : 3 * block]
        send_ref[1, rows, :] = made[3 * block :]

    @pl.when(step == last)
    def _():
        if first:
            out_refs[0][...] = total_ref[...]
        else:
            for number in range(4):
                rows = slice((number // 2) * block, (number // 2 + 1) * block)
                source = slice(number * block, (number + 1) * block)
                out_refs[number % 2][rows, :] = total_ref[source, :].astype(BF)
        grad_out_ref[...] = grad_total_ref[...]


def mlp_chunk(normed, upstream, base, grad_in, blocks):
    first = grad_in is None
    width, count = normed.shape
    rows, size = blocks[0].shape
    tile = TILE
    whole = pl.BlockSpec((width, count), lambda i: (0, 0), pipeline_mode=pl.Buffered(1))
    half = pl.BlockSpec((width // 2, count), lambda i: (0, 0), pipeline_mode=pl.Buffered(1))
    across = pl.BlockSpec((rows, tile), lambda i: (0, i))
    made = pl.BlockSpec((2, rows, tile), lambda i: (0, 0, i))
    operands = [normed, upstream, base] + ([] if first else [grad_in])
    return pl.pallas_call(
        functools.partial(mlp_kernel, first),
        grid=(size // tile,),
        in_specs=[whole] * len(operands) + [across] * 4,
        out_specs=([whole] if first else [half, half]) + [whole, made, made],
        out_shape=(
            [jax.ShapeDtypeStruct((width, count), F32)]
            if first
            else [jax.ShapeDtypeStruct((width // 2, count), BF)] * 2
        )
        + [
            jax.ShapeDtypeStruct((width, count), F32),
            jax.ShapeDtypeStruct((2, rows, size), BF),
            jax.ShapeDtypeStruct((2, rows, size), BF),
        ],
        scratch_shapes=[pltpu.VMEM((width, count), F32), pltpu.VMEM((width, count), F32)],
        compiler_params=pltpu.CompilerParams(vmem_limit_bytes=56 * 2**20),
        cost_estimate=TINY,
        name="feed_forward",
    )(*operands, *blocks)


VMEM = pl.BlockSpec(memory_space=pltpu.VMEM)
SMEM = pl.BlockSpec(memory_space=pltpu.SMEM)
Q_WIDTH = HEADS * HEAD
KV_WIDTH = KV_HEADS * HEAD
QKV_WIDTH = Q_WIDTH + 2 * KV_WIDTH
QKV_PART = QKV_WIDTH // 2
OUT_PART = Q_WIDTH // 2
WIDE = 256


def place_of(flip_ref, half, size):
    return pl.ds(pl.multiple_of((flip_ref[0] ^ half) * size, 16), size)


def stacked(refs, columns):
    return jnp.concatenate([ref[:, columns] for ref in refs], axis=0)


QKV_COLUMNS = slice(0, QKV_PART)
OUT_COLUMNS = slice(QKV_PART, QKV_PART + OUT_PART)


def norm_scale_of(values):
    return lax.rsqrt(jnp.mean(values * values, axis=0, keepdims=True) + EPS)


def norm_back(values, scale, gain, gradient):
    weighted = gradient * gain
    inner = jnp.mean(weighted * values, axis=0, keepdims=True)
    values_grad = scale * weighted - values * (scale * scale * scale) * inner
    return (values_grad, jnp.sum(gradient * values * scale, axis=1, keepdims=True))


def project_kernel(flip_ref, near_ref, got_ref, far_ref, gain_ref, cos_ref, sin_ref, *refs):
    weights = refs[:8]
    x_ref, normed_ref, q_ref, own_ref, prior_ref, made = refs[8:]
    block = near_ref.shape[0]
    x_ref[:block, :] = near_ref[...]
    x_ref[block : 2 * block, :] = got_ref[:block, :]
    x_ref[2 * block : 3 * block, :] = far_ref[...]
    x_ref[3 * block :, :] = got_ref[block:, :]
    x = x_ref[...].astype(F32)
    normed = (x * norm_scale_of(x) * gain_ref[...]).astype(BF)
    normed_ref[...] = normed
    for half in range(2):
        weight = stacked(weights[4 * half : 4 * half + 4], QKV_COLUMNS)
        made[place_of(flip_ref, half, QKV_PART), :] = dot(weight, normed, 0, 0).astype(BF)
    cosine, sine = cos_ref[...], sin_ref[...]
    count = cosine.shape[1]

    def rotated(base, scale):
        front = made[base : base + HALF, :].astype(F32)
        back = made[base + HALF : base + HEAD, :].astype(F32)
        return (
            ((front * cosine - back * sine) * scale).astype(BF),
            ((back * cosine + front * sine) * scale).astype(BF),
        )

    for head in range(HEADS):
        base = head * HEAD
        front, back = rotated(base, HEAD ** (-0.5))
        q_ref[base : base + HALF, :] = front
        q_ref[base + HALF : base + HEAD, :] = back
    for head in range(KV_HEADS):
        front, back = rotated(Q_WIDTH + head * HEAD, 1.0)
        base = Q_WIDTH + KV_WIDTH + head * HEAD
        value = made[base : base + HEAD, :]
        own_ref[head, :HALF, :] = front
        own_ref[head, HALF:HEAD, :] = back
        own_ref[head, HEAD:, :] = value
        prior_ref[head, :HALF, :] = front[:, count - PRIOR :]
        prior_ref[head, HALF:HEAD, :] = back[:, count - PRIOR :]
        prior_ref[head, HEAD:, :] = value[:, count - PRIOR :]


def call_whole(kernel, name, ins, outs, scratch=()):
    return pl.pallas_call(
        kernel,
        in_specs=[SMEM] + [VMEM] * (len(ins) - 1),
        out_specs=[VMEM] * len(outs),
        out_shape=[jax.ShapeDtypeStruct(shape, kind) for shape, kind in outs],
        scratch_shapes=list(scratch),
        compiler_params=pltpu.CompilerParams(vmem_limit_bytes=56 * 2**20),
        cost_estimate=TINY,
        name=name,
    )(*ins)


def project(flip, pieces, gain, cosine, sine, weights):
    block, count = pieces[0].shape
    width = 4 * block
    return call_whole(
        project_kernel,
        "project",
        (flip, *pieces, gain, cosine, sine, *weights),
        (
            ((width, count), BF),
            ((width, count), BF),
            ((Q_WIDTH, count), BF),
            ((KV_HEADS, 2 * HEAD, count), BF),
            ((KV_HEADS, 2 * HEAD, PRIOR), BF),
        ),
        (pltpu.VMEM((QKV_WIDTH, count), BF),),
    )


def branch_kernel(flip_ref, x_ref, gain_ref, mixed_ref, *refs):
    weights = refs[:8]
    middle_ref, normed_ref = refs[8:]
    middle = x_ref[...].astype(F32)
    for half in range(2):
        weight = stacked(weights[4 * half : 4 * half + 4], OUT_COLUMNS)
        middle = middle + dot(weight, mixed_ref[place_of(flip_ref, half, OUT_PART), :], 1, 0)
    middle_ref[...] = middle
    normed_ref[...] = (middle * norm_scale_of(middle) * gain_ref[...]).astype(BF)


def branch(flip, inputs, gain, mixed, weights):
    shape = inputs.shape
    return call_whole(
        branch_kernel,
        "branch",
        (flip, inputs, gain, mixed, *weights),
        ((shape, F32), (shape, BF)),
    )


def branch_back_kernel(flip_ref, grad_ref, middle_ref, up_ref, gain_ref, mixed_ref, *refs):
    weights = refs[:8]
    mid_grad_ref, mixed_grad_ref, gain_grad_ref, keep_ref, send_ref = refs[8:]
    middle = middle_ref[...]
    mid_grad, gain_grad = norm_back(
        middle, norm_scale_of(middle), gain_ref[...], grad_ref[...]
    )
    gain_grad_ref[...] = gain_grad
    mid_grad = mid_grad + up_ref[...].astype(F32)
    mid_grad_ref[...] = mid_grad
    branch_grad = mid_grad.astype(BF)
    block = branch_grad.shape[0] // 4
    for half in range(2):
        place = place_of(flip_ref, half, OUT_PART)
        weight = stacked(weights[4 * half : 4 * half + 4], OUT_COLUMNS)
        mixed_grad_ref[place, :] = dot(weight, branch_grad, 0, 0).astype(BF)
        heads = mixed_ref[place, :]
        for number in range(4):
            rows = branch_grad[number * block : (number + 1) * block]
            target = send_ref if number % 2 else keep_ref
            target[half, number // 2] = dot(heads, rows, 1, 1).astype(BF)


def branch_back(flip, grad, middle, upstream, gain, mixed, weights):
    width, count = middle.shape
    parts = (2, 2, OUT_PART, width // 4)
    return call_whole(
        branch_back_kernel,
        "branch_back",
        (flip, grad, middle, upstream, gain, mixed, *weights),
        (
            ((width, count), F32),
            ((Q_WIDTH, count), BF),
            ((width, 1), F32),
            (parts, BF),
            (parts, BF),
        ),
    )


def qkv_grad_kernel(
    flip_ref,
    normed_ref,
    dq_ref,
    own_ref,
    prior_ref,
    cos_ref,
    sin_ref,
    out_keep_ref,
    out_send_ref,
    made_ref,
    keep_ref,
    send_ref,
):
    block = out_keep_ref.shape[3]
    for target, source in ((keep_ref, out_keep_ref), (send_ref, out_send_ref)):
        target[:, :, :, block:] = jnp.zeros((*target.shape[:3], WIDE - block), BF)
        target[:, :, QKV_PART:, :block] = source[...]
    made_ref[:Q_WIDTH, :] = dq_ref[...]
    count = own_ref.shape[2]
    cosine, sine = cos_ref[...], sin_ref[...]
    for head in range(KV_HEADS):
        sent = prior_ref[head].astype(F32)
        both = jnp.concatenate(
            [own_ref[head, :, : count - PRIOR], own_ref[head, :, count - PRIOR :] + sent], axis=1
        )
        front, back = both[:HALF], both[HALF:HEAD]
        base = Q_WIDTH + head * HEAD
        made_ref[base : base + HALF, :] = (front * cosine + back * sine).astype(BF)
        made_ref[base + HALF : base + HEAD, :] = (back * cosine - front * sine).astype(BF)
        base += KV_WIDTH
        made_ref[base : base + HEAD, :] = both[HEAD:].astype(BF)
    normed = normed_ref[...]
    block = normed.shape[0] // 4
    for half in range(2):
        grads = made_ref[place_of(flip_ref, half, QKV_PART), :]
        for number in range(4):
            rows = normed[number * block : (number + 1) * block]
            target = send_ref if number % 2 else keep_ref
            target[half, number // 2, :QKV_PART, :block] = dot(grads, rows, 1, 1).astype(BF)


def qkv_grad(flip, normed, dq, own, prior, cosine, sine, out_keep, out_send):
    width, count = normed.shape
    parts = (2, 2, QKV_PART + OUT_PART, WIDE)
    return call_whole(
        qkv_grad_kernel,
        "qkv_grad",
        (flip, normed, dq, own, prior, cosine, sine, out_keep, out_send),
        (((QKV_WIDTH, count), BF), (parts, BF), (parts, BF)),
    )


def input_grad_kernel(flip_ref, grads_ref, x_ref, gain_ref, mid_grad_ref, *refs):
    weights = refs[:8]
    keep_ref, send_ref, gain_grad_ref = refs[8:]
    total = jnp.zeros(x_ref.shape, F32)
    for half in range(2):
        weight = stacked(weights[4 * half : 4 * half + 4], QKV_COLUMNS)
        total = total + dot(weight, grads_ref[place_of(flip_ref, half, QKV_PART), :], 1, 0)
    x = x_ref[...].astype(F32)
    grad, gain_grad = norm_back(x, norm_scale_of(x), gain_ref[...], total)
    gain_grad_ref[...] = gain_grad
    grad = (grad + mid_grad_ref[...]).astype(BF)
    block = grad.shape[0] // 4
    for number in range(4):
        target = send_ref if number % 2 else keep_ref
        rows = slice((number // 2) * block, (number // 2 + 1) * block)
        target[rows, :] = grad[number * block : (number + 1) * block]


def input_grad(flip, grads, inputs, gain, mid_grad, weights):
    width, count = inputs.shape
    return call_whole(
        input_grad_kernel,
        "input_grad",
        (flip, grads, inputs, gain, mid_grad, *weights),
        (((width // 2, count), BF), ((width // 2, count), BF), ((width, 1), F32)),
    )


def attention_halves(shard, cut):
    if lax.axis_size("gx") == 2:
        return [shard, swap(shard, "gx", 1)]
    peers = lax.axis_size("gx")
    block, width = shard.shape
    whole = lax.all_gather(shard, "gx", axis=1, tiled=True)
    whole = whole.reshape(block, 2, peers // 2, width)
    return [
        jnp.concatenate(
            [
                whole[:, c, :, :cut].reshape(block, peers // 2 * cut),
                whole[:, c, :, cut:].reshape(block, peers // 2 * (width - cut)),
            ],
            axis=1,
        )
        for c in range(2)
    ]


def on_device(
    tokens, doc_start, cotangent, attn_gain, mlp_gain, w_qkv, w_out, w_gate, w_up, w_down
):
    count = doc_start.shape[0]
    block = w_qkv.shape[0]
    pairs_x = lax.axis_size("gx") == 2
    flip = lax.axis_index("gx") if pairs_x else jnp.int32(0)
    flip = jnp.reshape(flip, (1,)).astype(jnp.int32)

    shard = jnp.concatenate([w_qkv, w_out.T], axis=1)
    shard_far = swap(shard, "gy", 2)
    mate = swap(shard, "gy", 1)
    near_halves = attention_halves(shard, w_qkv.shape[1])
    inputs_far = tokens_far(after(tokens, shard_far, *near_halves))
    far_halves = attention_halves(shard_far, w_qkv.shape[1])
    weights = []
    for half, (near, far) in enumerate(zip(near_halves, far_halves)):
        near_mate = mate if pairs_x and half == 0 else swap(near, "gy", 1)
        weights += [near, near_mate, far, swap(far, "gy", 1)]
    pieces = tokens_near(tokens, inputs_far)

    ff_shard = jnp.concatenate([w_gate, w_up, w_down.T], axis=0)
    ff_shard = after(ff_shard, inputs_far, *near_halves, *far_halves)
    ff_far = swap(ff_shard, "gy", 2)
    ff_near_halves = gather_x(ff_shard)
    ff_mate = swap(ff_shard, "gy", 1)

    attn_gain = reorder(attn_gain)[:, None]
    mlp_gain = reorder(mlp_gain)[:, None]

    first_row = lax.axis_index(("dp", "gx", "gy")) * count
    places = first_row + jnp.arange(count, dtype=jnp.int32)
    angle = frequencies()[:, None] * (places - doc_start).astype(F32)[None, :]
    cosine, sine = jnp.cos(angle), jnp.sin(angle)
    starts = (doc_start - first_row)[None, :]

    inputs, normed_one, queries, own_kv, sent_kv = project(
        flip, pieces, attn_gain, cosine, sine, weights
    )
    cotangent = after(cotangent, sent_kv)
    upstream_far = tokens_far(cotangent)
    peers = lax.axis_size("gy")
    ahead = [(i, i + 1) for i in range(0, peers, 2)]
    behind = [(i + 1, i) for i in range(0, peers, 2)]
    prior_kv = lax.ppermute(sent_kv, "gy", ahead)
    mixed, lse = attention_forward(starts, queries, prior_kv, own_kv)

    ff_far, ff_other, upstream_far = after((ff_far, ff_near_halves[1], upstream_far), mixed)
    ff_far_halves = gather_x(ff_far)
    ff_own = ff_near_halves[0] if pairs_x else after(ff_near_halves[0], mixed)
    ff_blocks = [
        [ff_own, ff_mate if pairs_x else swap(ff_own, "gy", 1)],
        [ff_other, swap(ff_other, "gy", 1)],
    ]
    ff_blocks[0] += [ff_far_halves[0], swap(ff_far_halves[0], "gy", 1)]
    near, got, far = tokens_near(cotangent, upstream_far)
    upstream = jnp.concatenate([near, got[:block], far, got[block:]], axis=0)
    middle, normed_two = branch(flip, inputs, mlp_gain, mixed, weights)

    made = mlp_chunk(normed_two, upstream, middle, None, ff_blocks[0])
    ff_far_other = after(ff_far_halves[1], made[0])
    ff_blocks[1] += [ff_far_other, swap(ff_far_other, "gy", 1)]
    later = mlp_chunk(normed_two, upstream, made[0], made[1], ff_blocks[1])
    result_keep, result_send, normed_two_grad, later_keep, later_send = later
    result_near, result_sent = to_features(result_keep, swap(result_send, "gy", 1))
    result_far = swap(result_sent, "gy", 2)
    first_got = swap(made[3], "gy", 1)
    later_got = swap(later_send, "gy", 1)

    early = (result_near, result_sent)
    if pairs_x:
        low_own, near_own, far_own = pair_sums(made[2], first_got)
        low_other, near_other, far_other = pair_sums(
            later_keep, after(later_got, near_own)
        )
        early += (low_own, near_own, far_own, low_other, near_other, far_other)
        low_got = swap(low_other, "gx", 1)
        own_got = swap(far_own, "gy", 2)
        other_got = swap(far_other, "gy", 2)
    mid_grad, mixed_grad, gain_two, out_keep, out_send = branch_back(
        flip, after(normed_two_grad, *early), middle, upstream, mlp_gain, mixed, weights
    )

    def attend_back(mixed_grad, *earlier):
        dq, sent_grad, own_grad = attention_backward(
            starts, cosine, sine, queries, prior_kv, own_kv, mixed, lse, mixed_grad
        )
        prior_grad = lax.ppermute(sent_grad, "gy", behind)
        own_grad = after(own_grad, *earlier)
        grads, keep, send = qkv_grad(
            flip, normed_one, dq, own_grad, prior_grad, cosine, sine, out_keep, out_send
        )
        return grads, keep, swap(send, "gy", 1)

    if not pairs_x:
        grads, qkv_keep, qkv_mate = attend_back(mixed_grad)
        ff_both = reduce_x([add(made[2], first_got), add(later_keep, later_got)])
        ff_sum = sum_z(add(ff_both[0], swap(ff_both[1], "gy", 2)))
        paired = add(qkv_keep, qkv_mate)[..., :block]
        sums = [
            reduce_x([paired[0, :, rows], paired[1, :, rows]], -2)
            for rows in (slice(0, QKV_PART), slice(QKV_PART, None))
        ]
        sum_qkv, sum_out = (sum_z(add(both[0], swap(both[1], "gy", 2))) for both in sums)
        result_shard = assemble(result_near, result_far)
        grad_keep, grad_send, gain_one = input_grad(
            flip, grads, inputs, attn_gain, mid_grad, weights
        )
        grad_near, grad_sent = to_features(grad_keep, swap(grad_send, "gy", 1))
        grad_far = swap(grad_sent, "gy", 2)
        gains = sum_all(jnp.stack([reorder(gain_one[:, 0]), reorder(gain_two[:, 0])]))
    else:
        grads, qkv_keep, qkv_mate = attend_back(
            mixed_grad, own_got, other_got, result_far, low_got
        )

        high_sent = add(near_other, after(other_got, grads))
        high_near = add(near_own, after(own_got, high_sent))
        low_near, low_sent = add_pair(low_own, after(low_got, high_near))
        low_got = swap(low_sent, "gy", 2)
        qkv_near, qkv_sent = add_pair(qkv_keep, after(qkv_mate, low_near))
        qkv_got = swap(qkv_sent, "gx", 1)
        high_got = swap(after(high_sent, qkv_near), "gx", 1)
        grad_keep, grad_send, gain_one = input_grad(
            flip, after(grads, qkv_near), inputs, attn_gain, mid_grad, weights
        )
        grad_got = swap(grad_send, "gy", 1)
        qkv_near, qkv_sent = add_pair(qkv_near, after(qkv_got, grad_keep))
        qkv_got = swap(qkv_sent, "gy", 2)
        low = add(low_near, after(low_got, qkv_near))
        low_got = halve_z(low, 1)
        grad_near, grad_sent = to_features(grad_keep, after(grad_got, low))
        grad_far = swap(grad_sent, "gy", 2)
        result_shard = assemble(result_near, after(result_far, grad_near))
        low = add(kept_z(low, 1), after(low_got, result_shard))
        low_got = halve_z(low, 2)
        qkv_sum = add(qkv_near, after(qkv_got, low))
        qkv_got = halve_z(qkv_sum, 1)
        high = add(high_near, after(high_got, qkv_sum))
        high_got = halve_z(high, 1)
        gain_one, gain_two = after((gain_one, gain_two), high)
        gains = jnp.stack([reorder(gain_one[:, 0]), reorder(gain_two[:, 0])])
        gains_got = swap(gains, "gx", 1)
        low = add(kept_z(low, 2), after(low_got, gains))
        low_got = swap(low, "dp", 2)
        qkv_sum = add(kept_z(qkv_sum, 1), after(qkv_got, low))
        qkv_got = halve_z(qkv_sum, 2)
        gains = gains + after(gains_got, qkv_sum)
        gains_got = swap(gains, "gy", 1)
        high = add(kept_z(high, 1), after(high_got, gains))
        high_got = halve_z(high, 2)
        gains = gains + after(gains_got, high)
        gains_got = swap(gains, "gy", 2)
        qkv_sum = add(kept_z(qkv_sum, 2), after(qkv_got, gains))
        qkv_got = swap(qkv_sum, "dp", 2)
        low = ordered(low, after(low_got, qkv_sum), bit_z(2), 0)
        low_got = swap(low, "dp", 1)
        high = add(kept_z(high, 2), after(high_got, low))
        high_got = swap(high, "dp", 2)
        gains = gains + after(gains_got, high)
        gains_got = swap(gains, "dp", 1)
        qkv_sum = ordered(qkv_sum, after(qkv_got, gains), bit_z(2), 0)
        qkv_got = swap(qkv_sum, "dp", 1)
        low = ordered(low, after(low_got, qkv_sum), bit_z(1), 0).astype(F32)
        high = ordered(high, after(high_got, low), bit_z(2), 0)
        high_got = swap(high, "dp", 1)
        gains = gains + after(gains_got, high)
        gains_got = swap(gains, "dp", 2)
        qkv_sum = ordered(qkv_sum, after(qkv_got, gains), bit_z(1), 0).astype(F32)
        sum_qkv, sum_out = qkv_sum[:QKV_PART, :block], qkv_sum[QKV_PART:, :block]
        high = ordered(high, after(high_got, qkv_sum), bit_z(1), 0).astype(F32)
        gains = gains + after(gains_got, high)
        ff_sum = jnp.concatenate([low, high[: high.shape[0] - HIGH_PAD]], axis=0)
    return (
        result_shard,
        assemble(grad_near, grad_far),
        sum_qkv.T,
        sum_out,
        ff_sum[:block],
        ff_sum[block : 2 * block],
        ff_sum[2 * block :].T,
        gains[0],
        gains[1],
    )


def solution(mesh):
    placed = (
        P("gy", ("dp", "gx")),
        P(("dp", "gx", "gy")),
        P("gy", ("dp", "gx")),
        P(),
        P(),
        P("gy", "gx"),
        P("gx", "gy"),
        P("gy", "gx"),
        P("gy", "gx"),
        P("gx", "gy"),
    )
    return jax.shard_map(
        on_device,
        mesh=mesh,
        in_specs=placed,
        out_specs=(
            P("gy", ("dp", "gx")),
            P("gy", ("dp", "gx")),
            P("gy", "gx"),
            P("gx", "gy"),
            P("gy", "gx"),
            P("gy", "gx"),
            P("gx", "gy"),
            P(),
            P(),
        ),
        check_vma=False,
    )
```

```python
import functools

import jax
import jax.numpy as jnp
from jax import lax
from jax.experimental import pallas as pl
from jax.experimental.pallas import tpu as pltpu
from jax.sharding import PartitionSpec as P

HEADS = 15
KV_HEADS = 5
GROUP = HEADS // KV_HEADS
HEAD = 64
HALF = HEAD // 2
PRIOR = 512
TILE = 256

EPS = 1e-05
THETA = 100000.0
NEG = -1e30

TINY = pl.CostEstimate(flops=1000, bytes_accessed=1000, transcendentals=0)

BF = jnp.bfloat16
F32 = jnp.float32


def swap(value, axis, by):
    peers = lax.axis_size(axis)
    return lax.ppermute(value, axis, [(i, i ^ by) for i in range(peers)])


def dot(left, right, left_dim, right_dim):
    return lax.dot_general(
        left, right, (((left_dim,), (right_dim,)), ((), ())), preferred_element_type=F32
    )


def add_kernel(left_ref, right_ref, out_ref):
    out_ref[...] = (left_ref[...].astype(F32) + right_ref[...].astype(F32)).astype(BF)


def add(left, right):
    width = left.shape[-1]
    rows = left.size // width
    if left.shape[-2] % 16:
        return (left.astype(F32) + right.astype(F32)).astype(BF)
    step = max(
        size for size in range(16, 513, 16) if rows % size == 0
    )
    spec = pl.BlockSpec((step, width), lambda i: (i, 0))
    return pl.pallas_call(
        add_kernel,
        grid=(rows // step,),
        in_specs=[spec, spec],
        out_specs=spec,
        out_shape=jax.ShapeDtypeStruct((rows, width), BF),
        compiler_params=pltpu.CompilerParams(vmem_limit_bytes=24 * 2**20),
        cost_estimate=TINY,
        name="add",
    )(left.reshape(rows, width), right.reshape(rows, width)).reshape(left.shape)


def add_pair_kernel(left_ref, right_ref, first_ref, second_ref):
    for k, out_ref in enumerate((first_ref, second_ref)):
        out_ref[...] = (left_ref[k].astype(F32) + right_ref[k].astype(F32)).astype(BF)


def add_pair(left, right):
    shape = left.shape[1:]
    width = shape[-1]
    rows = left.size // (2 * width)
    step = max(size for size in range(16, 257, 16) if rows % size == 0)
    spec = pl.BlockSpec((2, step, width), lambda i: (0, i, 0))
    out = pl.BlockSpec((step, width), lambda i: (i, 0))
    first, second = pl.pallas_call(
        add_pair_kernel,
        grid=(rows // step,),
        in_specs=[spec, spec],
        out_specs=[out, out],
        out_shape=[jax.ShapeDtypeStruct((rows, width), BF)] * 2,
        compiler_params=pltpu.CompilerParams(vmem_limit_bytes=24 * 2**20),
        cost_estimate=TINY,
        name="add_pair",
    )(left.reshape(2, rows, width), right.reshape(2, rows, width))
    return first.reshape(shape), second.reshape(shape)


def frequencies():
    return jnp.power(THETA, -jnp.arange(HALF, dtype=F32) / HALF)


def after(value, *earlier):
    return lax.optimization_barrier((value, earlier))[0]


def ordered(mine, theirs, bit, axis):
    return jnp.where(
        bit == 0,
        jnp.concatenate([mine, theirs], axis=axis),
        jnp.concatenate([theirs, mine], axis=axis),
    )


def tokens_far(shard):
    me = lax.axis_index("gy")
    pair = shard.shape[1] // 2
    other = lax.dynamic_slice_in_dim(shard, (1 - me // 2) * pair, pair, 1)
    return swap(other, "gy", 2)


def tokens_near(shard, far):
    me = lax.axis_index("gy")
    rows = far.shape[1] // 2
    own, mate = (me % 2) * rows, (1 - me % 2) * rows
    base = (me // 2) * 2 * rows
    sent = jnp.concatenate(
        [
            lax.dynamic_slice_in_dim(shard, base + mate, rows, 1),
            lax.dynamic_slice_in_dim(far, mate, rows, 1),
        ],
        axis=0,
    )
    got = swap(sent, "gy", 1)
    return (
        lax.dynamic_slice_in_dim(shard, base + own, rows, 1),
        got,
        lax.dynamic_slice_in_dim(far, own, rows, 1),
    )


def to_features(kept, got):
    me = lax.axis_index("gy")
    block = kept.shape[0] // 2
    near = ordered(kept[:block], got[:block], me % 2, 1)
    far = ordered(kept[block:], got[block:], me % 2, 1)
    return near, far


def assemble(near, far):
    return ordered(near, far, lax.axis_index("gy") // 2, 1)


def reorder(vector):
    me = lax.axis_index("gy")
    block = vector.shape[0] // 4
    return jnp.concatenate(
        [lax.dynamic_slice_in_dim(vector, (me ^ by) * block, block, 0) for by in range(4)]
    )


def gather_x(block):
    if lax.axis_size("gx") == 2:
        return [block, swap(block, "gx", 1)]
    whole = lax.all_gather(block, "gx", axis=1, tiled=True)
    half = whole.shape[1] // 2
    return [whole[:, :half], whole[:, half:]]


def split_x(whole):
    half = whole.shape[-1] // 2
    if lax.axis_size("gx") == 2:
        me = lax.axis_index("gx")
        return [
            lax.dynamic_slice_in_dim(whole, me * half, half, whole.ndim - 1),
            lax.dynamic_slice_in_dim(whole, (1 - me) * half, half, whole.ndim - 1),
        ]
    return [whole[..., :half], whole[..., half:]]


def reduce_x(chunks, dim=-1):
    if lax.axis_size("gx") == 2:
        return add(chunks[0], swap(chunks[1], "gx", 1))
    dim = chunks[0].ndim + dim
    return lax.psum_scatter(
        jnp.concatenate(chunks, axis=dim), "gx", scatter_dimension=dim, tiled=True
    )


def sum_z(value):
    peers = lax.axis_size("dp")
    if peers != 4:
        return lax.psum(value.astype(F32), "dp")
    me = lax.axis_index("dp")
    inner = add(value, lax.ppermute(value, "dp", [(0, 1), (3, 2)]))
    total = add(inner, lax.ppermute(inner, "dp", [(1, 2), (2, 1)]))
    outer = lax.ppermute(total, "dp", [(1, 0), (2, 3)])
    return jnp.where((me == 0) | (me == 3), outer, total).astype(F32)


LOW = 448
HIGH_PAD = 48


def pair_sums_kernel(bit_ref, keep_ref, got_ref, low_ref, low_sent_ref, near_ref, far_ref):
    half = LOW // 2

    def total(k, rows):
        return (keep_ref[k, rows, :].astype(F32) + got_ref[k, rows, :].astype(F32)).astype(BF)

    for k, high_ref in enumerate((near_ref, far_ref)):
        for target, bit in ((low_ref, bit_ref[0]), (low_sent_ref, 1 - bit_ref[0])):
            target[k] = total(k, pl.ds(pl.multiple_of(bit * half, 16), half))
        size = high_ref.shape[0] - HIGH_PAD
        high_ref[:size, :] = total(k, slice(LOW, LOW + size))
        high_ref[size:, :] = jnp.zeros((HIGH_PAD, high_ref.shape[1]), BF)


def pair_sums(bit, keep, got):
    rows, width = keep.shape[1:]
    high = rows - LOW + HIGH_PAD
    tile = 256

    def block(*dims):
        return pl.BlockSpec((*dims, tile), lambda i: (*(0 for _ in dims), i))

    return pl.pallas_call(
        pair_sums_kernel,
        grid=(width // tile,),
        in_specs=[SMEM, block(2, rows), block(2, rows)],
        out_specs=[block(2, LOW // 2), block(2, LOW // 2), block(high), block(high)],
        out_shape=[
            jax.ShapeDtypeStruct((2, LOW // 2, width), BF),
            jax.ShapeDtypeStruct((2, LOW // 2, width), BF),
            jax.ShapeDtypeStruct((high, width), BF),
            jax.ShapeDtypeStruct((high, width), BF),
        ],
        compiler_params=pltpu.CompilerParams(vmem_limit_bytes=32 * 2**20),
        cost_estimate=TINY,
        name="pair_sums",
    )(bit, keep, got)


def bit_z(by):
    return (lax.axis_index("dp") // by) % 2


def kept_z(value, by):
    half = value.shape[0] // 2
    return lax.dynamic_slice_in_dim(value, bit_z(by) * half, half, 0)


def halve_z(value, by):
    half = value.shape[0] // 2
    return swap(lax.dynamic_slice_in_dim(value, (1 - bit_z(by)) * half, half, 0), "dp", by)


def sum_all(value):
    for axis in ("gy", "gx", "dp"):
        by = 1
        while by < lax.axis_size(axis):
            value = value + swap(value, axis, by)
            by *= 2
    return value


RANGES = ((0, 768), (0, 1024), (512, 1280), (512, 1536))


def fill_bias(starts_ref, bias_ref):
    offset = 0
    for tile, (low, high) in enumerate(RANGES):
        size = high - low
        place = lax.broadcasted_iota(jnp.int32, (size, TILE), 0) + (low - PRIOR)
        query = lax.broadcasted_iota(jnp.int32, (size, TILE), 1) + tile * TILE
        start = starts_ref[:, tile * TILE : (tile + 1) * TILE]
        allowed = (place >= start) & (place <= query)
        bias_ref[offset : offset + size, :] = jnp.where(allowed, 0.0, NEG)
        offset += size


BIAS_ROWS = sum(high - low for low, high in RANGES)


def turned(prior, own, out_ref):
    out_ref[:PRIOR, :] = prior.astype(F32).T.astype(BF)
    out_ref[PRIOR:, :] = own.astype(F32).T.astype(BF)


def forward_kernel(
    starts_ref, q_ref, prior_ref, own_ref, mixed_ref, lse_ref, keys, values, bias
):
    @pl.when(pl.program_id(0) == 0)
    def _():
        fill_bias(starts_ref, bias)

    turned(prior_ref[0, :HEAD, :], own_ref[0, :HEAD, :], keys)
    values[:, :PRIOR] = prior_ref[0, HEAD:, :]
    values[:, PRIOR:] = own_ref[0, HEAD:, :]
    offset = 0
    for tile, (low, high) in enumerate(RANGES):
        size = high - low
        lanes = slice(tile * TILE, (tile + 1) * TILE)
        for head in range(GROUP):
            rows = slice(head * HEAD, (head + 1) * HEAD)
            scores = dot(keys[low:high, :], q_ref[rows, lanes], 1, 0)
            scores = scores + bias[offset : offset + size, :]
            top = jnp.max(scores, axis=0, keepdims=True)
            weights = jnp.exp(scores - top)
            total = jnp.sum(weights, axis=0, keepdims=True)
            out = dot(values[:, low:high], weights.astype(BF), 1, 0)
            mixed_ref[rows, lanes] = (out / total).astype(BF)
            lse_ref[0, head : head + 1, lanes] = top + jnp.log(total)
        offset += size


def attention_forward(starts, queries, prior_kv, own_kv):
    count = queries.shape[1]
    wide = GROUP * HEAD
    prior = pl.BlockSpec((1, 2 * HEAD, PRIOR), lambda g: (g, 0, 0))
    own = pl.BlockSpec((1, 2 * HEAD, count), lambda g: (g, 0, 0))
    return pl.pallas_call(
        forward_kernel,
        grid=(KV_HEADS,),
        in_specs=[
            pl.BlockSpec((1, count), lambda g: (0, 0)),
            pl.BlockSpec((wide, count), lambda g: (g, 0)),
            prior,
            own,
        ],
        out_specs=[
            pl.BlockSpec((wide, count), lambda g: (g, 0)),
            pl.BlockSpec((1, 8, count), lambda g: (g, 0, 0)),
        ],
        out_shape=[
            jax.ShapeDtypeStruct((HEADS * HEAD, count), BF),
            jax.ShapeDtypeStruct((KV_HEADS, 8, count), F32),
        ],
        scratch_shapes=[
            pltpu.VMEM((PRIOR + count, HEAD), BF),
            pltpu.VMEM((HEAD, PRIOR + count), BF),
            pltpu.VMEM((BIAS_ROWS, TILE), F32),
        ],
        compiler_params=pltpu.CompilerParams(vmem_limit_bytes=40 * 2**20),
        cost_estimate=TINY,
        name="attend_forward",
    )(starts, queries, prior_kv, own_kv)


def backward_kernel(
    starts_ref,
    cos_ref,
    sin_ref,
    q_ref,
    prior_ref,
    own_ref,
    mixed_ref,
    lse_ref,
    grad_ref,
    dq_ref,
    dprior_ref,
    down_ref,
    keys,
    turned_keys,
    turned_values,
    dk,
    dv,
    bias,
):
    @pl.when(pl.program_id(0) == 0)
    def _():
        fill_bias(starts_ref, bias)

    turned(prior_ref[0, :HEAD, :], own_ref[0, :HEAD, :], turned_keys)
    turned(prior_ref[0, HEAD:, :], own_ref[0, HEAD:, :], turned_values)
    keys[:, :PRIOR] = prior_ref[0, :HEAD, :]
    keys[:, PRIOR:] = own_ref[0, :HEAD, :]
    dk[...] = jnp.zeros_like(dk)
    dv[...] = jnp.zeros_like(dv)
    offset = 0
    for tile, (low, high) in enumerate(RANGES):
        size = high - low
        lanes = slice(tile * TILE, (tile + 1) * TILE)
        for head in range(GROUP):
            rows = slice(head * HEAD, (head + 1) * HEAD)
            query = q_ref[rows, lanes]
            grad = grad_ref[rows, lanes]
            inner = jnp.sum(
                grad.astype(F32) * mixed_ref[rows, lanes].astype(F32), axis=0, keepdims=True
            )
            lse = lse_ref[0, head : head + 1, lanes]
            scores = dot(turned_keys[low:high, :], query, 1, 0)
            weights = jnp.exp(scores + bias[offset : offset + size, :] - lse)
            prob_grad = dot(turned_values[low:high, :], grad, 1, 0)
            score_grad = (weights * (prob_grad - inner)).astype(BF)
            weights = weights.astype(BF)
            dv[low:high, :] += dot(weights, grad, 1, 1)
            dk[low:high, :] += dot(score_grad, query, 1, 1)
            dq = dot(keys[:, low:high], score_grad, 1, 0) * HEAD ** (-0.5)
            cosine, sine = cos_ref[:, lanes], sin_ref[:, lanes]
            front, back = dq[:HALF], dq[HALF:]
            base = head * HEAD
            dq_ref[base : base + HALF, lanes] = (front * cosine + back * sine).astype(BF)
            dq_ref[base + HALF : base + HEAD, lanes] = (back * cosine - front * sine).astype(BF)
        offset += size
    dprior_ref[0, :HEAD, :] = dk[:PRIOR, :].T.astype(BF)
    dprior_ref[0, HEAD:, :] = dv[:PRIOR, :].T.astype(BF)
    down_ref[0, :HEAD, :] = dk[PRIOR:, :].T
    down_ref[0, HEAD:, :] = dv[PRIOR:, :].T


def attention_backward(
    starts, cosine, sine, queries, prior_kv, own_kv, mixed, lse, grads
):
    count = queries.shape[1]
    wide = GROUP * HEAD
    prior = pl.BlockSpec((1, 2 * HEAD, PRIOR), lambda g: (g, 0, 0))
    own = pl.BlockSpec((1, 2 * HEAD, count), lambda g: (g, 0, 0))
    heads = pl.BlockSpec((wide, count), lambda g: (g, 0))
    table = pl.BlockSpec((HALF, count), lambda g: (0, 0))
    return pl.pallas_call(
        backward_kernel,
        grid=(KV_HEADS,),
        in_specs=[
            pl.BlockSpec((1, count), lambda g: (0, 0)),
            table,
            table,
            heads,
            prior,
            own,
            heads,
            pl.BlockSpec((1, 8, count), lambda g: (g, 0, 0)),
            heads,
        ],
        out_specs=[heads, prior, own],
        out_shape=[
            jax.ShapeDtypeStruct((HEADS * HEAD, count), BF),
            jax.ShapeDtypeStruct((KV_HEADS, 2 * HEAD, PRIOR), BF),
            jax.ShapeDtypeStruct((KV_HEADS, 2 * HEAD, count), F32),
        ],
        scratch_shapes=[
            pltpu.VMEM((HEAD, PRIOR + count), BF),
            pltpu.VMEM((PRIOR + count, HEAD), BF),
            pltpu.VMEM((PRIOR + count, HEAD), BF),
            pltpu.VMEM((PRIOR + count, HEAD), F32),
            pltpu.VMEM((PRIOR + count, HEAD), F32),
            pltpu.VMEM((BIAS_ROWS, TILE), F32),
        ],
        compiler_params=pltpu.CompilerParams(vmem_limit_bytes=44 * 2**20),
        cost_estimate=TINY,
        name="attend_backward",
    )(starts, cosine, sine, queries, prior_kv, own_kv, mixed, lse, grads)


def mlp_kernel(first, *refs):
    normed_ref, up_ref, base_ref = refs[:3]
    refs = refs[3:]
    if not first:
        grad_in_ref, refs = refs[0], refs[1:]
    blocks, refs = refs[:4], refs[4:]
    out_refs, refs = (refs[:1], refs[1:]) if first else (refs[:2], refs[2:])
    grad_out_ref, keep_ref, send_ref, total_ref, grad_total_ref = refs
    step = pl.program_id(0)
    last = pl.num_programs(0) - 1

    @pl.when(step == 0)
    def _():
        total_ref[...] = base_ref[...]
        if first:
            grad_total_ref[...] = jnp.zeros_like(grad_total_ref)
        else:
            grad_total_ref[...] = grad_in_ref[...]

    normed = normed_ref[...]
    upstream = up_ref[...]
    block = normed.shape[0] // 4
    w_gate = jnp.concatenate([ref[:block] for ref in blocks], axis=0)
    w_up = jnp.concatenate([ref[block : 2 * block] for ref in blocks], axis=0)
    w_down = jnp.concatenate([ref[2 * block :] for ref in blocks], axis=0)
    gate = dot(w_gate, normed, 0, 0)
    up = dot(w_up, normed, 0, 0)
    hidden_grad = dot(w_down, upstream, 0, 0)
    sigmoid = 1.0 / (1.0 + jnp.exp(-gate))
    silu = gate * sigmoid
    hidden = (silu * up).astype(BF)
    gate_grad = (hidden_grad * up * (sigmoid * (1.0 + gate * (1.0 - sigmoid)))).astype(BF)
    up_grad = (hidden_grad * silu).astype(BF)
    total_ref[...] += dot(w_down, hidden, 1, 0)
    grad_total_ref[...] += dot(w_gate, gate_grad, 1, 0) + dot(w_up, up_grad, 1, 0)
    for place, (left, right) in enumerate(
        ((normed, gate_grad), (normed, up_grad), (upstream, hidden))
    ):
        made = dot(left, right, 1, 1).astype(BF)
        rows = slice(place * block, (place + 1) * block)
        keep_ref[0, rows, :] = made[:block]
        send_ref[0, rows, :] = made[block : 2 * block]
        keep_ref[1, rows, :] = made[2 * block : 3 * block]
        send_ref[1, rows, :] = made[3 * block :]

    @pl.when(step == last)
    def _():
        if first:
            out_refs[0][...] = total_ref[...]
        else:
            for number in range(4):
                rows = slice((number // 2) * block, (number // 2 + 1) * block)
                source = slice(number * block, (number + 1) * block)
                out_refs[number % 2][rows, :] = total_ref[source, :].astype(BF)
        grad_out_ref[...] = grad_total_ref[...]


def mlp_chunk(normed, upstream, base, grad_in, blocks):
    first = grad_in is None
    width, count = normed.shape
    rows, size = blocks[0].shape
    tile = TILE
    whole = pl.BlockSpec((width, count), lambda i: (0, 0), pipeline_mode=pl.Buffered(1))
    half = pl.BlockSpec((width // 2, count), lambda i: (0, 0), pipeline_mode=pl.Buffered(1))
    across = pl.BlockSpec((rows, tile), lambda i: (0, i))
    made = pl.BlockSpec((2, rows, tile), lambda i: (0, 0, i))
    operands = [normed, upstream, base] + ([] if first else [grad_in])
    return pl.pallas_call(
        functools.partial(mlp_kernel, first),
        grid=(size // tile,),
        in_specs=[whole] * len(operands) + [across] * 4,
        out_specs=([whole] if first else [half, half]) + [whole, made, made],
        out_shape=(
            [jax.ShapeDtypeStruct((width, count), F32)]
            if first
            else [jax.ShapeDtypeStruct((width // 2, count), BF)] * 2
        )
        + [
            jax.ShapeDtypeStruct((width, count), F32),
            jax.ShapeDtypeStruct((2, rows, size), BF),
            jax.ShapeDtypeStruct((2, rows, size), BF),
        ],
        scratch_shapes=[pltpu.VMEM((width, count), F32), pltpu.VMEM((width, count), F32)],
        compiler_params=pltpu.CompilerParams(vmem_limit_bytes=56 * 2**20),
        cost_estimate=TINY,
        name="feed_forward",
    )(*operands, *blocks)


VMEM = pl.BlockSpec(memory_space=pltpu.VMEM)
SMEM = pl.BlockSpec(memory_space=pltpu.SMEM)
Q_WIDTH = HEADS * HEAD
KV_WIDTH = KV_HEADS * HEAD
QKV_WIDTH = Q_WIDTH + 2 * KV_WIDTH
QKV_PART = QKV_WIDTH // 2
OUT_PART = Q_WIDTH // 2
WIDE = 256


def place_of(flip_ref, half, size):
    return pl.ds(pl.multiple_of((flip_ref[0] ^ half) * size, 16), size)


def stacked(refs, columns):
    return jnp.concatenate([ref[:, columns] for ref in refs], axis=0)


QKV_COLUMNS = slice(0, QKV_PART)
OUT_COLUMNS = slice(QKV_PART, QKV_PART + OUT_PART)


def norm_scale_of(values):
    return lax.rsqrt(jnp.mean(values * values, axis=0, keepdims=True) + EPS)


def norm_back(values, scale, gain, gradient):
    weighted = gradient * gain
    inner = jnp.mean(weighted * values, axis=0, keepdims=True)
    values_grad = scale * weighted - values * (scale * scale * scale) * inner
    return (values_grad, jnp.sum(gradient * values * scale, axis=1, keepdims=True))


def project_kernel(flip_ref, near_ref, got_ref, far_ref, gain_ref, cos_ref, sin_ref, *refs):
    weights = refs[:8]
    x_ref, normed_ref, q_ref, own_ref, prior_ref, made = refs[8:]
    block = near_ref.shape[0]
    x_ref[:block, :] = near_ref[...]
    x_ref[block : 2 * block, :] = got_ref[:block, :]
    x_ref[2 * block : 3 * block, :] = far_ref[...]
    x_ref[3 * block :, :] = got_ref[block:, :]
    x = x_ref[...].astype(F32)
    normed = (x * norm_scale_of(x) * gain_ref[...]).astype(BF)
    normed_ref[...] = normed
    for half in range(2):
        weight = stacked(weights[4 * half : 4 * half + 4], QKV_COLUMNS)
        made[place_of(flip_ref, half, QKV_PART), :] = dot(weight, normed, 0, 0).astype(BF)
    cosine, sine = cos_ref[...], sin_ref[...]
    count = cosine.shape[1]

    def rotated(base, scale):
        front = made[base : base + HALF, :].astype(F32)
        back = made[base + HALF : base + HEAD, :].astype(F32)
        return (
            ((front * cosine - back * sine) * scale).astype(BF),
            ((back * cosine + front * sine) * scale).astype(BF),
        )

    for head in range(HEADS):
        base = head * HEAD
        front, back = rotated(base, HEAD ** (-0.5))
        q_ref[base : base + HALF, :] = front
        q_ref[base + HALF : base + HEAD, :] = back
    for head in range(KV_HEADS):
        front, back = rotated(Q_WIDTH + head * HEAD, 1.0)
        base = Q_WIDTH + KV_WIDTH + head * HEAD
        value = made[base : base + HEAD, :]
        own_ref[head, :HALF, :] = front
        own_ref[head, HALF:HEAD, :] = back
        own_ref[head, HEAD:, :] = value
        prior_ref[head, :HALF, :] = front[:, count - PRIOR :]
        prior_ref[head, HALF:HEAD, :] = back[:, count - PRIOR :]
        prior_ref[head, HEAD:, :] = value[:, count - PRIOR :]


def call_whole(kernel, name, ins, outs, scratch=()):
    return pl.pallas_call(
        kernel,
        in_specs=[SMEM] + [VMEM] * (len(ins) - 1),
        out_specs=[VMEM] * len(outs),
        out_shape=[jax.ShapeDtypeStruct(shape, kind) for shape, kind in outs],
        scratch_shapes=list(scratch),
        compiler_params=pltpu.CompilerParams(vmem_limit_bytes=56 * 2**20),
        cost_estimate=TINY,
        name=name,
    )(*ins)


def project(flip, pieces, gain, cosine, sine, weights):
    block, count = pieces[0].shape
    width = 4 * block
    return call_whole(
        project_kernel,
        "project",
        (flip, *pieces, gain, cosine, sine, *weights),
        (
            ((width, count), BF),
            ((width, count), BF),
            ((Q_WIDTH, count), BF),
            ((KV_HEADS, 2 * HEAD, count), BF),
            ((KV_HEADS, 2 * HEAD, PRIOR), BF),
        ),
        (pltpu.VMEM((QKV_WIDTH, count), BF),),
    )


def branch_kernel(flip_ref, x_ref, gain_ref, mixed_ref, *refs):
    weights = refs[:8]
    middle_ref, normed_ref = refs[8:]
    middle = x_ref[...].astype(F32)
    for half in range(2):
        weight = stacked(weights[4 * half : 4 * half + 4], OUT_COLUMNS)
        middle = middle + dot(weight, mixed_ref[place_of(flip_ref, half, OUT_PART), :], 1, 0)
    middle_ref[...] = middle
    normed_ref[...] = (middle * norm_scale_of(middle) * gain_ref[...]).astype(BF)


def branch(flip, inputs, gain, mixed, weights):
    shape = inputs.shape
    return call_whole(
        branch_kernel,
        "branch",
        (flip, inputs, gain, mixed, *weights),
        ((shape, F32), (shape, BF)),
    )


def branch_back_kernel(flip_ref, grad_ref, middle_ref, up_ref, gain_ref, mixed_ref, *refs):
    weights = refs[:8]
    mid_grad_ref, mixed_grad_ref, gain_grad_ref, keep_ref, send_ref = refs[8:]
    middle = middle_ref[...]
    mid_grad, gain_grad = norm_back(
        middle, norm_scale_of(middle), gain_ref[...], grad_ref[...]
    )
    gain_grad_ref[...] = gain_grad
    mid_grad = mid_grad + up_ref[...].astype(F32)
    mid_grad_ref[...] = mid_grad
    branch_grad = mid_grad.astype(BF)
    block = branch_grad.shape[0] // 4
    for half in range(2):
        place = place_of(flip_ref, half, OUT_PART)
        weight = stacked(weights[4 * half : 4 * half + 4], OUT_COLUMNS)
        mixed_grad_ref[place, :] = dot(weight, branch_grad, 0, 0).astype(BF)
        heads = mixed_ref[place, :]
        for number in range(4):
            rows = branch_grad[number * block : (number + 1) * block]
            target = send_ref if number % 2 else keep_ref
            target[half, number // 2] = dot(heads, rows, 1, 1).astype(BF)


def branch_back(flip, grad, middle, upstream, gain, mixed, weights):
    width, count = middle.shape
    parts = (2, 2, OUT_PART, width // 4)
    return call_whole(
        branch_back_kernel,
        "branch_back",
        (flip, grad, middle, upstream, gain, mixed, *weights),
        (
            ((width, count), F32),
            ((Q_WIDTH, count), BF),
            ((width, 1), F32),
            (parts, BF),
            (parts, BF),
        ),
    )


def qkv_grad_kernel(
    flip_ref,
    normed_ref,
    dq_ref,
    own_ref,
    prior_ref,
    cos_ref,
    sin_ref,
    out_keep_ref,
    out_send_ref,
    made_ref,
    keep_ref,
    send_ref,
):
    block = out_keep_ref.shape[3]
    for target, source in ((keep_ref, out_keep_ref), (send_ref, out_send_ref)):
        target[:, :, :, block:] = jnp.zeros((*target.shape[:3], WIDE - block), BF)
        target[:, :, QKV_PART:, :block] = source[...]
    made_ref[:Q_WIDTH, :] = dq_ref[...]
    count = own_ref.shape[2]
    cosine, sine = cos_ref[...], sin_ref[...]
    for head in range(KV_HEADS):
        sent = prior_ref[head].astype(F32)
        both = jnp.concatenate(
            [own_ref[head, :, : count - PRIOR], own_ref[head, :, count - PRIOR :] + sent], axis=1
        )
        front, back = both[:HALF], both[HALF:HEAD]
        base = Q_WIDTH + head * HEAD
        made_ref[base : base + HALF, :] = (front * cosine + back * sine).astype(BF)
        made_ref[base + HALF : base + HEAD, :] = (back * cosine - front * sine).astype(BF)
        base += KV_WIDTH
        made_ref[base : base + HEAD, :] = both[HEAD:].astype(BF)
    normed = normed_ref[...]
    block = normed.shape[0] // 4
    for half in range(2):
        grads = made_ref[place_of(flip_ref, half, QKV_PART), :]
        for number in range(4):
            rows = normed[number * block : (number + 1) * block]
            target = send_ref if number % 2 else keep_ref
            target[half, number // 2, :QKV_PART, :block] = dot(grads, rows, 1, 1).astype(BF)


def qkv_grad(flip, normed, dq, own, prior, cosine, sine, out_keep, out_send):
    width, count = normed.shape
    parts = (2, 2, QKV_PART + OUT_PART, WIDE)
    return call_whole(
        qkv_grad_kernel,
        "qkv_grad",
        (flip, normed, dq, own, prior, cosine, sine, out_keep, out_send),
        (((QKV_WIDTH, count), BF), (parts, BF), (parts, BF)),
    )


def input_grad_kernel(flip_ref, grads_ref, x_ref, gain_ref, mid_grad_ref, *refs):
    weights = refs[:8]
    keep_ref, send_ref, gain_grad_ref = refs[8:]
    total = jnp.zeros(x_ref.shape, F32)
    for half in range(2):
        weight = stacked(weights[4 * half : 4 * half + 4], QKV_COLUMNS)
        total = total + dot(weight, grads_ref[place_of(flip_ref, half, QKV_PART), :], 1, 0)
    x = x_ref[...].astype(F32)
    grad, gain_grad = norm_back(x, norm_scale_of(x), gain_ref[...], total)
    gain_grad_ref[...] = gain_grad
    grad = (grad + mid_grad_ref[...]).astype(BF)
    block = grad.shape[0] // 4
    for number in range(4):
        target = send_ref if number % 2 else keep_ref
        rows = slice((number // 2) * block, (number // 2 + 1) * block)
        target[rows, :] = grad[number * block : (number + 1) * block]


def input_grad(flip, grads, inputs, gain, mid_grad, weights):
    width, count = inputs.shape
    return call_whole(
        input_grad_kernel,
        "input_grad",
        (flip, grads, inputs, gain, mid_grad, *weights),
        (((width // 2, count), BF), ((width // 2, count), BF), ((width, 1), F32)),
    )


def attention_halves(shard, cut):
    if lax.axis_size("gx") == 2:
        return [shard, swap(shard, "gx", 1)]
    peers = lax.axis_size("gx")
    block, width = shard.shape
    whole = lax.all_gather(shard, "gx", axis=1, tiled=True)
    whole = whole.reshape(block, 2, peers // 2, width)
    return [
        jnp.concatenate(
            [
                whole[:, c, :, :cut].reshape(block, peers // 2 * cut),
                whole[:, c, :, cut:].reshape(block, peers // 2 * (width - cut)),
            ],
            axis=1,
        )
        for c in range(2)
    ]


def on_device(
    tokens, doc_start, cotangent, attn_gain, mlp_gain, w_qkv, w_out, w_gate, w_up, w_down
):
    count = doc_start.shape[0]
    block = w_qkv.shape[0]
    pairs_x = lax.axis_size("gx") == 2
    flip = lax.axis_index("gx") if pairs_x else jnp.int32(0)
    flip = jnp.reshape(flip, (1,)).astype(jnp.int32)

    shard = jnp.concatenate([w_qkv, w_out.T], axis=1)
    shard_far = swap(shard, "gy", 2)
    mate = swap(shard, "gy", 1)
    near_halves = attention_halves(shard, w_qkv.shape[1])
    inputs_far = tokens_far(after(tokens, shard_far, *near_halves))
    far_halves = attention_halves(shard_far, w_qkv.shape[1])
    weights = []
    for half, (near, far) in enumerate(zip(near_halves, far_halves)):
        near_mate = mate if pairs_x and half == 0 else swap(near, "gy", 1)
        weights += [near, near_mate, far, swap(far, "gy", 1)]
    pieces = tokens_near(tokens, inputs_far)

    ff_shard = jnp.concatenate([w_gate, w_up, w_down.T], axis=0)
    ff_shard = after(ff_shard, inputs_far, *near_halves, *far_halves)
    ff_far = swap(ff_shard, "gy", 2)
    ff_near_halves = gather_x(ff_shard)
    ff_mate = swap(ff_shard, "gy", 1)

    attn_gain = reorder(attn_gain)[:, None]
    mlp_gain = reorder(mlp_gain)[:, None]

    first_row = lax.axis_index(("dp", "gx", "gy")) * count
    places = first_row + jnp.arange(count, dtype=jnp.int32)
    angle = frequencies()[:, None] * (places - doc_start).astype(F32)[None, :]
    cosine, sine = jnp.cos(angle), jnp.sin(angle)
    starts = (doc_start - first_row)[None, :]

    inputs, normed_one, queries, own_kv, sent_kv = project(
        flip, pieces, attn_gain, cosine, sine, weights
    )
    cotangent = after(cotangent, sent_kv)
    upstream_far = tokens_far(cotangent)
    peers = lax.axis_size("gy")
    ahead = [(i, i + 1) for i in range(0, peers, 2)]
    behind = [(i + 1, i) for i in range(0, peers, 2)]
    prior_kv = lax.ppermute(sent_kv, "gy", ahead)
    mixed, lse = attention_forward(starts, queries, prior_kv, own_kv)

    ff_far, ff_other, upstream_far = after((ff_far, ff_near_halves[1], upstream_far), mixed)
    ff_far_halves = gather_x(ff_far)
    ff_own = ff_near_halves[0] if pairs_x else after(ff_near_halves[0], mixed)
    ff_blocks = [
        [ff_own, ff_mate if pairs_x else swap(ff_own, "gy", 1)],
        [ff_other, swap(ff_other, "gy", 1)],
    ]
    ff_blocks[0] += [ff_far_halves[0], swap(ff_far_halves[0], "gy", 1)]
    near, got, far = tokens_near(cotangent, upstream_far)
    upstream = jnp.concatenate([near, got[:block], far, got[block:]], axis=0)
    middle, normed_two = branch(flip, inputs, mlp_gain, mixed, weights)

    made = mlp_chunk(normed_two, upstream, middle, None, ff_blocks[0])
    ff_far_other = after(ff_far_halves[1], made[0])
    ff_blocks[1] += [ff_far_other, swap(ff_far_other, "gy", 1)]
    later = mlp_chunk(normed_two, upstream, made[0], made[1], ff_blocks[1])
    result_keep, result_send, normed_two_grad, later_keep, later_send = later
    result_near, result_sent = to_features(result_keep, swap(result_send, "gy", 1))
    result_far = swap(result_sent, "gy", 2)
    first_got = swap(made[3], "gy", 1)
    later_got = swap(later_send, "gy", 1)

    early = (result_near, result_sent)
    if pairs_x:
        bit = jnp.reshape(bit_z(1), (1,)).astype(jnp.int32)
        first_sums = pair_sums(bit, made[2], first_got)
        low_own, low_own_sent, near_own, far_own = first_sums
        later_sums = pair_sums(bit, later_keep, after(later_got, near_own))
        low_other, low_other_sent, near_other, far_other = later_sums
        early += (*first_sums, *later_sums)
        own_halved = swap(low_own_sent, "dp", 1)
        other_halved = swap(low_other_sent, "dp", 1)
        own_got = swap(far_own, "gy", 2)
        other_got = swap(far_other, "gy", 2)
    mid_grad, mixed_grad, gain_two, out_keep, out_send = branch_back(
        flip, after(normed_two_grad, *early), middle, upstream, mlp_gain, mixed, weights
    )

    def attend_back(mixed_grad, between=lambda dq: ()):
        dq, sent_grad, own_grad = attention_backward(
            starts, cosine, sine, queries, prior_kv, own_kv, mixed, lse, mixed_grad
        )
        prior_grad = lax.ppermute(sent_grad, "gy", behind)
        earlier = between(dq)
        own_grad = after(own_grad, *earlier)
        grads, keep, send = qkv_grad(
            flip, normed_one, dq, own_grad, prior_grad, cosine, sine, out_keep, out_send
        )
        return earlier, grads, keep, swap(send, "gy", 1)

    if not pairs_x:
        _, grads, qkv_keep, qkv_mate = attend_back(mixed_grad)
        ff_both = reduce_x([add(made[2], first_got), add(later_keep, later_got)])
        ff_sum = sum_z(add(ff_both[0], swap(ff_both[1], "gy", 2)))
        paired = add(qkv_keep, qkv_mate)[..., :block]
        sums = [
            reduce_x([paired[0, :, rows], paired[1, :, rows]], -2)
            for rows in (slice(0, QKV_PART), slice(QKV_PART, None))
        ]
        sum_qkv, sum_out = (sum_z(add(both[0], swap(both[1], "gy", 2))) for both in sums)
        result_shard = assemble(result_near, result_far)
        grad_keep, grad_send, gain_one = input_grad(
            flip, grads, inputs, attn_gain, mid_grad, weights
        )
        grad_near, grad_sent = to_features(grad_keep, swap(grad_send, "gy", 1))
        grad_far = swap(grad_sent, "gy", 2)
        gains = sum_all(jnp.stack([reorder(gain_one[:, 0]), reorder(gain_two[:, 0])]))
    else:

        def between(dq):
            own = add(low_own, after(own_halved, dq))
            other = add(low_other, after(other_halved, dq))
            return own, other, own_got, other_got, result_far

        earlier, grads, qkv_keep, qkv_mate = attend_back(mixed_grad, between)
        summed_own, summed_other = earlier[:2]
        low_got = swap(summed_other, "gx", 1)

        high_sent = add(near_other, after(other_got, grads))
        high_near = add(near_own, after(own_got, high_sent))
        qkv_near, qkv_sent = add_pair(qkv_keep, after(qkv_mate, high_near))
        qkv_got = swap(qkv_sent, "gx", 1)
        high_got = swap(after(high_sent, qkv_near), "gx", 1)
        grad_keep, grad_send, gain_one = input_grad(
            flip, after(grads, qkv_near), inputs, attn_gain, mid_grad, weights
        )
        grad_got = swap(grad_send, "gy", 1)
        low_near, low_sent = add_pair(summed_own, after(low_got, grad_keep))
        low_got = swap(low_sent, "gy", 2)
        qkv_near, qkv_sent = add_pair(qkv_near, after(qkv_got, low_near))
        qkv_got = swap(qkv_sent, "gy", 2)
        low = add(low_near, after(low_got, qkv_near))
        low_got = halve_z(low, 2)
        grad_near, grad_sent = to_features(grad_keep, after(grad_got, low))
        grad_far = swap(grad_sent, "gy", 2)
        result_shard = assemble(result_near, after(result_far, grad_near))
        qkv_sum = add(qkv_near, after(qkv_got, result_shard))
        qkv_got = halve_z(qkv_sum, 1)
        high = add(high_near, after(high_got, qkv_sum))
        high_got = halve_z(high, 1)
        gain_one, gain_two = after((gain_one, gain_two), high)
        gains = jnp.stack([reorder(gain_one[:, 0]), reorder(gain_two[:, 0])])
        gains_got = swap(gains, "gx", 1)
        low = add(kept_z(low, 2), after(low_got, gains))
        low_got = swap(low, "dp", 2)
        qkv_sum = add(kept_z(qkv_sum, 1), after(qkv_got, low))
        qkv_got = halve_z(qkv_sum, 2)
        gains = gains + after(gains_got, qkv_sum)
        gains_got = swap(gains, "gy", 1)
        high = add(kept_z(high, 1), after(high_got, gains))
        high_got = halve_z(high, 2)
        gains = gains + after(gains_got, high)
        gains_got = swap(gains, "gy", 2)
        qkv_sum = add(kept_z(qkv_sum, 2), after(qkv_got, gains))
        qkv_got = swap(qkv_sum, "dp", 2)
        low = ordered(low, after(low_got, qkv_sum), bit_z(2), 0)
        low_got = swap(low, "dp", 1)
        high = add(kept_z(high, 2), after(high_got, low))
        high_got = swap(high, "dp", 2)
        gains = gains + after(gains_got, high)
        gains_got = swap(gains, "dp", 1)
        qkv_sum = ordered(qkv_sum, after(qkv_got, gains), bit_z(2), 0)
        qkv_got = swap(qkv_sum, "dp", 1)
        low = ordered(low, after(low_got, qkv_sum), bit_z(1), 0).astype(F32)
        high = ordered(high, after(high_got, low), bit_z(2), 0)
        high_got = swap(high, "dp", 1)
        gains = gains + after(gains_got, high)
        gains_got = swap(gains, "dp", 2)
        qkv_sum = ordered(qkv_sum, after(qkv_got, gains), bit_z(1), 0).astype(F32)
        sum_qkv, sum_out = qkv_sum[:QKV_PART, :block], qkv_sum[QKV_PART:, :block]
        high = ordered(high, after(high_got, qkv_sum), bit_z(1), 0).astype(F32)
        gains = gains + after(gains_got, high)
        ff_sum = jnp.concatenate([low, high[: high.shape[0] - HIGH_PAD]], axis=0)
    return (
        result_shard,
        assemble(grad_near, grad_far),
        sum_qkv.T,
        sum_out,
        ff_sum[:block],
        ff_sum[block : 2 * block],
        ff_sum[2 * block :].T,
        gains[0],
        gains[1],
    )


def solution(mesh):
    placed = (
        P("gy", ("dp", "gx")),
        P(("dp", "gx", "gy")),
        P("gy", ("dp", "gx")),
        P(),
        P(),
        P("gy", "gx"),
        P("gx", "gy"),
        P("gy", "gx"),
        P("gy", "gx"),
        P("gx", "gy"),
    )
    return jax.shard_map(
        on_device,
        mesh=mesh,
        in_specs=placed,
        out_specs=(
            P("gy", ("dp", "gx")),
            P("gy", ("dp", "gx")),
            P("gy", "gx"),
            P("gx", "gy"),
            P("gy", "gx"),
            P("gy", "gx"),
            P("gx", "gy"),
            P(),
            P(),
        ),
        check_vma=False,
    )
```

```python
import functools

import jax
import jax.numpy as jnp
from jax import lax
from jax.experimental import pallas as pl
from jax.experimental.pallas import tpu as pltpu
from jax.sharding import PartitionSpec as P

HEADS = 15
KV_HEADS = 5
GROUP = HEADS // KV_HEADS
HEAD = 64
HALF = HEAD // 2
PRIOR = 512
TILE = 256

EPS = 1e-05
THETA = 100000.0
NEG = -1e30

TINY = pl.CostEstimate(flops=1000, bytes_accessed=1000, transcendentals=0)

BF = jnp.bfloat16
F32 = jnp.float32


def swap(value, axis, by):
    peers = lax.axis_size(axis)
    return lax.ppermute(value, axis, [(i, i ^ by) for i in range(peers)])


def dot(left, right, left_dim, right_dim):
    return lax.dot_general(
        left, right, (((left_dim,), (right_dim,)), ((), ())), preferred_element_type=F32
    )


def add_kernel(left_ref, right_ref, out_ref):
    out_ref[...] = (left_ref[...].astype(F32) + right_ref[...].astype(F32)).astype(BF)


def add(left, right):
    width = left.shape[-1]
    rows = left.size // width
    if left.shape[-2] % 16:
        return (left.astype(F32) + right.astype(F32)).astype(BF)
    step = max(
        size for size in range(16, 513, 16) if rows % size == 0
    )
    spec = pl.BlockSpec((step, width), lambda i: (i, 0))
    return pl.pallas_call(
        add_kernel,
        grid=(rows // step,),
        in_specs=[spec, spec],
        out_specs=spec,
        out_shape=jax.ShapeDtypeStruct((rows, width), BF),
        compiler_params=pltpu.CompilerParams(vmem_limit_bytes=24 * 2**20),
        cost_estimate=TINY,
        name="add",
    )(left.reshape(rows, width), right.reshape(rows, width)).reshape(left.shape)


def add_pair_kernel(left_ref, right_ref, first_ref, second_ref):
    for k, out_ref in enumerate((first_ref, second_ref)):
        out_ref[...] = (left_ref[k].astype(F32) + right_ref[k].astype(F32)).astype(BF)


def add_pair(left, right):
    shape = left.shape[1:]
    width = shape[-1]
    rows = left.size // (2 * width)
    step = max(size for size in range(16, 257, 16) if rows % size == 0)
    spec = pl.BlockSpec((2, step, width), lambda i: (0, i, 0))
    out = pl.BlockSpec((step, width), lambda i: (i, 0))
    first, second = pl.pallas_call(
        add_pair_kernel,
        grid=(rows // step,),
        in_specs=[spec, spec],
        out_specs=[out, out],
        out_shape=[jax.ShapeDtypeStruct((rows, width), BF)] * 2,
        compiler_params=pltpu.CompilerParams(vmem_limit_bytes=24 * 2**20),
        cost_estimate=TINY,
        name="add_pair",
    )(left.reshape(2, rows, width), right.reshape(2, rows, width))
    return first.reshape(shape), second.reshape(shape)


def frequencies():
    return jnp.power(THETA, -jnp.arange(HALF, dtype=F32) / HALF)


def after(value, *earlier):
    return lax.optimization_barrier((value, earlier))[0]


def ordered(mine, theirs, bit, axis):
    return jnp.where(
        bit == 0,
        jnp.concatenate([mine, theirs], axis=axis),
        jnp.concatenate([theirs, mine], axis=axis),
    )


def tokens_far(shard):
    me = lax.axis_index("gy")
    pair = shard.shape[1] // 2
    other = lax.dynamic_slice_in_dim(shard, (1 - me // 2) * pair, pair, 1)
    return swap(other, "gy", 2)


def tokens_near(shard, far):
    me = lax.axis_index("gy")
    rows = far.shape[1] // 2
    own, mate = (me % 2) * rows, (1 - me % 2) * rows
    base = (me // 2) * 2 * rows
    sent = jnp.concatenate(
        [
            lax.dynamic_slice_in_dim(shard, base + mate, rows, 1),
            lax.dynamic_slice_in_dim(far, mate, rows, 1),
        ],
        axis=0,
    )
    got = swap(sent, "gy", 1)
    return (
        lax.dynamic_slice_in_dim(shard, base + own, rows, 1),
        got,
        lax.dynamic_slice_in_dim(far, own, rows, 1),
    )


def to_features(kept, got):
    me = lax.axis_index("gy")
    block = kept.shape[0] // 2
    near = ordered(kept[:block], got[:block], me % 2, 1)
    far = ordered(kept[block:], got[block:], me % 2, 1)
    return near, far


def assemble(near, far):
    return ordered(near, far, lax.axis_index("gy") // 2, 1)


def reorder(vector):
    me = lax.axis_index("gy")
    block = vector.shape[0] // 4
    return jnp.concatenate(
        [lax.dynamic_slice_in_dim(vector, (me ^ by) * block, block, 0) for by in range(4)]
    )


def gather_x(block):
    if lax.axis_size("gx") == 2:
        return [block, swap(block, "gx", 1)]
    whole = lax.all_gather(block, "gx", axis=1, tiled=True)
    half = whole.shape[1] // 2
    return [whole[:, :half], whole[:, half:]]


def split_x(whole):
    half = whole.shape[-1] // 2
    if lax.axis_size("gx") == 2:
        me = lax.axis_index("gx")
        return [
            lax.dynamic_slice_in_dim(whole, me * half, half, whole.ndim - 1),
            lax.dynamic_slice_in_dim(whole, (1 - me) * half, half, whole.ndim - 1),
        ]
    return [whole[..., :half], whole[..., half:]]


def reduce_x(chunks, dim=-1):
    if lax.axis_size("gx") == 2:
        return add(chunks[0], swap(chunks[1], "gx", 1))
    dim = chunks[0].ndim + dim
    return lax.psum_scatter(
        jnp.concatenate(chunks, axis=dim), "gx", scatter_dimension=dim, tiled=True
    )


def sum_z(value):
    peers = lax.axis_size("dp")
    if peers != 4:
        return lax.psum(value.astype(F32), "dp")
    me = lax.axis_index("dp")
    inner = add(value, lax.ppermute(value, "dp", [(0, 1), (3, 2)]))
    total = add(inner, lax.ppermute(inner, "dp", [(1, 2), (2, 1)]))
    outer = lax.ppermute(total, "dp", [(1, 0), (2, 3)])
    return jnp.where((me == 0) | (me == 3), outer, total).astype(F32)


LOW = 448
HIGH_PAD = 48


def pair_sums_kernel(bit_ref, keep_ref, got_ref, low_ref, low_sent_ref, near_ref, far_ref):
    half = LOW // 2

    def total(k, rows):
        return (keep_ref[k, rows, :].astype(F32) + got_ref[k, rows, :].astype(F32)).astype(BF)

    for k, high_ref in enumerate((near_ref, far_ref)):
        for target, bit in ((low_ref, bit_ref[0]), (low_sent_ref, 1 - bit_ref[0])):
            target[k] = total(k, pl.ds(pl.multiple_of(bit * half, 16), half))
        size = high_ref.shape[0] - HIGH_PAD
        high_ref[:size, :] = total(k, slice(LOW, LOW + size))
        high_ref[size:, :] = jnp.zeros((HIGH_PAD, high_ref.shape[1]), BF)


def pair_sums(bit, keep, got):
    rows, width = keep.shape[1:]
    high = rows - LOW + HIGH_PAD
    tile = 256

    def block(*dims):
        return pl.BlockSpec((*dims, tile), lambda i: (*(0 for _ in dims), i))

    return pl.pallas_call(
        pair_sums_kernel,
        grid=(width // tile,),
        in_specs=[SMEM, block(2, rows), block(2, rows)],
        out_specs=[block(2, LOW // 2), block(2, LOW // 2), block(high), block(high)],
        out_shape=[
            jax.ShapeDtypeStruct((2, LOW // 2, width), BF),
            jax.ShapeDtypeStruct((2, LOW // 2, width), BF),
            jax.ShapeDtypeStruct((high, width), BF),
            jax.ShapeDtypeStruct((high, width), BF),
        ],
        compiler_params=pltpu.CompilerParams(vmem_limit_bytes=32 * 2**20),
        cost_estimate=TINY,
        name="pair_sums",
    )(bit, keep, got)


def bit_z(by):
    return (lax.axis_index("dp") // by) % 2


def kept_z(value, by):
    half = value.shape[0] // 2
    return lax.dynamic_slice_in_dim(value, bit_z(by) * half, half, 0)


def halve_z(value, by):
    half = value.shape[0] // 2
    return swap(lax.dynamic_slice_in_dim(value, (1 - bit_z(by)) * half, half, 0), "dp", by)


def sum_all(value):
    for axis in ("gy", "gx", "dp"):
        by = 1
        while by < lax.axis_size(axis):
            value = value + swap(value, axis, by)
            by *= 2
    return value


RANGES = ((0, 768), (0, 1024), (512, 1280), (512, 1536))


def fill_bias(starts_ref, bias_ref):
    offset = 0
    for tile, (low, high) in enumerate(RANGES):
        size = high - low
        place = lax.broadcasted_iota(jnp.int32, (size, TILE), 0) + (low - PRIOR)
        query = lax.broadcasted_iota(jnp.int32, (size, TILE), 1) + tile * TILE
        start = starts_ref[:, tile * TILE : (tile + 1) * TILE]
        allowed = (place >= start) & (place <= query)
        bias_ref[offset : offset + size, :] = jnp.where(allowed, 0.0, NEG)
        offset += size


BIAS_ROWS = sum(high - low for low, high in RANGES)


def turned(prior, own, out_ref):
    out_ref[:PRIOR, :] = prior.astype(F32).T.astype(BF)
    out_ref[PRIOR:, :] = own.astype(F32).T.astype(BF)


def forward_kernel(
    starts_ref, q_ref, prior_ref, own_ref, mixed_ref, lse_ref, keys, values, bias
):
    @pl.when(pl.program_id(0) == 0)
    def _():
        fill_bias(starts_ref, bias)

    turned(prior_ref[0, :HEAD, :], own_ref[0, :HEAD, :], keys)
    values[:, :PRIOR] = prior_ref[0, HEAD:, :]
    values[:, PRIOR:] = own_ref[0, HEAD:, :]
    offset = 0
    for tile, (low, high) in enumerate(RANGES):
        size = high - low
        lanes = slice(tile * TILE, (tile + 1) * TILE)
        for head in range(GROUP):
            rows = slice(head * HEAD, (head + 1) * HEAD)
            scores = dot(keys[low:high, :], q_ref[rows, lanes], 1, 0)
            scores = scores + bias[offset : offset + size, :]
            top = jnp.max(scores, axis=0, keepdims=True)
            weights = jnp.exp(scores - top)
            total = jnp.sum(weights, axis=0, keepdims=True)
            out = dot(values[:, low:high], weights.astype(BF), 1, 0)
            mixed_ref[rows, lanes] = (out / total).astype(BF)
            lse_ref[0, head : head + 1, lanes] = top + jnp.log(total)
        offset += size


def attention_forward(starts, queries, prior_kv, own_kv):
    count = queries.shape[1]
    wide = GROUP * HEAD
    prior = pl.BlockSpec((1, 2 * HEAD, PRIOR), lambda g: (g, 0, 0))
    own = pl.BlockSpec((1, 2 * HEAD, count), lambda g: (g, 0, 0))
    return pl.pallas_call(
        forward_kernel,
        grid=(KV_HEADS,),
        in_specs=[
            pl.BlockSpec((1, count), lambda g: (0, 0)),
            pl.BlockSpec((wide, count), lambda g: (g, 0)),
            prior,
            own,
        ],
        out_specs=[
            pl.BlockSpec((wide, count), lambda g: (g, 0)),
            pl.BlockSpec((1, 8, count), lambda g: (g, 0, 0)),
        ],
        out_shape=[
            jax.ShapeDtypeStruct((HEADS * HEAD, count), BF),
            jax.ShapeDtypeStruct((KV_HEADS, 8, count), F32),
        ],
        scratch_shapes=[
            pltpu.VMEM((PRIOR + count, HEAD), BF),
            pltpu.VMEM((HEAD, PRIOR + count), BF),
            pltpu.VMEM((BIAS_ROWS, TILE), F32),
        ],
        compiler_params=pltpu.CompilerParams(vmem_limit_bytes=40 * 2**20),
        cost_estimate=TINY,
        name="attend_forward",
    )(starts, queries, prior_kv, own_kv)


def backward_kernel(
    starts_ref,
    cos_ref,
    sin_ref,
    q_ref,
    prior_ref,
    own_ref,
    mixed_ref,
    lse_ref,
    grad_ref,
    dq_ref,
    dprior_ref,
    down_ref,
    keys,
    turned_keys,
    turned_values,
    dk,
    dv,
    bias,
):
    @pl.when(pl.program_id(0) == 0)
    def _():
        fill_bias(starts_ref, bias)

    turned(prior_ref[0, :HEAD, :], own_ref[0, :HEAD, :], turned_keys)
    turned(prior_ref[0, HEAD:, :], own_ref[0, HEAD:, :], turned_values)
    keys[:, :PRIOR] = prior_ref[0, :HEAD, :]
    keys[:, PRIOR:] = own_ref[0, :HEAD, :]
    dk[...] = jnp.zeros_like(dk)
    dv[...] = jnp.zeros_like(dv)
    offset = 0
    for tile, (low, high) in enumerate(RANGES):
        size = high - low
        lanes = slice(tile * TILE, (tile + 1) * TILE)
        for head in range(GROUP):
            rows = slice(head * HEAD, (head + 1) * HEAD)
            query = q_ref[rows, lanes]
            grad = grad_ref[rows, lanes]
            inner = jnp.sum(
                grad.astype(F32) * mixed_ref[rows, lanes].astype(F32), axis=0, keepdims=True
            )
            lse = lse_ref[0, head : head + 1, lanes]
            scores = dot(turned_keys[low:high, :], query, 1, 0)
            weights = jnp.exp(scores + bias[offset : offset + size, :] - lse)
            prob_grad = dot(turned_values[low:high, :], grad, 1, 0)
            score_grad = (weights * (prob_grad - inner)).astype(BF)
            weights = weights.astype(BF)
            dv[low:high, :] += dot(weights, grad, 1, 1)
            dk[low:high, :] += dot(score_grad, query, 1, 1)
            dq = dot(keys[:, low:high], score_grad, 1, 0) * HEAD ** (-0.5)
            cosine, sine = cos_ref[:, lanes], sin_ref[:, lanes]
            front, back = dq[:HALF], dq[HALF:]
            base = head * HEAD
            dq_ref[base : base + HALF, lanes] = (front * cosine + back * sine).astype(BF)
            dq_ref[base + HALF : base + HEAD, lanes] = (back * cosine - front * sine).astype(BF)
        offset += size
    dprior_ref[0, :HEAD, :] = dk[:PRIOR, :].T.astype(BF)
    dprior_ref[0, HEAD:, :] = dv[:PRIOR, :].T.astype(BF)
    down_ref[0, :HEAD, :] = dk[PRIOR:, :].T
    down_ref[0, HEAD:, :] = dv[PRIOR:, :].T


def attention_backward(
    starts, cosine, sine, queries, prior_kv, own_kv, mixed, lse, grads
):
    count = queries.shape[1]
    wide = GROUP * HEAD
    prior = pl.BlockSpec((1, 2 * HEAD, PRIOR), lambda g: (g, 0, 0))
    own = pl.BlockSpec((1, 2 * HEAD, count), lambda g: (g, 0, 0))
    heads = pl.BlockSpec((wide, count), lambda g: (g, 0))
    table = pl.BlockSpec((HALF, count), lambda g: (0, 0))
    return pl.pallas_call(
        backward_kernel,
        grid=(KV_HEADS,),
        in_specs=[
            pl.BlockSpec((1, count), lambda g: (0, 0)),
            table,
            table,
            heads,
            prior,
            own,
            heads,
            pl.BlockSpec((1, 8, count), lambda g: (g, 0, 0)),
            heads,
        ],
        out_specs=[heads, prior, own],
        out_shape=[
            jax.ShapeDtypeStruct((HEADS * HEAD, count), BF),
            jax.ShapeDtypeStruct((KV_HEADS, 2 * HEAD, PRIOR), BF),
            jax.ShapeDtypeStruct((KV_HEADS, 2 * HEAD, count), F32),
        ],
        scratch_shapes=[
            pltpu.VMEM((HEAD, PRIOR + count), BF),
            pltpu.VMEM((PRIOR + count, HEAD), BF),
            pltpu.VMEM((PRIOR + count, HEAD), BF),
            pltpu.VMEM((PRIOR + count, HEAD), F32),
            pltpu.VMEM((PRIOR + count, HEAD), F32),
            pltpu.VMEM((BIAS_ROWS, TILE), F32),
        ],
        compiler_params=pltpu.CompilerParams(vmem_limit_bytes=44 * 2**20),
        cost_estimate=TINY,
        name="attend_backward",
    )(starts, cosine, sine, queries, prior_kv, own_kv, mixed, lse, grads)


def mlp_kernel(first, *refs):
    normed_ref, up_ref, base_ref = refs[:3]
    refs = refs[3:]
    if not first:
        grad_in_ref, refs = refs[0], refs[1:]
    blocks, refs = refs[:4], refs[4:]
    out_refs, refs = (refs[:1], refs[1:]) if first else (refs[:2], refs[2:])
    grad_out_ref, keep_ref, send_ref, total_ref, grad_total_ref = refs
    step = pl.program_id(0)
    last = pl.num_programs(0) - 1

    @pl.when(step == 0)
    def _():
        total_ref[...] = base_ref[...]
        if first:
            grad_total_ref[...] = jnp.zeros_like(grad_total_ref)
        else:
            grad_total_ref[...] = grad_in_ref[...]

    normed = normed_ref[...]
    upstream = up_ref[...]
    block = normed.shape[0] // 4
    w_gate = jnp.concatenate([ref[:block] for ref in blocks], axis=0)
    w_up = jnp.concatenate([ref[block : 2 * block] for ref in blocks], axis=0)
    w_down = jnp.concatenate([ref[2 * block :] for ref in blocks], axis=0)
    gate = dot(w_gate, normed, 0, 0)
    up = dot(w_up, normed, 0, 0)
    hidden_grad = dot(w_down, upstream, 0, 0)
    sigmoid = 1.0 / (1.0 + jnp.exp(-gate))
    silu = gate * sigmoid
    hidden = (silu * up).astype(BF)
    gate_grad = (hidden_grad * up * (sigmoid * (1.0 + gate * (1.0 - sigmoid)))).astype(BF)
    up_grad = (hidden_grad * silu).astype(BF)
    total_ref[...] += dot(w_down, hidden, 1, 0)
    grad_total_ref[...] += dot(w_gate, gate_grad, 1, 0) + dot(w_up, up_grad, 1, 0)
    for place, (left, right) in enumerate(
        ((normed, gate_grad), (normed, up_grad), (upstream, hidden))
    ):
        made = dot(left, right, 1, 1).astype(BF)
        rows = slice(place * block, (place + 1) * block)
        keep_ref[0, rows, :] = made[:block]
        send_ref[0, rows, :] = made[block : 2 * block]
        keep_ref[1, rows, :] = made[2 * block : 3 * block]
        send_ref[1, rows, :] = made[3 * block :]

    @pl.when(step == last)
    def _():
        if first:
            out_refs[0][...] = total_ref[...]
        else:
            for number in range(4):
                rows = slice((number // 2) * block, (number // 2 + 1) * block)
                source = slice(number * block, (number + 1) * block)
                out_refs[number % 2][rows, :] = total_ref[source, :].astype(BF)
        grad_out_ref[...] = grad_total_ref[...]


def mlp_chunk(normed, upstream, base, grad_in, blocks):
    first = grad_in is None
    width, count = normed.shape
    rows, size = blocks[0].shape
    tile = TILE
    whole = pl.BlockSpec((width, count), lambda i: (0, 0), pipeline_mode=pl.Buffered(1))
    half = pl.BlockSpec((width // 2, count), lambda i: (0, 0), pipeline_mode=pl.Buffered(1))
    across = pl.BlockSpec((rows, tile), lambda i: (0, i))
    made = pl.BlockSpec((2, rows, tile), lambda i: (0, 0, i))
    operands = [normed, upstream, base] + ([] if first else [grad_in])
    return pl.pallas_call(
        functools.partial(mlp_kernel, first),
        grid=(size // tile,),
        in_specs=[whole] * len(operands) + [across] * 4,
        out_specs=([whole] if first else [half, half]) + [whole, made, made],
        out_shape=(
            [jax.ShapeDtypeStruct((width, count), F32)]
            if first
            else [jax.ShapeDtypeStruct((width // 2, count), BF)] * 2
        )
        + [
            jax.ShapeDtypeStruct((width, count), F32),
            jax.ShapeDtypeStruct((2, rows, size), BF),
            jax.ShapeDtypeStruct((2, rows, size), BF),
        ],
        scratch_shapes=[pltpu.VMEM((width, count), F32), pltpu.VMEM((width, count), F32)],
        compiler_params=pltpu.CompilerParams(vmem_limit_bytes=56 * 2**20),
        cost_estimate=TINY,
        name="feed_forward",
    )(*operands, *blocks)


VMEM = pl.BlockSpec(memory_space=pltpu.VMEM)
SMEM = pl.BlockSpec(memory_space=pltpu.SMEM)
Q_WIDTH = HEADS * HEAD
KV_WIDTH = KV_HEADS * HEAD
QKV_WIDTH = Q_WIDTH + 2 * KV_WIDTH
QKV_PART = QKV_WIDTH // 2
OUT_PART = Q_WIDTH // 2
WIDE = 256


def place_of(flip_ref, half, size):
    return pl.ds(pl.multiple_of((flip_ref[0] ^ half) * size, 16), size)


def stacked(refs, columns):
    return jnp.concatenate([ref[:, columns] for ref in refs], axis=0)


QKV_COLUMNS = slice(0, QKV_PART)
OUT_COLUMNS = slice(QKV_PART, QKV_PART + OUT_PART)


def norm_scale_of(values):
    return lax.rsqrt(jnp.mean(values * values, axis=0, keepdims=True) + EPS)


def norm_back(values, scale, gain, gradient):
    weighted = gradient * gain
    inner = jnp.mean(weighted * values, axis=0, keepdims=True)
    values_grad = scale * weighted - values * (scale * scale * scale) * inner
    return (values_grad, jnp.sum(gradient * values * scale, axis=1, keepdims=True))


def project_kernel(flip_ref, near_ref, got_ref, far_ref, gain_ref, cos_ref, sin_ref, *refs):
    weights = refs[:8]
    x_ref, normed_ref, q_ref, own_ref, prior_ref, made = refs[8:]
    block = near_ref.shape[0]
    x_ref[:block, :] = near_ref[...]
    x_ref[block : 2 * block, :] = got_ref[:block, :]
    x_ref[2 * block : 3 * block, :] = far_ref[...]
    x_ref[3 * block :, :] = got_ref[block:, :]
    x = x_ref[...].astype(F32)
    normed = (x * norm_scale_of(x) * gain_ref[...]).astype(BF)
    normed_ref[...] = normed
    for half in range(2):
        weight = stacked(weights[4 * half : 4 * half + 4], QKV_COLUMNS)
        made[place_of(flip_ref, half, QKV_PART), :] = dot(weight, normed, 0, 0).astype(BF)
    cosine, sine = cos_ref[...], sin_ref[...]
    count = cosine.shape[1]

    def rotated(base, scale):
        front = made[base : base + HALF, :].astype(F32)
        back = made[base + HALF : base + HEAD, :].astype(F32)
        return (
            ((front * cosine - back * sine) * scale).astype(BF),
            ((back * cosine + front * sine) * scale).astype(BF),
        )

    for head in range(HEADS):
        base = head * HEAD
        front, back = rotated(base, HEAD ** (-0.5))
        q_ref[base : base + HALF, :] = front
        q_ref[base + HALF : base + HEAD, :] = back
    for head in range(KV_HEADS):
        front, back = rotated(Q_WIDTH + head * HEAD, 1.0)
        base = Q_WIDTH + KV_WIDTH + head * HEAD
        value = made[base : base + HEAD, :]
        own_ref[head, :HALF, :] = front
        own_ref[head, HALF:HEAD, :] = back
        own_ref[head, HEAD:, :] = value
        prior_ref[head, :HALF, :] = front[:, count - PRIOR :]
        prior_ref[head, HALF:HEAD, :] = back[:, count - PRIOR :]
        prior_ref[head, HEAD:, :] = value[:, count - PRIOR :]


def call_whole(kernel, name, ins, outs, scratch=()):
    return pl.pallas_call(
        kernel,
        in_specs=[SMEM] + [VMEM] * (len(ins) - 1),
        out_specs=[VMEM] * len(outs),
        out_shape=[jax.ShapeDtypeStruct(shape, kind) for shape, kind in outs],
        scratch_shapes=list(scratch),
        compiler_params=pltpu.CompilerParams(vmem_limit_bytes=56 * 2**20),
        cost_estimate=TINY,
        name=name,
    )(*ins)


def project(flip, pieces, gain, cosine, sine, weights):
    block, count = pieces[0].shape
    width = 4 * block
    return call_whole(
        project_kernel,
        "project",
        (flip, *pieces, gain, cosine, sine, *weights),
        (
            ((width, count), BF),
            ((width, count), BF),
            ((Q_WIDTH, count), BF),
            ((KV_HEADS, 2 * HEAD, count), BF),
            ((KV_HEADS, 2 * HEAD, PRIOR), BF),
        ),
        (pltpu.VMEM((QKV_WIDTH, count), BF),),
    )


def branch_kernel(flip_ref, x_ref, gain_ref, mixed_ref, *refs):
    weights = refs[:8]
    middle_ref, normed_ref = refs[8:]
    middle = x_ref[...].astype(F32)
    for half in range(2):
        weight = stacked(weights[4 * half : 4 * half + 4], OUT_COLUMNS)
        middle = middle + dot(weight, mixed_ref[place_of(flip_ref, half, OUT_PART), :], 1, 0)
    middle_ref[...] = middle
    normed_ref[...] = (middle * norm_scale_of(middle) * gain_ref[...]).astype(BF)


def branch(flip, inputs, gain, mixed, weights):
    shape = inputs.shape
    return call_whole(
        branch_kernel,
        "branch",
        (flip, inputs, gain, mixed, *weights),
        ((shape, F32), (shape, BF)),
    )


def branch_back_kernel(flip_ref, grad_ref, middle_ref, up_ref, gain_ref, mixed_ref, *refs):
    weights = refs[:8]
    mid_grad_ref, mixed_grad_ref, gain_grad_ref, keep_ref, send_ref = refs[8:]
    middle = middle_ref[...]
    mid_grad, gain_grad = norm_back(
        middle, norm_scale_of(middle), gain_ref[...], grad_ref[...]
    )
    gain_grad_ref[...] = gain_grad
    mid_grad = mid_grad + up_ref[...].astype(F32)
    mid_grad_ref[...] = mid_grad
    branch_grad = mid_grad.astype(BF)
    block = branch_grad.shape[0] // 4
    for half in range(2):
        place = place_of(flip_ref, half, OUT_PART)
        weight = stacked(weights[4 * half : 4 * half + 4], OUT_COLUMNS)
        mixed_grad_ref[place, :] = dot(weight, branch_grad, 0, 0).astype(BF)
        heads = mixed_ref[place, :]
        for number in range(4):
            rows = branch_grad[number * block : (number + 1) * block]
            target = send_ref if number % 2 else keep_ref
            target[half, number // 2] = dot(heads, rows, 1, 1).astype(BF)


def branch_back(flip, grad, middle, upstream, gain, mixed, weights):
    width, count = middle.shape
    parts = (2, 2, OUT_PART, width // 4)
    return call_whole(
        branch_back_kernel,
        "branch_back",
        (flip, grad, middle, upstream, gain, mixed, *weights),
        (
            ((width, count), F32),
            ((Q_WIDTH, count), BF),
            ((width, 1), F32),
            (parts, BF),
            (parts, BF),
        ),
    )


def qkv_grad_kernel(
    flip_ref,
    normed_ref,
    dq_ref,
    own_ref,
    prior_ref,
    cos_ref,
    sin_ref,
    out_keep_ref,
    out_send_ref,
    made_ref,
    keep_ref,
    send_ref,
):
    block = out_keep_ref.shape[3]
    for target, source in ((keep_ref, out_keep_ref), (send_ref, out_send_ref)):
        target[:, :, :, block:] = jnp.zeros((*target.shape[:3], WIDE - block), BF)
        target[:, :, QKV_PART:, :block] = source[...]
    made_ref[:Q_WIDTH, :] = dq_ref[...]
    count = own_ref.shape[2]
    cosine, sine = cos_ref[...], sin_ref[...]
    for head in range(KV_HEADS):
        sent = prior_ref[head].astype(F32)
        both = jnp.concatenate(
            [own_ref[head, :, : count - PRIOR], own_ref[head, :, count - PRIOR :] + sent], axis=1
        )
        front, back = both[:HALF], both[HALF:HEAD]
        base = Q_WIDTH + head * HEAD
        made_ref[base : base + HALF, :] = (front * cosine + back * sine).astype(BF)
        made_ref[base + HALF : base + HEAD, :] = (back * cosine - front * sine).astype(BF)
        base += KV_WIDTH
        made_ref[base : base + HEAD, :] = both[HEAD:].astype(BF)
    normed = normed_ref[...]
    block = normed.shape[0] // 4
    for half in range(2):
        grads = made_ref[place_of(flip_ref, half, QKV_PART), :]
        for number in range(4):
            rows = normed[number * block : (number + 1) * block]
            target = send_ref if number % 2 else keep_ref
            target[half, number // 2, :QKV_PART, :block] = dot(grads, rows, 1, 1).astype(BF)


def qkv_grad(flip, normed, dq, own, prior, cosine, sine, out_keep, out_send):
    width, count = normed.shape
    parts = (2, 2, QKV_PART + OUT_PART, WIDE)
    return call_whole(
        qkv_grad_kernel,
        "qkv_grad",
        (flip, normed, dq, own, prior, cosine, sine, out_keep, out_send),
        (((QKV_WIDTH, count), BF), (parts, BF), (parts, BF)),
    )


def input_grad_kernel(flip_ref, grads_ref, x_ref, gain_ref, mid_grad_ref, *refs):
    weights = refs[:8]
    keep_ref, send_ref, gain_grad_ref = refs[8:]
    total = jnp.zeros(x_ref.shape, F32)
    for half in range(2):
        weight = stacked(weights[4 * half : 4 * half + 4], QKV_COLUMNS)
        total = total + dot(weight, grads_ref[place_of(flip_ref, half, QKV_PART), :], 1, 0)
    x = x_ref[...].astype(F32)
    grad, gain_grad = norm_back(x, norm_scale_of(x), gain_ref[...], total)
    gain_grad_ref[...] = gain_grad
    grad = (grad + mid_grad_ref[...]).astype(BF)
    block = grad.shape[0] // 4
    for number in range(4):
        target = send_ref if number % 2 else keep_ref
        rows = slice((number // 2) * block, (number // 2 + 1) * block)
        target[rows, :] = grad[number * block : (number + 1) * block]


def input_grad(flip, grads, inputs, gain, mid_grad, weights):
    width, count = inputs.shape
    return call_whole(
        input_grad_kernel,
        "input_grad",
        (flip, grads, inputs, gain, mid_grad, *weights),
        (((width // 2, count), BF), ((width // 2, count), BF), ((width, 1), F32)),
    )


def attention_halves(shard, cut):
    if lax.axis_size("gx") == 2:
        return [shard, swap(shard, "gx", 1)]
    peers = lax.axis_size("gx")
    block, width = shard.shape
    whole = lax.all_gather(shard, "gx", axis=1, tiled=True)
    whole = whole.reshape(block, 2, peers // 2, width)
    return [
        jnp.concatenate(
            [
                whole[:, c, :, :cut].reshape(block, peers // 2 * cut),
                whole[:, c, :, cut:].reshape(block, peers // 2 * (width - cut)),
            ],
            axis=1,
        )
        for c in range(2)
    ]


def on_device(
    tokens, doc_start, cotangent, attn_gain, mlp_gain, w_qkv, w_out, w_gate, w_up, w_down
):
    count = doc_start.shape[0]
    block = w_qkv.shape[0]
    pairs_x = lax.axis_size("gx") == 2
    flip = lax.axis_index("gx") if pairs_x else jnp.int32(0)
    flip = jnp.reshape(flip, (1,)).astype(jnp.int32)

    shard = jnp.concatenate([w_qkv, w_out.T], axis=1)
    shard_far = swap(shard, "gy", 2)
    mate = swap(shard, "gy", 1)
    near_halves = attention_halves(shard, w_qkv.shape[1])
    inputs_far = tokens_far(after(tokens, shard_far, *near_halves))
    far_halves = attention_halves(shard_far, w_qkv.shape[1])
    weights = []
    for half, (near, far) in enumerate(zip(near_halves, far_halves)):
        near_mate = mate if pairs_x and half == 0 else swap(near, "gy", 1)
        weights += [near, near_mate, far, swap(far, "gy", 1)]
    pieces = tokens_near(tokens, inputs_far)

    ff_shard = jnp.concatenate([w_gate, w_up, w_down.T], axis=0)
    ff_shard = after(ff_shard, inputs_far, *near_halves, *far_halves)
    ff_far = swap(ff_shard, "gy", 2)
    ff_near_halves = gather_x(ff_shard)
    ff_mate = swap(ff_shard, "gy", 1)

    attn_gain = reorder(attn_gain)[:, None]
    mlp_gain = reorder(mlp_gain)[:, None]

    first_row = lax.axis_index(("dp", "gx", "gy")) * count
    places = first_row + jnp.arange(count, dtype=jnp.int32)
    angle = frequencies()[:, None] * (places - doc_start).astype(F32)[None, :]
    cosine, sine = jnp.cos(angle), jnp.sin(angle)
    starts = (doc_start - first_row)[None, :]

    inputs, normed_one, queries, own_kv, sent_kv = project(
        flip, pieces, attn_gain, cosine, sine, weights
    )
    cotangent = after(cotangent, sent_kv)
    upstream_far = tokens_far(cotangent)
    peers = lax.axis_size("gy")
    ahead = [(i, i + 1) for i in range(0, peers, 2)]
    behind = [(i + 1, i) for i in range(0, peers, 2)]
    prior_kv = lax.ppermute(sent_kv, "gy", ahead)
    mixed, lse = attention_forward(starts, queries, prior_kv, own_kv)

    ff_far, ff_other, upstream_far = after((ff_far, ff_near_halves[1], upstream_far), mixed)
    ff_far_halves = gather_x(ff_far)
    ff_own = ff_near_halves[0] if pairs_x else after(ff_near_halves[0], mixed)
    ff_blocks = [
        [ff_own, ff_mate if pairs_x else swap(ff_own, "gy", 1)],
        [ff_other, swap(ff_other, "gy", 1)],
    ]
    ff_blocks[0] += [ff_far_halves[0], swap(ff_far_halves[0], "gy", 1)]
    near, got, far = tokens_near(cotangent, upstream_far)
    upstream = jnp.concatenate([near, got[:block], far, got[block:]], axis=0)
    middle, normed_two = branch(flip, inputs, mlp_gain, mixed, weights)

    made = mlp_chunk(normed_two, upstream, middle, None, ff_blocks[0])
    ff_far_other = after(ff_far_halves[1], made[0])
    ff_blocks[1] += [ff_far_other, swap(ff_far_other, "gy", 1)]
    later = mlp_chunk(normed_two, upstream, made[0], made[1], ff_blocks[1])
    result_keep, result_send, normed_two_grad, later_keep, later_send = later
    result_near, result_sent = to_features(result_keep, swap(result_send, "gy", 1))
    result_far = swap(result_sent, "gy", 2)
    first_got = swap(made[3], "gy", 1)
    later_got = swap(later_send, "gy", 1)

    early = (result_near, result_sent)
    if pairs_x:
        bit = jnp.reshape(bit_z(1), (1,)).astype(jnp.int32)
        first_sums = pair_sums(bit, made[2], first_got)
        low_own, low_own_sent, near_own, far_own = first_sums
        later_sums = pair_sums(bit, later_keep, after(later_got, near_own))
        low_other, low_other_sent, near_other, far_other = later_sums
        early += (*first_sums, *later_sums)
        own_halved = swap(low_own_sent, "dp", 1)
        other_halved = swap(low_other_sent, "dp", 1)
        own_got = swap(far_own, "gy", 2)
        other_got = swap(far_other, "gy", 2)
    mid_grad, mixed_grad, gain_two, out_keep, out_send = branch_back(
        flip, after(normed_two_grad, *early), middle, upstream, mlp_gain, mixed, weights
    )

    def attend_back(mixed_grad, between=lambda dq: ()):
        dq, sent_grad, own_grad = attention_backward(
            starts, cosine, sine, queries, prior_kv, own_kv, mixed, lse, mixed_grad
        )
        prior_grad = lax.ppermute(sent_grad, "gy", behind)
        earlier = between(dq)
        own_grad = after(own_grad, *earlier)
        grads, keep, send = qkv_grad(
            flip, normed_one, dq, own_grad, prior_grad, cosine, sine, out_keep, out_send
        )
        return earlier, grads, keep, swap(send, "gy", 1)

    if not pairs_x:
        _, grads, qkv_keep, qkv_mate = attend_back(mixed_grad)
        ff_both = reduce_x([add(made[2], first_got), add(later_keep, later_got)])
        ff_sum = sum_z(add(ff_both[0], swap(ff_both[1], "gy", 2)))
        paired = add(qkv_keep, qkv_mate)[..., :block]
        sums = [
            reduce_x([paired[0, :, rows], paired[1, :, rows]], -2)
            for rows in (slice(0, QKV_PART), slice(QKV_PART, None))
        ]
        sum_qkv, sum_out = (sum_z(add(both[0], swap(both[1], "gy", 2))) for both in sums)
        result_shard = assemble(result_near, result_far)
        grad_keep, grad_send, gain_one = input_grad(
            flip, grads, inputs, attn_gain, mid_grad, weights
        )
        grad_near, grad_sent = to_features(grad_keep, swap(grad_send, "gy", 1))
        grad_far = swap(grad_sent, "gy", 2)
        gains = sum_all(jnp.stack([reorder(gain_one[:, 0]), reorder(gain_two[:, 0])]))
    else:

        def between(dq):
            own = add_pair(first_sums[0], after(own_halved, dq))
            other = add_pair(later_sums[0], after(other_halved, dq))
            return *own, *other, own_got, other_got, result_far

        earlier, grads, qkv_keep, qkv_mate = attend_back(mixed_grad, between)
        low_near, low_far, low_other, low_other_far = earlier[:4]
        low_got = swap(low_far, "gy", 2)
        low_other_got = swap(low_other_far, "gy", 2)

        high_sent = add(near_other, after(other_got, grads))
        high_near = add(near_own, after(own_got, high_sent))
        qkv_near, qkv_sent = add_pair(qkv_keep, after(qkv_mate, high_near))
        qkv_got = swap(qkv_sent, "gx", 1)
        high_got = swap(after(high_sent, qkv_near), "gx", 1)
        grad_keep, grad_send, gain_one = input_grad(
            flip, after(grads, qkv_near), inputs, attn_gain, mid_grad, weights
        )
        grad_got = swap(grad_send, "gy", 1)
        low_other = add(low_other, after(low_other_got, grad_keep))
        low_near = add(low_near, after(low_got, low_other))
        low_got = swap(low_other, "gx", 1)
        qkv_near, qkv_sent = add_pair(qkv_near, after(qkv_got, low_near))
        qkv_got = swap(qkv_sent, "gy", 2)
        low = add(low_near, after(low_got, qkv_near))
        low_got = halve_z(low, 2)
        grad_near, grad_sent = to_features(grad_keep, after(grad_got, low))
        grad_far = swap(grad_sent, "gy", 2)
        result_shard = assemble(result_near, after(result_far, grad_near))
        qkv_sum = add(qkv_near, after(qkv_got, result_shard))
        qkv_got = halve_z(qkv_sum, 1)
        high = add(high_near, after(high_got, qkv_sum))
        high_got = halve_z(high, 1)
        gain_one, gain_two = after((gain_one, gain_two), high)
        gains = jnp.stack([reorder(gain_one[:, 0]), reorder(gain_two[:, 0])])
        gains_got = swap(gains, "gx", 1)
        low = add(kept_z(low, 2), after(low_got, gains))
        low_got = swap(low, "dp", 2)
        qkv_sum = add(kept_z(qkv_sum, 1), after(qkv_got, low))
        qkv_got = halve_z(qkv_sum, 2)
        gains = gains + after(gains_got, qkv_sum)
        gains_got = swap(gains, "gy", 1)
        high = add(kept_z(high, 1), after(high_got, gains))
        high_got = halve_z(high, 2)
        gains = gains + after(gains_got, high)
        gains_got = swap(gains, "gy", 2)
        qkv_sum = add(kept_z(qkv_sum, 2), after(qkv_got, gains))
        qkv_got = swap(qkv_sum, "dp", 2)
        low = ordered(low, after(low_got, qkv_sum), bit_z(2), 0)
        low_got = swap(low, "dp", 1)
        high = add(kept_z(high, 2), after(high_got, low))
        high_got = swap(high, "dp", 2)
        gains = gains + after(gains_got, high)
        gains_got = swap(gains, "dp", 1)
        qkv_sum = ordered(qkv_sum, after(qkv_got, gains), bit_z(2), 0)
        qkv_got = swap(qkv_sum, "dp", 1)
        low = ordered(low, after(low_got, qkv_sum), bit_z(1), 0).astype(F32)
        high = ordered(high, after(high_got, low), bit_z(2), 0)
        high_got = swap(high, "dp", 1)
        gains = gains + after(gains_got, high)
        gains_got = swap(gains, "dp", 2)
        qkv_sum = ordered(qkv_sum, after(qkv_got, gains), bit_z(1), 0).astype(F32)
        sum_qkv, sum_out = qkv_sum[:QKV_PART, :block], qkv_sum[QKV_PART:, :block]
        high = ordered(high, after(high_got, qkv_sum), bit_z(1), 0).astype(F32)
        gains = gains + after(gains_got, high)
        ff_sum = jnp.concatenate([low, high[: high.shape[0] - HIGH_PAD]], axis=0)
    return (
        result_shard,
        assemble(grad_near, grad_far),
        sum_qkv.T,
        sum_out,
        ff_sum[:block],
        ff_sum[block : 2 * block],
        ff_sum[2 * block :].T,
        gains[0],
        gains[1],
    )


def solution(mesh):
    placed = (
        P("gy", ("dp", "gx")),
        P(("dp", "gx", "gy")),
        P("gy", ("dp", "gx")),
        P(),
        P(),
        P("gy", "gx"),
        P("gx", "gy"),
        P("gy", "gx"),
        P("gy", "gx"),
        P("gx", "gy"),
    )
    return jax.shard_map(
        on_device,
        mesh=mesh,
        in_specs=placed,
        out_specs=(
            P("gy", ("dp", "gx")),
            P("gy", ("dp", "gx")),
            P("gy", "gx"),
            P("gx", "gy"),
            P("gy", "gx"),
            P("gy", "gx"),
            P("gx", "gy"),
            P(),
            P(),
        ),
        check_vma=False,
    )
```
